32 devices in a mesh: dp: 8 (over z, core), cp: 4 (over y, x).
Axes of the slice: x: 2, y: 2, z: 4, core: 2. Of those that a mesh axis runs over, the one named last changes fastest.
Arguments:
- tokens: bfloat16 [8, 1152, 960], P('dp', 'cp'), may hold values from -6 to 6
- recur_depth: int32 [8, 1152], P('dp', 'cp'), may hold values from 1 to 3
- document_ids: int32 [8, 1152], P('dp', 'cp'), may hold values from 0 to 1151, as said below
- cotangent: bfloat16 [8, 1152, 960], P('dp', 'cp'), may hold values from -6 to 6
- query_weight: bfloat16 [960, 960], P('cp'), may hold values from -0.1875 to 0.1875
- key_weight: bfloat16 [960, 320], P('cp'), may hold values from -0.1875 to 0.1875
- value_weight: bfloat16 [960, 320], P('cp'), may hold values from -0.1875 to 0.1875
- output_weight: bfloat16 [960, 960], P('cp'), may hold values from -1 to 1
- gate_weight: bfloat16 [960, 2560], P('cp'), may hold values from -0.1875 to 0.1875
- up_weight: bfloat16 [960, 2560], P('cp'), may hold values from -0.1875 to 0.1875
- down_weight: bfloat16 [2560, 960], P('cp'), may hold values from -0.125 to 0.125
- router_weight: bfloat16 [3, 960], P(None, 'cp'), may hold values from -0.1875 to 0.1875
- attention_gain: bfloat16 [960], P('cp'), may hold values from 0.5 to 1.5
- feedforward_gain: bfloat16 [960], P('cp'), may hold values from 0.5 to 1.5
Outputs:
- activations: bfloat16 [8, 1152, 960], P('dp', 'cp')
- input_grad: bfloat16 [8, 1152, 960], P('dp', 'cp')
- grad_query: float32 [960, 960], P('cp')
- grad_key: float32 [960, 320], P('cp')
- grad_value: float32 [960, 320], P('cp')
- grad_output: float32 [960, 960], P('cp')
- grad_gate: float32 [960, 2560], P('cp')
- grad_up: float32 [960, 2560], P('cp')
- grad_down: float32 [2560, 960], P('cp')
- grad_router: float32 [3, 960], P(None, 'cp')
- grad_attention_gain: float32 [960], P('cp')
- grad_feedforward_gain: float32 [960], P('cp')
The draws below stay inside these ranges and needn't reach their ends.
Inputs may be any that keep to these rules, and one draw needn't show every extreme that they name: `document_ids`: A token's id is the position within its sequence where its document begins, so ids never fall along a sequence; the first token has id 0 and the last token of every sequence is a document of its own; in every sequence one document begins on the tokens of the first device of cp and ends on those of its last.
All inputs are finite; a program needn't handle non-finite values.
Results may differ from the reference program's by a relative error of at most 0.028.
Values may be sent and summed in bfloat16 or wider, within the bound.
No kernel may reach another device: no remote copies, remote signals or barrier semaphores. Data moves between devices by JAX's collectives and lax.ppermute only.
A program may use at most 320 MiB of HBM per device.

```python
import jax
import jax.numpy as jnp
from jax import lax

D = 960
FF = 2560
HEADS = 15
KV_HEADS = 5
HEAD_DIM = 64
RECUR = 3
SEQ_LEN = 1152
TOK_CP = 288
SEQS_ALL = 8


def draw_document_ids(key, part):
    key = jax.random.fold_in(key, 7)
    first_key, last_key, break_key = jax.random.split(key, 3)
    starts = jax.random.randint(first_key, (SEQS_ALL, 1), 0, TOK_CP)
    end_places = jax.random.randint(last_key, (SEQS_ALL, 1), SEQ_LEN - TOK_CP + 1, SEQ_LEN)
    places = jnp.arange(SEQ_LEN, dtype=jnp.int32)[None, :]
    breaks = jax.random.randint(break_key, (SEQS_ALL, SEQ_LEN), 0, 24) == 0
    inside = (places > starts) & (places < end_places)
    breaks = breaks & jnp.logical_not(inside) | (places == starts) | (places == end_places)
    breaks = (breaks | (places == SEQ_LEN - 1)) & (places > 0)
    marks = jnp.where(breaks, places, jnp.zeros_like(places)).astype(jnp.int32)
    return lax.cummax(marks, axis=1).astype(jnp.int32)


def plant(values, stream_key, low, high):
    spot = [jax.random.randint(jax.random.fold_in(stream_key, axis), (), 0, length) for axis, length in enumerate(values.shape)]
    main_axis = values.shape.index(max(values.shape))
    beside = spot[:main_axis] + [(spot[main_axis] + 1) % values.shape[main_axis]] + spot[main_axis + 1:]
    return values.at[tuple(spot)].set(low).at[tuple(beside)].set(high)


def block_levels(key, shape, cuts, low, top_value):
    gain, own = 1.0, jax.random.fold_in(key, 6)
    for axis_at, shards_of in cuts:
        draws = jnp.exp(jax.random.uniform(jax.random.fold_in(own, axis_at), (shards_of,), jnp.float32, low / len(cuts), top_value / len(cuts)))
        gain = gain * jnp.repeat(draws, shape[axis_at] // shards_of).reshape([-1 if axis == axis_at else 1 for axis in range(len(shape))])
    return gain


def noise(key, dims, scale, bound, cuts=(), held_as=jnp.bfloat16):
    factor_of = block_levels(key, dims, cuts, -0.22, 0.18) if cuts else 1.0
    entries = jax.random.normal(key, dims, jnp.float32) * scale * factor_of
    return jnp.minimum(jnp.maximum(entries, -bound), bound).astype(held_as)


def setup_inputs(seed: int = 0) -> dict:
    arg_keys = jax.random.split(jax.random.key(seed), 15)
    return {
        "tokens": noise(arg_keys[0], (SEQS_ALL, SEQ_LEN, D), 1.0, 6.0, ((0, 8), (1, 4))),
        "recur_depth": plant(jax.random.randint(arg_keys[1], (SEQS_ALL, SEQ_LEN), 1, RECUR + 1), jax.random.fold_in(arg_keys[1], 1), 1, RECUR).astype(jnp.int32),
        "document_ids": draw_document_ids(jax.random.fold_in(arg_keys[14], 71), 0),
        "cotangent": noise(arg_keys[3], (SEQS_ALL, SEQ_LEN, D), 1.0, 6.0, ((0, 8), (1, 4))),
        "query_weight": noise(arg_keys[4], (D, HEADS * HEAD_DIM), D ** -0.5, 0.1875, ((0, 4),)),
        "key_weight": noise(arg_keys[5], (D, KV_HEADS * HEAD_DIM), D ** -0.5, 0.1875, ((0, 4),)),
        "value_weight": noise(arg_keys[6], (D, KV_HEADS * HEAD_DIM), D ** -0.5, 0.1875, ((0, 4),)),
        "output_weight": noise(arg_keys[7], (HEADS * HEAD_DIM, D), (HEAD_DIM // 2) ** -0.5, 1.0, ((0, 4),)),
        "gate_weight": noise(arg_keys[8], (D, FF), D ** -0.5, 0.1875, ((0, 4),)),
        "up_weight": noise(arg_keys[9], (D, FF), D ** -0.5, 0.1875, ((0, 4),)),
        "down_weight": noise(arg_keys[10], (FF, D), FF ** -0.5, 0.125, ((0, 4),)),
        "router_weight": noise(arg_keys[11], (RECUR, D), D ** -0.5, 0.1875, ((1, 4),)),
        "attention_gain": jnp.clip(1.0 + 0.1 * jax.random.normal(arg_keys[12], (D,), jnp.float32), 0.5, 1.5).astype(jnp.bfloat16),
        "feedforward_gain": jnp.clip(1.0 + 0.1 * jax.random.normal(arg_keys[13], (D,), jnp.float32), 0.5, 1.5).astype(jnp.bfloat16),
    }


NORM_EPSILON = 1e-05
MASKED_SCORE = -1e+30
ROPE_BASE = 10000.0

@jax.custom_vjp
def low(v):
    return lax.optimization_barrier(v.astype(jnp.bfloat16)).astype(jnp.float32)

@jax.custom_vjp
def low_back(v):
    return v

def low_keep(v):
    return (low(v), None)

def low_pass(kept, grad):
    return (grad,)

def back_keep(v):
    return (v, None)

def back_low(kept, grad):
    return (low(grad),)
low.defvjp(low_keep, low_pass)
low_back.defvjp(back_keep, back_low)

def inverse_rms(matrix):
    return lax.rsqrt(lax.optimization_barrier(jnp.mean(matrix * matrix, axis=-1, keepdims=True)) + NORM_EPSILON)

def rope_tables(offset, length, head_size):
    halfway = head_size // 2
    inverse = jnp.power(ROPE_BASE, -2.0 * jnp.arange(halfway, dtype=jnp.float32) / head_size)
    places = (offset + jnp.arange(length)).astype(jnp.float32)
    angles = places[:, None] * inverse[None, :]
    return (jnp.cos(angles), jnp.sin(angles))

def rotate_heads(matrix, cosine, sine):
    halfway = matrix.shape[-1] // 2
    front_half = matrix[..., :halfway]
    back_half = matrix[..., halfway:]
    cosine_rows = cosine[:, None, :]
    sine_rows = sine[:, None, :]
    return jnp.concatenate([front_half * cosine_rows - back_half * sine_rows, back_half * cosine_rows + front_half * sine_rows], axis=-1)

def recursion_step(state, weights, recursion, depth_row, doc_row, cosine, sine):
    query_weight, key_weight, value_weight, output_weight, gate_weight, up_weight, down_weight, router_weight, attention_gain, feedforward_gain = weights
    highest = lax.Precision.HIGHEST
    length = state.shape[0]
    head_count = query_weight.shape[1] // HEAD_DIM
    key_heads = key_weight.shape[1] // HEAD_DIM
    group_size = head_count // key_heads
    normed = low(state * inverse_rms(state) * attention_gain)
    query_proj = low_back(jnp.dot(normed, query_weight, precision=highest))
    key_proj = low_back(jnp.dot(normed, key_weight, precision=highest))
    value_rows = low(low_back(jnp.dot(normed, value_weight, precision=highest)))
    query_rows = low(rotate_heads(query_proj.reshape(length, head_count, HEAD_DIM), cosine, sine))
    key_rows = low(rotate_heads(key_proj.reshape(length, key_heads, HEAD_DIM), cosine, sine))
    value_rows = value_rows.reshape(length, key_heads, HEAD_DIM)
    query_group = query_rows.reshape(length, key_heads, group_size, HEAD_DIM)
    scores = low_back(jnp.einsum('ckgd,lkd->kgcl', query_group, key_rows, precision=highest)) * HEAD_DIM ** (-0.5)
    places = jnp.arange(length)
    key_mask = (places[None, :] <= places[:, None]) & (doc_row[None, :] == doc_row[:, None])
    key_mask = key_mask & ((depth_row[None, :] > recursion) | (places[None, :] == places[:, None]))
    scores = jnp.where(key_mask[None, None], scores, MASKED_SCORE)
    row_peak = lax.optimization_barrier(jnp.max(scores, axis=-1, keepdims=True))
    exponent = jnp.exp(scores - row_peak)
    probs_rows = exponent / lax.optimization_barrier(jnp.sum(exponent, axis=-1, keepdims=True))
    mixed_rows = jnp.einsum('kgcl,lkd->ckgd', low(probs_rows), value_rows, precision=highest)
    attended = low(low_back(mixed_rows.reshape(length, head_count * HEAD_DIM)))
    attention_out = low_back(jnp.dot(attended, output_weight, precision=highest))
    after_attention = state + attention_out
    normed_ffn = low(after_attention * inverse_rms(after_attention) * feedforward_gain)
    gate_value = low_back(jnp.dot(normed_ffn, gate_weight, precision=highest))
    up_value = low_back(jnp.dot(normed_ffn, up_weight, precision=highest))
    inner_rows = low(jax.nn.silu(gate_value) * up_value)
    feedforward_out = low_back(jnp.dot(inner_rows, down_weight, precision=highest))
    branch_sum = attention_out + feedforward_out
    router_logit = jnp.dot(state, router_weight[recursion], precision=highest)
    gate_factor = jax.nn.sigmoid(router_logit) * (depth_row > recursion).astype(jnp.float32)
    return state + gate_factor[:, None] * branch_sum

def run_sequences(field, weights, recur_depth, document_ids):
    cosine, sine = rope_tables(0, field.shape[1], HEAD_DIM)

    def one_sequence(sequence_items):
        state, depth_row, doc_row = sequence_items
        for recursion in range(RECUR):
            state = recursion_step(state, weights, recursion, depth_row, doc_row, cosine, sine)
        return state
    return lax.map(jax.checkpoint(one_sequence), (field, recur_depth, document_ids))

def reference(tokens, recur_depth, document_ids, cotangent, query_weight, key_weight, value_weight, output_weight, gate_weight, up_weight, down_weight, router_weight, attention_gain, feedforward_gain):
    params = (query_weight.astype(jnp.float32), key_weight.astype(jnp.float32), value_weight.astype(jnp.float32), output_weight.astype(jnp.float32), gate_weight.astype(jnp.float32), up_weight.astype(jnp.float32), down_weight.astype(jnp.float32), router_weight.astype(jnp.float32), attention_gain.astype(jnp.float32), feedforward_gain.astype(jnp.float32))
    inputs = tokens.astype(jnp.float32)

    def forward_all(field, weights):
        return run_sequences(field, weights, recur_depth, document_ids)
    outputs, pullback = jax.vjp(forward_all, inputs, params)
    grad_inputs, grad_params = pullback(cotangent.astype(jnp.float32))
    return (outputs.astype(jnp.bfloat16), grad_inputs.astype(jnp.bfloat16), grad_params[0], grad_params[1], grad_params[2], grad_params[3], grad_params[4], grad_params[5], grad_params[6], grad_params[7], grad_params[8], grad_params[9])
```

```python
import functools

import jax
import jax.numpy as jnp
from jax import lax
from jax.experimental import pallas as pl
from jax.experimental.pallas import tpu as pltpu
from jax.sharding import PartitionSpec as P

HEAD_DIM = 64
LANES = 128
GROUP = 3
RECUR = 3
NORM_EPSILON = 1e-05
MASKED_SCORE = -1e30
ROPE_BASE = 10000.0
SCALE = HEAD_DIM ** (-0.5)
MIB = 2**20
F32, BF16 = jnp.float32, jnp.bfloat16
NN = (((1,), (0,)), ((), ()))
NT = (((1,), (1,)), ((), ()))
TN = (((0,), (0,)), ((), ()))


def dotf(a, b, dims=NN):
    return lax.dot_general(a, b, dims, preferred_element_type=F32)


def whole(*shape):
    return pl.BlockSpec(shape, lambda g: (0,) * len(shape))


def turn(u):
    lane = lax.broadcasted_iota(jnp.int32, u.shape, 1) % HEAD_DIM
    return jnp.where(lane < HEAD_DIM // 2, pltpu.roll(u, LANES - 32, 1), pltpu.roll(u, 32, 1))


def qkv_kernel(x_ref, gain_ref, wq_ref, wkv_ref, cq_ref, sq_ref, ck_ref, sk_ref, q_ref, kv_ref, normed_ref):
    x = x_ref[...]
    factor = lax.rsqrt(jnp.mean(x * x, axis=-1, keepdims=True) + NORM_EPSILON)
    normed_ref[...] = (x * factor * gain_ref[...]).astype(BF16)
    normed = normed_ref[...]
    kv = dotf(normed, wkv_ref[...])
    cos, sin = ck_ref[...], sk_ref[...]
    for at in range(0, kv_ref.shape[1], LANES):
        u = kv[:, at : at + LANES]
        kv_ref[:, at : at + LANES] = (u * cos + turn(u) * sin).astype(BF16)
    q = dotf(normed, wq_ref[...])
    cos, sin = cq_ref[...], sq_ref[...]
    width = q_ref.shape[1]
    for at in range(0, width, LANES):
        if at + LANES <= width:
            u = q[:, at : at + LANES]
        else:
            u = jnp.concatenate([q[:, at:], jnp.zeros((q.shape[0], at + LANES - width), F32)], axis=1)
        r = (u * cos + turn(u) * sin).astype(BF16)
        q_ref[:, at : min(at + LANES, width)] = r[:, : min(LANES, width - at)]


def qkv_call(x, gain, wq, wkv, tables):
    rows, width = x.shape
    heads, both = wq.shape[1], wkv.shape[1]
    return pl.pallas_call(
        qkv_kernel,
        grid=(1,),
        in_specs=[whole(rows, width), whole(1, width), whole(width, heads), whole(width, both)]
        + [whole(rows, LANES)] * 4,
        out_specs=[whole(rows, heads), whole(rows, both), whole(rows, width)],
        out_shape=[
            jax.ShapeDtypeStruct((rows, heads), BF16),
            jax.ShapeDtypeStruct((rows, both), BF16),
            jax.ShapeDtypeStruct((rows, width), BF16),
        ],
        compiler_params=pltpu.CompilerParams(vmem_limit_bytes=32 * MIB),
        cost_estimate=pl.CostEstimate(
            flops=2 * rows * width * (heads + both),
            bytes_accessed=2 * width * (heads + both) + 8 * rows * width,
            transcendentals=0,
        ),
        name="norm_qkv_rope",
    )(x, gain, wq, wkv, *tables)


def make_bias(row_info, col_info, recursion):
    doc_r, pos_r = row_info[:, 0:1], row_info[:, 1:2]
    doc_c, pos_c, depth_c = col_info[0:1, :], col_info[1:2, :], col_info[2:3, :]
    live = (depth_c > recursion) | (pos_c == pos_r)
    allowed = (pos_c <= pos_r) & (doc_c == doc_r) & live
    return jnp.where(allowed, 0.0, MASKED_SCORE).astype(F32)


def split_pairs(packed, out, to_left):
    rows, width = packed.shape
    lane = lax.broadcasted_iota(jnp.int32, (rows, LANES), 1)
    for at in range(0, width, LANES):
        h = at // HEAD_DIM
        if at + LANES <= width:
            u = packed[:, at : at + LANES].astype(F32)
        else:
            u = jnp.concatenate([packed[:, at:].astype(F32), jnp.zeros((rows, at + LANES - width), F32)], axis=1)
        v = pltpu.roll(u, HEAD_DIM, 1)
        first, second = (u, v) if to_left else (v, u)
        keep = (lane < HEAD_DIM) if to_left else (lane >= HEAD_DIM)
        out[h] = jnp.where(keep, first, 0.0).astype(out.dtype)
        if at + LANES <= width:
            out[h + 1] = jnp.where(keep, second, 0.0).astype(out.dtype)


def join_pairs(scr, out_ref, from_left):
    heads = scr.shape[0]
    lane = lax.broadcasted_iota(jnp.int32, scr.shape[1:], 1)
    for h in range(0, heads, 2):
        at = h * HEAD_DIM
        a = scr[h] if from_left else pltpu.roll(scr[h], HEAD_DIM, 1)
        if h + 1 < heads:
            b = pltpu.roll(scr[h + 1], HEAD_DIM, 1) if from_left else scr[h + 1]
            out_ref[:, at : at + LANES] = jnp.where(lane < HEAD_DIM, a, b).astype(out_ref.dtype)
        else:
            out_ref[:, at : at + HEAD_DIM] = a[:, :HEAD_DIM].astype(out_ref.dtype)


def attend_kernel(recursion, count, q_ref, *refs):
    key_refs, (row_ref, col_ref, att_ref, lse_ref, bias, q_all, o_all) = refs[:count], refs[count:]
    g = pl.program_id(0)

    @pl.when(g == 0)
    def _():
        bias[...] = make_bias(row_ref[...], col_ref[...], recursion)
        split_pairs(q_ref[...], q_all, True)

    kv = jnp.concatenate([k[...] for k in key_refs], axis=0)
    for j in range(GROUP):
        h = g * GROUP + j
        s = dotf(q_all[h], kv, NT) * SCALE + bias[...]
        peak = jnp.max(s, axis=1, keepdims=True)
        e = jnp.exp(s - peak)
        total = jnp.sum(e, axis=1, keepdims=True)
        o_all[h] = dotf(e.astype(BF16), kv) / total
        lse_ref[0, :, j : j + 1] = peak + jnp.log(total)

    @pl.when(g == pl.num_programs(0) - 1)
    def _():
        join_pairs(o_all, att_ref, False)


def attend_call(recursion, q, kvs, row_info, col_info):
    rows, width = q.shape
    keys = sum(k.shape[0] for k in kvs)
    groups = kvs[0].shape[1] // LANES
    heads = groups * GROUP
    return pl.pallas_call(
        functools.partial(attend_kernel, recursion, len(kvs)),
        grid=(groups,),
        in_specs=[whole(rows, width)]
        + [pl.BlockSpec((k.shape[0], LANES), lambda g: (0, g)) for k in kvs]
        + [whole(rows, 2), whole(3, keys)],
        out_specs=[whole(rows, width), pl.BlockSpec((1, rows, GROUP), lambda g: (g, 0, 0))],
        out_shape=[
            jax.ShapeDtypeStruct((rows, width), BF16),
            jax.ShapeDtypeStruct((groups, rows, GROUP), F32),
        ],
        scratch_shapes=[
            pltpu.VMEM((rows, keys), F32),
            pltpu.VMEM((heads, rows, LANES), BF16),
            pltpu.VMEM((heads, rows, LANES), F32),
        ],
        compiler_params=pltpu.CompilerParams(vmem_limit_bytes=40 * MIB),
        cost_estimate=pl.CostEstimate(
            flops=4 * rows * keys * LANES * heads,
            bytes_accessed=4 * q.size + 2 * keys * groups * LANES,
            transcendentals=heads * rows * keys,
        ),
        name="attend",
    )(q, *kvs, row_info, col_info)


def attend_back_kernel(recursion, count, q_ref, do_ref, att_ref, *refs):
    key_refs, refs = refs[:count], refs[count:]
    lse_ref, row_ref, col_ref, cos_ref, sin_ref, dq_ref, dkv_ref, bias, q_all, do_all, dot_all, p3, ds3, dq_all = refs
    g = pl.program_id(0)
    rows, width = q_ref.shape

    @pl.when(g == 0)
    def _():
        bias[...] = make_bias(row_ref[...], col_ref[...], recursion)
        split_pairs(q_ref[...], q_all, True)
        split_pairs(do_ref[...], do_all, False)
        prod = do_ref[...].astype(F32) * att_ref[...].astype(F32)
        for h in range(width // HEAD_DIM):
            dot_all[h] = jnp.sum(prod[:, h * HEAD_DIM : (h + 1) * HEAD_DIM], axis=1, keepdims=True)

    kv = jnp.concatenate([k[...] for k in key_refs], axis=0)
    for j in range(GROUP):
        h = g * GROUP + j
        here = slice(j * rows, (j + 1) * rows)
        s = dotf(q_all[h], kv, NT) * SCALE + bias[...]
        p = jnp.exp(s - lse_ref[0, :, j : j + 1])
        dp = dotf(do_all[h], kv, NT)
        ds = (p * (dp - dot_all[h])).astype(BF16)
        p3[here, :] = p.astype(BF16)
        ds3[here, :] = ds
        dq = dotf(ds, kv) * SCALE
        dq_all[h] = dq * cos_ref[...] - turn(dq) * sin_ref[...]
    q3 = jnp.concatenate([q_all[g * GROUP + j] for j in range(GROUP)], axis=0)
    do3 = jnp.concatenate([do_all[g * GROUP + j] for j in range(GROUP)], axis=0)
    dkv = dotf(q3, ds3[...], TN) * SCALE + dotf(do3, p3[...], TN)
    dkv_ref[...] = dkv.T.astype(BF16)

    @pl.when(g == pl.num_programs(0) - 1)
    def _():
        join_pairs(dq_all, dq_ref, True)


def attend_back_call(recursion, q, do, att, kvs, lse, row_info, col_info, cos, sin):
    rows, width = q.shape
    keys = sum(k.shape[0] for k in kvs)
    groups = kvs[0].shape[1] // LANES
    heads = groups * GROUP
    return pl.pallas_call(
        functools.partial(attend_back_kernel, recursion, len(kvs)),
        grid=(groups,),
        in_specs=[whole(rows, width)] * 3
        + [pl.BlockSpec((k.shape[0], LANES), lambda g: (0, g)) for k in kvs]
        + [pl.BlockSpec((1, rows, GROUP), lambda g: (g, 0, 0)), whole(rows, 2), whole(3, keys)]
        + [whole(rows, LANES)] * 2,
        out_specs=[whole(rows, width), pl.BlockSpec((keys, LANES), lambda g: (0, g))],
        out_shape=[
            jax.ShapeDtypeStruct((rows, width), BF16),
            jax.ShapeDtypeStruct((keys, groups * LANES), BF16),
        ],
        scratch_shapes=[
            pltpu.VMEM((rows, keys), F32),
            pltpu.VMEM((heads, rows, LANES), BF16),
            pltpu.VMEM((heads, rows, LANES), BF16),
            pltpu.VMEM((heads, rows, 1), F32),
            pltpu.VMEM((GROUP * rows, keys), BF16),
            pltpu.VMEM((GROUP * rows, keys), BF16),
            pltpu.VMEM((heads, rows, LANES), F32),
        ],
        compiler_params=pltpu.CompilerParams(vmem_limit_bytes=48 * MIB),
        cost_estimate=pl.CostEstimate(
            flops=10 * rows * keys * LANES * heads,
            bytes_accessed=8 * q.size + 4 * keys * groups * LANES,
            transcendentals=heads * rows * keys,
        ),
        name="attend_back",
    )(q, do, att, *kvs, lse, row_info, col_info, cos, sin)


class Place:
    def __init__(self, dp, cp):
        self.dp, self.cp, self.square = dp, cp, cp == 4
        dp_at, cp_at = lax.axis_index("dp"), lax.axis_index("cp")
        self.core, self.z = dp_at % 2, dp_at // 2
        self.y, self.x = cp_at // 2, cp_at % 2

    def over_x(self, a):
        return lax.ppermute(a, "cp", [(i, i ^ 1) for i in range(self.cp)])

    def over_y(self, a):
        return lax.ppermute(a, "cp", [(i, i ^ 2) for i in range(self.cp)])

    def over_core(self, a):
        return lax.ppermute(a, "dp", [(i, i ^ 1) for i in range(self.dp)])

    def move_tokens(self, a):
        if not self.square:
            return a
        pairs = []
        for d in range(self.dp):
            for c in range(self.cp):
                z, core, y, x = d // 2, d % 2, c // 2, c % 2
                pairs.append((d * self.cp + c, (2 * z + y) * self.cp + 2 * core + x))
        return lax.ppermute(a, ("dp", "cp"), pairs)

    def key_blocks(self):
        if not self.square:
            return list(range(self.cp)), lax.axis_index("cp")
        own = 2 * self.core + self.x
        return [own ^ k for k in range(4)], own

    def gather_keys(self, a):
        if not self.square:
            return (lax.all_gather(a, "cp", axis=0, tiled=True),)
        from_x, from_core = self.over_x(a), self.over_core(a)
        return a, from_x, from_core, self.over_core(from_x)

    def scatter_keys(self, a):
        if not self.square:
            return lax.psum_scatter(a, "cp", scatter_dimension=0, tiled=True).astype(F32)
        rows = a.shape[0] // 4
        got = self.over_core(a[2 * rows :])
        pair = (a[: 2 * rows].astype(F32) + got.astype(F32)).astype(BF16)
        return pair[:rows].astype(F32) + self.over_x(pair[rows:]).astype(F32)

    def sum_z(self, a):
        n = self.dp // 2

        def hop(b, moves):
            return lax.ppermute(b, "dp", [(2 * s + c, 2 * t + c) for s, t in moves for c in range(2)])

        def add(b, c):
            return (b.astype(F32) + c.astype(F32)).astype(BF16)

        if n == 1:
            return a
        half = n // 2
        for t in range(half - 1):
            a = add(a, hop(a, [(t, t + 1), (n - 1 - t, n - 2 - t)]))
        a = add(a, hop(a, [(half - 1, half), (half, half - 1)]))
        for t in reversed(range(half - 1)):
            back = hop(a, [(t + 1, t), (n - 2 - t, n - 1 - t)])
            a = jnp.where((self.z == t) | (self.z == n - 1 - t), back, a)
        return a

    def scatter_sum(self, blocks, cut):
        _, rows, width = blocks.shape
        if not self.square:
            return lax.psum_scatter(blocks, "cp", scatter_dimension=0, tiled=False)

        def step(b, at, axis, over):
            away = lax.dynamic_index_in_dim(b, 1 - at, axis, keepdims=False)
            kept = lax.dynamic_index_in_dim(b, at, axis, keepdims=False)
            return (kept.astype(F32) + over(away).astype(F32)).astype(BF16)

        blocks = blocks.reshape(2, 2, rows, width)
        first = step(blocks[:, :, :cut], self.x, 1, self.over_x)
        second = step(blocks[:, :, cut:], self.y, 0, self.over_y)
        first = step(first, self.y, 0, self.over_y)
        second = step(second, self.x, 0, self.over_x)
        return jnp.concatenate([first, second], axis=0)

    def pick(self, a, b):
        return jnp.where(self.core == 0, a, b)


def inverse_rms(matrix):
    return lax.rsqrt(jnp.mean(matrix * matrix, axis=-1, keepdims=True) + NORM_EPSILON)


def norm_back(matrix, gain, upstream):
    factor = inverse_rms(matrix)
    unit = matrix * factor
    scaled = upstream * gain
    grad = factor * (scaled - unit * jnp.mean(scaled * unit, axis=-1, keepdims=True))
    return grad, jnp.sum(upstream * unit, axis=0)


def rope_tables(places):
    half = HEAD_DIM // 2
    inverse = jnp.power(ROPE_BASE, -2.0 * jnp.arange(half, dtype=F32) / HEAD_DIM)
    angles = places.astype(F32)[:, None] * inverse[None, :]
    cos, sin = jnp.cos(angles), jnp.sin(angles)
    cos, sin = jnp.concatenate([cos, cos], 1), jnp.concatenate([-sin, sin], 1)
    one, zero = jnp.ones_like(cos), jnp.zeros_like(sin)
    both = lambda a, b: jnp.concatenate([a, b], 1)
    return both(cos, cos), both(sin, sin), both(cos, one), both(sin, zero)


def gather_weights(place, shards):
    wq, wk, wv, wo, gate, up, down, router, gain_a, gain_f = shards
    rows, kv_heads = wk.shape[0], wk.shape[1] // HEAD_DIM
    gather = lambda a: lax.all_gather(a, "cp", axis=0, tiled=True)
    wkv = jnp.stack([wk.reshape(rows, kv_heads, HEAD_DIM), wv.reshape(rows, kv_heads, HEAD_DIM)], axis=2)
    wkv = wkv.reshape(rows, 2 * kv_heads * HEAD_DIM)
    both, width = wkv.shape[1], wq.shape[1]
    small = jnp.concatenate([gain_a[:, None], gain_f[:, None], router.T], axis=1)
    total = jnp.concatenate([wkv, wq, wo], axis=1)
    half = total.shape[1] // 2
    mine = gather(jnp.concatenate([place.pick(total[:, :half], total[:, half:]), small], axis=1))
    theirs = place.over_core(mine)
    total = jnp.concatenate([place.pick(mine, theirs)[:, :half], place.pick(theirs, mine)[:, :half]], axis=1)
    small = mine[:, half:]
    wkv, wq, wo = total[:, :both], total[:, both : both + width], total[:, both + width :]
    mine = gather(place.pick(gate, up))
    theirs = place.over_core(mine)
    gate, up = place.pick(mine, theirs), place.pick(theirs, mine)
    each, wide = down.shape
    mine = gather(place.pick(down[: each // 2], down[each // 2 :]))
    theirs = place.over_core(mine)
    down = jnp.stack(
        [
            place.pick(mine, theirs).reshape(place.cp, each // 2, wide),
            place.pick(theirs, mine).reshape(place.cp, each // 2, wide),
        ],
        axis=1,
    ).reshape(place.cp * each, wide)
    return wkv, wq, wo, gate, up, down, small


def forward_level(state, weights, recursion, context):
    wkv, wq, wo, gate_w, up_w, down_w, small = weights
    place, tables, row_info, col_info, depth = context
    gain_a, gain_f = small[:, 0].astype(F32), small[:, 1].astype(F32)
    q, kv, normed = qkv_call(state, gain_a[None, :], wq, wkv, tables)
    kvs = place.gather_keys(kv)
    att, lse = attend_call(recursion, q, kvs, row_info, col_info)
    attn = dotf(att, wo)
    after = state + attn
    normed2 = (after * inverse_rms(after) * gain_f).astype(BF16)
    gate = dotf(normed2, gate_w)
    up = dotf(normed2, up_w)
    inner = (jax.nn.silu(gate) * up).astype(BF16)
    branch = attn + dotf(inner, down_w)
    router_row = small[:, 2 + recursion].astype(F32)
    router = jax.nn.sigmoid(jnp.sum(state * router_row, axis=-1, keepdims=True))
    active = (depth[:, None] > recursion).astype(F32)
    following = state + active * router * branch
    saved = (state, normed, q, kvs, lse, att, after, normed2, gate.astype(BF16), up.astype(BF16), inner, branch, router_row, router, active)
    return following, saved


def backward_level(saved, weights, recursion, context, grad):
    wkv, wq, wo, gate_w, up_w, down_w, small = weights
    place, tables, row_info, col_info, _ = context
    cos_q, sin_q, cos_k, sin_k = tables
    gain_a, gain_f = small[:, 0].astype(F32), small[:, 1].astype(F32)
    state, normed, q, kvs, lse, att, after, normed2, gate, up, inner, branch, router_row, router, active = saved
    rows = state.shape[0]
    g_branch = grad * (active * router)
    g_logit = jnp.sum(grad * branch, axis=-1, keepdims=True) * active * router * (1.0 - router)
    g_router = jnp.sum(g_logit * state, axis=0)
    g_state = grad + g_logit * router_row
    g_ffn = g_branch.astype(BF16)
    g_inner = dotf(g_ffn, down_w, NT)
    gate, up = gate.astype(F32), up.astype(F32)
    sig = jax.nn.sigmoid(gate)
    g_gate = (g_inner * up * sig * (1.0 + gate * (1.0 - sig))).astype(BF16)
    g_up = (g_inner * gate * sig).astype(BF16)
    g_normed2 = dotf(g_gate, gate_w, NT) + dotf(g_up, up_w, NT)
    g_after, g_gain_f = norm_back(after, gain_f, g_normed2)
    g_state = g_state + g_after
    g_attn = (g_after + g_branch).astype(BF16)
    g_att = dotf(g_attn, wo, NT).astype(BF16)
    dq, dkv = attend_back_call(recursion, q, g_att, att, kvs, lse, row_info, col_info, cos_q, sin_q)
    dkv = place.scatter_keys(dkv)
    parts = dkv.reshape(rows, -1, 2, 2, HEAD_DIM // 2)
    swapped = parts[:, :, :, ::-1, :].reshape(rows, -1)
    spread = lambda t: jnp.tile(t, (1, dkv.shape[1] // LANES))
    dkv = (dkv * spread(cos_k) - swapped * spread(sin_k)).astype(BF16)
    g_normed = dotf(dq, wq, NT) + dotf(dkv, wkv, NT)
    g_rows, g_gain_a = norm_back(state, gain_a, g_normed)
    g_state = g_state + g_rows
    return g_state, (g_ffn, inner), (g_gate, g_up, normed2), (g_attn, att), (dq, dkv, normed), (g_router, g_gain_a, g_gain_f)


def local(tokens, recur_depth, document_ids, cotangent, *shards, dp, cp):
    place = Place(dp, cp)
    rows = tokens.shape[1]
    ids = jnp.stack([document_ids[0], recur_depth[0]])
    ids = place.move_tokens(ids)
    state = place.move_tokens(tokens[0]).astype(F32)
    grad = place.move_tokens(cotangent[0]).astype(F32)
    steps = jnp.arange(rows, dtype=jnp.int32)
    blocks, block = place.key_blocks()
    every = jnp.concatenate(place.gather_keys(ids.T), axis=0)
    spots = jnp.concatenate([b * rows + steps for b in blocks])
    col_info = jnp.stack([every[:, 0], spots, every[:, 1]])
    row_info = jnp.stack([ids[0], block * rows + steps], axis=1)
    tables = rope_tables(row_info[:, 1])
    context = (place, tables, row_info, col_info, ids[1])
    weights = gather_weights(place, shards)
    saved = []
    for recursion in range(RECUR):
        state, kept = forward_level(state, weights, recursion, context)
        saved.append(kept)
    activations = place.move_tokens(state.astype(BF16))[None]
    downs, ups, outs, ins, smalls = [], [], [], [], []
    for recursion in reversed(range(RECUR)):
        grad, a, b, c, d, e = backward_level(saved[recursion], weights, recursion, context, grad)
        for group, item in zip((downs, ups, outs, ins, smalls), (a, b, c, d, e)):
            group.append(item)
    input_grad = place.move_tokens(grad.astype(BF16))[None]
    column = lambda group, i: jnp.concatenate([item[i] for item in group], axis=0)
    width = shards[0].shape[0] * cp

    def reduce(left, away, kept):
        got = place.over_core(dotf(left, away, TN).astype(BF16))
        own = (dotf(left, kept, TN) + got.astype(F32)).astype(BF16)
        own = own.reshape(cp, -1, own.shape[1])
        cut = -(-own.shape[1] // 32) * 16
        return place.sum_z(place.scatter_sum(own, cut))

    def halves(right):
        n = right.shape[1] // 2
        return place.pick(right[:, n:], right[:, :n]), place.pick(right[:, :n], right[:, n:])

    def finish(own):
        other = place.over_core(own)
        return place.pick(own, other).astype(F32), place.pick(other, own).astype(F32)

    own_down = reduce(column(downs, 1), *halves(column(downs, 0)))
    g_gate, g_up = column(ups, 0), column(ups, 1)
    own_up = reduce(column(ups, 2), place.pick(g_up, g_gate), place.pick(g_gate, g_up))
    own_out = reduce(column(outs, 1), *halves(column(outs, 0)))
    own_in = reduce(column(ins, 2), *halves(jnp.concatenate([column(ins, 0), column(ins, 1)], axis=1)))
    grad_down = jnp.concatenate(finish(own_down), axis=1)
    grad_gate, grad_up = finish(own_up)
    grad_out = jnp.concatenate(finish(own_out), axis=1)
    grad_in = jnp.concatenate(finish(own_in), axis=1)
    grad_query = grad_in[:, :width]
    grad_kv = grad_in[:, width:].reshape(grad_in.shape[0], -1, 2, HEAD_DIM)
    grad_key = grad_kv[:, :, 0].reshape(grad_in.shape[0], -1)
    grad_value = grad_kv[:, :, 1].reshape(grad_in.shape[0], -1)
    vectors = [smalls[RECUR - 1 - r][0] for r in range(RECUR)]
    vectors += [sum(s[1] for s in smalls), sum(s[2] for s in smalls)]
    vectors = lax.psum(jnp.stack(vectors), ("dp", "cp"))
    vectors = lax.dynamic_slice_in_dim(vectors, lax.axis_index("cp") * (width // cp), width // cp, axis=1)
    return (
        activations,
        input_grad,
        grad_query,
        grad_key,
        grad_value,
        grad_out,
        grad_gate,
        grad_up,
        grad_down,
        vectors[:RECUR],
        vectors[RECUR],
        vectors[RECUR + 1],
    )


def solution(mesh):
    by_token = P("dp", "cp", None)
    by_row = P("cp", None)
    in_specs = (by_token, P("dp", "cp"), P("dp", "cp"), by_token) + (by_row,) * 7 + (P(None, "cp"), P("cp"), P("cp"))
    out_specs = (by_token, by_token) + (by_row,) * 7 + (P(None, "cp"), P("cp"), P("cp"))
    step = functools.partial(local, dp=mesh.shape["dp"], cp=mesh.shape["cp"])
    return jax.shard_map(step, mesh=mesh, in_specs=in_specs, out_specs=out_specs, check_vma=False)
```

```python
import functools

import jax
import jax.numpy as jnp
from jax import lax
from jax.experimental import pallas as pl
from jax.experimental.pallas import tpu as pltpu
from jax.sharding import PartitionSpec as P

HEAD_DIM = 64
LANES = 128
GROUP = 3
RECUR = 3
NORM_EPSILON = 1e-05
MASKED_SCORE = -1e30
ROPE_BASE = 10000.0
SCALE = HEAD_DIM ** (-0.5)
MIB = 2**20
F32, BF16 = jnp.float32, jnp.bfloat16
NN = (((1,), (0,)), ((), ()))
NT = (((1,), (1,)), ((), ()))
TN = (((0,), (0,)), ((), ()))


def dotf(a, b, dims=NN):
    return lax.dot_general(a, b, dims, preferred_element_type=F32)


def whole(*shape):
    return pl.BlockSpec(shape, lambda g: (0,) * len(shape))


def turn(u):
    lane = lax.broadcasted_iota(jnp.int32, u.shape, 1) % HEAD_DIM
    return jnp.where(lane < HEAD_DIM // 2, pltpu.roll(u, LANES - 32, 1), pltpu.roll(u, 32, 1))


def qkv_kernel(x_ref, gain_ref, wq_ref, wkv_ref, cq_ref, sq_ref, ck_ref, sk_ref, q_ref, kv_ref, normed_ref):
    x = x_ref[...]
    factor = lax.rsqrt(jnp.mean(x * x, axis=-1, keepdims=True) + NORM_EPSILON)
    normed_ref[...] = (x * factor * gain_ref[...]).astype(BF16)
    normed = normed_ref[...]
    kv = dotf(normed, wkv_ref[...])
    cos, sin = ck_ref[...], sk_ref[...]
    for at in range(0, kv_ref.shape[1], LANES):
        u = kv[:, at : at + LANES]
        kv_ref[:, at : at + LANES] = (u * cos + turn(u) * sin).astype(BF16)
    q = dotf(normed, wq_ref[...])
    cos, sin = cq_ref[...], sq_ref[...]
    width = q_ref.shape[1]
    for at in range(0, width, LANES):
        if at + LANES <= width:
            u = q[:, at : at + LANES]
        else:
            u = jnp.concatenate([q[:, at:], jnp.zeros((q.shape[0], at + LANES - width), F32)], axis=1)
        r = (u * cos + turn(u) * sin).astype(BF16)
        q_ref[:, at : min(at + LANES, width)] = r[:, : min(LANES, width - at)]


def qkv_call(x, gain, wq, wkv, tables):
    rows, width = x.shape
    heads, both = wq.shape[1], wkv.shape[1]
    return pl.pallas_call(
        qkv_kernel,
        grid=(1,),
        in_specs=[whole(rows, width), whole(1, width), whole(width, heads), whole(width, both)]
        + [whole(rows, LANES)] * 4,
        out_specs=[whole(rows, heads), whole(rows, both), whole(rows, width)],
        out_shape=[
            jax.ShapeDtypeStruct((rows, heads), BF16),
            jax.ShapeDtypeStruct((rows, both), BF16),
            jax.ShapeDtypeStruct((rows, width), BF16),
        ],
        compiler_params=pltpu.CompilerParams(vmem_limit_bytes=32 * MIB),
        cost_estimate=pl.CostEstimate(
            flops=2 * rows * width * (heads + both),
            bytes_accessed=2 * width * (heads + both) + 8 * rows * width,
            transcendentals=0,
        ),
        name="norm_qkv_rope",
    )(x, gain, wq, wkv, *tables)


def make_bias(row_info, col_info, recursion):
    doc_r, pos_r = row_info[:, 0:1], row_info[:, 1:2]
    doc_c, pos_c, depth_c = col_info[0:1, :], col_info[1:2, :], col_info[2:3, :]
    live = (depth_c > recursion) | (pos_c == pos_r)
    allowed = (pos_c <= pos_r) & (doc_c == doc_r) & live
    return jnp.where(allowed, 0.0, MASKED_SCORE).astype(F32)


def split_pairs(packed, out, to_left):
    rows, width = packed.shape
    lane = lax.broadcasted_iota(jnp.int32, (rows, LANES), 1)
    for at in range(0, width, LANES):
        h = at // HEAD_DIM
        if at + LANES <= width:
            u = packed[:, at : at + LANES].astype(F32)
        else:
            u = jnp.concatenate([packed[:, at:].astype(F32), jnp.zeros((rows, at + LANES - width), F32)], axis=1)
        v = pltpu.roll(u, HEAD_DIM, 1)
        first, second = (u, v) if to_left else (v, u)
        keep = (lane < HEAD_DIM) if to_left else (lane >= HEAD_DIM)
        out[h] = jnp.where(keep, first, 0.0).astype(out.dtype)
        if at + LANES <= width:
            out[h + 1] = jnp.where(keep, second, 0.0).astype(out.dtype)


def join_pairs(scr, out_ref, from_left):
    heads = scr.shape[0]
    lane = lax.broadcasted_iota(jnp.int32, scr.shape[1:], 1)
    for h in range(0, heads, 2):
        at = h * HEAD_DIM
        a = scr[h] if from_left else pltpu.roll(scr[h], HEAD_DIM, 1)
        if h + 1 < heads:
            b = pltpu.roll(scr[h + 1], HEAD_DIM, 1) if from_left else scr[h + 1]
            out_ref[:, at : at + LANES] = jnp.where(lane < HEAD_DIM, a, b).astype(out_ref.dtype)
        else:
            out_ref[:, at : at + HEAD_DIM] = a[:, :HEAD_DIM].astype(out_ref.dtype)


def attend_kernel(recursion, count, q_ref, *refs):
    key_refs, (row_ref, col_ref, att_ref, lse_ref, bias, q_all, o_all) = refs[:count], refs[count:]
    g = pl.program_id(0)

    @pl.when(g == 0)
    def _():
        bias[...] = make_bias(row_ref[...], col_ref[...], recursion)
        split_pairs(q_ref[...], q_all, True)

    kv = jnp.concatenate([k[...] for k in key_refs], axis=0)
    for j in range(GROUP):
        h = g * GROUP + j
        s = dotf(q_all[h], kv, NT) * SCALE + bias[...]
        peak = jnp.max(s, axis=1, keepdims=True)
        e = jnp.exp(s - peak)
        total = jnp.sum(e, axis=1, keepdims=True)
        o_all[h] = dotf(e.astype(BF16), kv) / total
        lse_ref[0, :, j : j + 1] = peak + jnp.log(total)

    @pl.when(g == pl.num_programs(0) - 1)
    def _():
        join_pairs(o_all, att_ref, False)


def attend_call(recursion, q, kvs, row_info, col_info):
    rows, width = q.shape
    keys = sum(k.shape[0] for k in kvs)
    groups = kvs[0].shape[1] // LANES
    heads = groups * GROUP
    return pl.pallas_call(
        functools.partial(attend_kernel, recursion, len(kvs)),
        grid=(groups,),
        in_specs=[whole(rows, width)]
        + [pl.BlockSpec((k.shape[0], LANES), lambda g: (0, g)) for k in kvs]
        + [whole(rows, 2), whole(3, keys)],
        out_specs=[whole(rows, width), pl.BlockSpec((1, rows, GROUP), lambda g: (g, 0, 0))],
        out_shape=[
            jax.ShapeDtypeStruct((rows, width), BF16),
            jax.ShapeDtypeStruct((groups, rows, GROUP), F32),
        ],
        scratch_shapes=[
            pltpu.VMEM((rows, keys), F32),
            pltpu.VMEM((heads, rows, LANES), BF16),
            pltpu.VMEM((heads, rows, LANES), F32),
        ],
        compiler_params=pltpu.CompilerParams(vmem_limit_bytes=40 * MIB),
        cost_estimate=pl.CostEstimate(
            flops=4 * rows * keys * LANES * heads,
            bytes_accessed=4 * q.size + 2 * keys * groups * LANES,
            transcendentals=heads * rows * keys,
        ),
        name="attend",
    )(q, *kvs, row_info, col_info)


def attend_back_kernel(recursion, count, q_ref, do_ref, att_ref, *refs):
    key_refs, refs = refs[:count], refs[count:]
    lse_ref, row_ref, col_ref, cos_ref, sin_ref, dq_ref, dkv_ref, bias, q_all, do_all, dot_all, p3, ds3, dq_all = refs
    g = pl.program_id(0)
    rows, width = q_ref.shape

    @pl.when(g == 0)
    def _():
        bias[...] = make_bias(row_ref[...], col_ref[...], recursion)
        split_pairs(q_ref[...], q_all, True)
        split_pairs(do_ref[...], do_all, False)
        prod = do_ref[...].astype(F32) * att_ref[...].astype(F32)
        for h in range(width // HEAD_DIM):
            dot_all[h] = jnp.sum(prod[:, h * HEAD_DIM : (h + 1) * HEAD_DIM], axis=1, keepdims=True)

    kv = jnp.concatenate([k[...] for k in key_refs], axis=0)
    for j in range(GROUP):
        h = g * GROUP + j
        here = slice(j * rows, (j + 1) * rows)
        s = dotf(q_all[h], kv, NT) * SCALE + bias[...]
        p = jnp.exp(s - lse_ref[0, :, j : j + 1])
        dp = dotf(do_all[h], kv, NT)
        ds = (p * (dp - dot_all[h])).astype(BF16)
        p3[here, :] = p.astype(BF16)
        ds3[here, :] = ds
        dq = dotf(ds, kv) * SCALE
        dq_all[h] = dq * cos_ref[...] - turn(dq) * sin_ref[...]
    q3 = jnp.concatenate([q_all[g * GROUP + j] for j in range(GROUP)], axis=0)
    do3 = jnp.concatenate([do_all[g * GROUP + j] for j in range(GROUP)], axis=0)
    dkv = dotf(q3, ds3[...], TN) * SCALE + dotf(do3, p3[...], TN)
    dkv_ref[...] = dkv.T.astype(BF16)

    @pl.when(g == pl.num_programs(0) - 1)
    def _():
        join_pairs(dq_all, dq_ref, True)


def attend_back_call(recursion, q, do, att, kvs, lse, row_info, col_info, cos, sin):
    rows, width = q.shape
    keys = sum(k.shape[0] for k in kvs)
    groups = kvs[0].shape[1] // LANES
    heads = groups * GROUP
    return pl.pallas_call(
        functools.partial(attend_back_kernel, recursion, len(kvs)),
        grid=(groups,),
        in_specs=[whole(rows, width)] * 3
        + [pl.BlockSpec((k.shape[0], LANES), lambda g: (0, g)) for k in kvs]
        + [pl.BlockSpec((1, rows, GROUP), lambda g: (g, 0, 0)), whole(rows, 2), whole(3, keys)]
        + [whole(rows, LANES)] * 2,
        out_specs=[whole(rows, width), pl.BlockSpec((keys, LANES), lambda g: (0, g))],
        out_shape=[
            jax.ShapeDtypeStruct((rows, width), BF16),
            jax.ShapeDtypeStruct((keys, groups * LANES), BF16),
        ],
        scratch_shapes=[
            pltpu.VMEM((rows, keys), F32),
            pltpu.VMEM((heads, rows, LANES), BF16),
            pltpu.VMEM((heads, rows, LANES), BF16),
            pltpu.VMEM((heads, rows, 1), F32),
            pltpu.VMEM((GROUP * rows, keys), BF16),
            pltpu.VMEM((GROUP * rows, keys), BF16),
            pltpu.VMEM((heads, rows, LANES), F32),
        ],
        compiler_params=pltpu.CompilerParams(vmem_limit_bytes=48 * MIB),
        cost_estimate=pl.CostEstimate(
            flops=10 * rows * keys * LANES * heads,
            bytes_accessed=8 * q.size + 4 * keys * groups * LANES,
            transcendentals=heads * rows * keys,
        ),
        name="attend_back",
    )(q, do, att, *kvs, lse, row_info, col_info, cos, sin)


def qkv_back_kernel(
    dq_ref, mine_ref, got_ref, wq_ref, wkv_ref, x_ref, gain_ref, up_ref, ck_ref, sk_ref, dkv_ref, out_ref, gain_grad_ref
):
    cos, sin = ck_ref[...], sk_ref[...]
    for at in range(0, dkv_ref.shape[1], LANES):
        cols = slice(at, at + LANES)
        u = mine_ref[:, cols].astype(F32) + got_ref[:, cols].astype(F32)
        dkv_ref[:, cols] = (u * cos - turn(u) * sin).astype(BF16)
    g = dotf(dq_ref[...], wq_ref[...], NT) + dotf(dkv_ref[...], wkv_ref[...], NT)
    x = x_ref[...]
    factor = lax.rsqrt(jnp.mean(x * x, axis=-1, keepdims=True) + NORM_EPSILON)
    unit = x * factor
    gain_grad_ref[...] = jnp.sum(g * unit, axis=0, keepdims=True)
    scaled = g * gain_ref[...]
    out_ref[...] = up_ref[...] + factor * (scaled - unit * jnp.mean(scaled * unit, axis=-1, keepdims=True))


def qkv_back_call(dq, mine, got, wq, wkv, x, gain, upstream, cos, sin):
    rows, width = x.shape
    heads, both = wq.shape[1], wkv.shape[1]
    return pl.pallas_call(
        qkv_back_kernel,
        grid=(1,),
        in_specs=[
            whole(rows, heads),
            whole(rows, both),
            whole(rows, both),
            whole(width, heads),
            whole(width, both),
            whole(rows, width),
            whole(1, width),
            whole(rows, width),
            whole(rows, LANES),
            whole(rows, LANES),
        ],
        out_specs=[whole(rows, both), whole(rows, width), whole(1, width)],
        out_shape=[
            jax.ShapeDtypeStruct((rows, both), BF16),
            jax.ShapeDtypeStruct((rows, width), F32),
            jax.ShapeDtypeStruct((1, width), F32),
        ],
        compiler_params=pltpu.CompilerParams(vmem_limit_bytes=32 * MIB),
        cost_estimate=pl.CostEstimate(
            flops=2 * rows * width * (heads + both),
            bytes_accessed=2 * width * (heads + both) + 16 * rows * width,
            transcendentals=0,
        ),
        name="qkv_back",
    )(dq, mine, got, wq, wkv, x, gain, upstream, cos, sin)


def weight_grad_kernel(fill, counts, stride, spot_ref, *refs):
    c = pl.program_id(0)
    n_left, n_right, n_extra, levels = counts
    sources, refs = refs[: n_left * levels], refs[n_left * levels :]
    rights, refs = refs[: n_right * levels], refs[n_right * levels :]
    extra, outs, scratch = refs[:n_extra], refs[n_extra : n_extra + 5], refs[n_extra + 5 :]
    staged, turned, values, sem = scratch[:n_left], scratch[n_left : 2 * n_left], scratch[-3:-1], scratch[-1]

    @pl.when(c == 0)
    def _():
        copies = []
        for i, source in enumerate(sources):
            rows = source.shape[0]
            target = staged[i // levels].at[pl.ds(i % levels * rows, rows), :]
            copies.append(pltpu.make_async_copy(source, target, sem.at[i]))
            copies[-1].start()
        for i, copy in enumerate(copies):
            copy.wait()
            if i % levels == levels - 1:
                turned[i // levels][...] = staged[i // levels][...].T

    def product(left, right):
        stacked = jnp.concatenate([a[...] for a in rights[right * levels : (right + 1) * levels]], axis=0)
        return dotf(turned[left][...], stacked)

    core = spot_ref[1]
    fill(core, c, product, values, extra)
    each, cut = outs[4].shape[1], outs[0].shape[1]
    kept, away = values
    for r in range(4):
        mine = other = pl.multiple_of((spot_ref[0] ^ r) * stride, 16)
        source = away
        if stride != each:
            other = pl.multiple_of(mine + (1 - core) * each, 16)
            mine = pl.multiple_of(mine + core * each, 16)
            source = kept
        outs[r % 2][r // 2] = kept[pl.ds(mine, cut), :]
        outs[2 + r // 2][r % 2] = kept[pl.ds(pl.multiple_of(mine + cut, 16), each - cut), :]
        outs[4][r] = source[pl.ds(other, each), :]


def fill_rows(core, c, product, values, extra):
    values[0][...] = product(0, 0).astype(BF16)


def fill_roles(core, c, product, values, extra):
    for i, value in enumerate(values):
        value[...] = product(0, i).astype(BF16)


def fill_choice(core, c, product, values, extra):
    kept, away = values
    first, second = product(0, 0).astype(BF16), product(1, 1).astype(BF16)
    kept[...] = jnp.where(core == 0, first, second)
    away[...] = jnp.where(core == 0, second, first)


def fill_groups(core, c, product, values, extra):
    kept, away = values
    v = product(0, 0)
    part = kept.shape[1] - LANES
    low, high = v[:, :part].astype(BF16), v[:, v.shape[1] - part :].astype(BF16)
    kept[:, :part] = jnp.where(core == 0, low, high)
    away[:, :part] = jnp.where(core == 0, high, low)
    vectors = extra[0][...].T
    rest = jnp.zeros((vectors.shape[0], LANES - vectors.shape[1]), F32)
    vectors = jnp.concatenate([vectors, rest], axis=1).astype(BF16)
    kept[:, part:] = vectors
    away[:, part:] = vectors


def weight_grad(spot, fill, lefts, rights, stride, each, n, step, extra=()):
    levels, rows = len(lefts[0]), lefts[0][0].shape[0]
    depth = levels * rows
    cut = -(-each // 32) * 16
    shapes = [(2, cut, n), (2, cut, n), (2, each - cut, n), (2, each - cut, n), (4, each, n)]
    flops = 2 * depth * 4 * stride * sum(right[0].shape[1] for right in rights)
    sources, moving = [a for group in lefts for a in group], [a for group in rights for a in group]
    by_step = pl.BlockSpec((rows, step), lambda c, s: (0, c))
    at_once = lambda a: pl.BlockSpec(a.shape, lambda c, s: (0, 0))
    return pl.pallas_call(
        functools.partial(weight_grad_kernel, fill, (len(lefts), len(rights), len(extra), levels), stride),
        grid_spec=pltpu.PrefetchScalarGridSpec(
            num_scalar_prefetch=1,
            grid=(-(-n // step),),
            in_specs=[pl.BlockSpec(memory_space=pl.ANY)] * len(sources)
            + [by_step if n > step else at_once(a) for a in moving]
            + [at_once(a) for a in extra],
            out_specs=[pl.BlockSpec(s[:2] + (step,), lambda c, s: (0, 0, c)) for s in shapes],
            scratch_shapes=[pltpu.VMEM((depth, group[0].shape[1]), BF16) for group in lefts]
            + [pltpu.VMEM((group[0].shape[1], depth), BF16) for group in lefts]
            + [pltpu.VMEM((4 * stride, step), BF16)] * 2
            + [pltpu.SemaphoreType.DMA((len(sources),))],
        ),
        out_shape=[jax.ShapeDtypeStruct(s, BF16) for s in shapes],
        compiler_params=pltpu.CompilerParams(vmem_limit_bytes=60 * MIB),
        cost_estimate=pl.CostEstimate(
            flops=flops, bytes_accessed=2 * sum(a.size for a in sources + moving) + 16 * each * n, transcendentals=0
        ),
        name="weight_grad",
    )(spot, *sources, *moving, *extra)


def tie(*trees):
    return lax.optimization_barrier(trees)


def add(*terms):
    return sum(a.astype(F32) for a in terms).astype(BF16)


def at(a, index, axis):
    return lax.dynamic_index_in_dim(a, index, axis, keepdims=False)


class Place:
    def __init__(self, dp, cp):
        self.dp, self.cp, self.square = dp, cp, cp == 4
        dp_at, cp_at = lax.axis_index("dp"), lax.axis_index("cp")
        self.core, self.z = dp_at % 2, dp_at // 2
        self.y, self.x = cp_at // 2, cp_at % 2

    def over_x(self, a):
        return lax.ppermute(a, "cp", [(i, i ^ 1) for i in range(self.cp)])

    def over_y(self, a):
        return lax.ppermute(a, "cp", [(i, i ^ 2) for i in range(self.cp)])

    def over_core(self, a):
        return lax.ppermute(a, "dp", [(i, i ^ 1) for i in range(self.dp)])

    def move_tokens(self, a):
        if not self.square:
            return a
        pairs = []
        for d in range(self.dp):
            for c in range(self.cp):
                z, core, y, x = d // 2, d % 2, c // 2, c % 2
                pairs.append((d * self.cp + c, (2 * z + y) * self.cp + 2 * core + x))
        return lax.ppermute(a, ("dp", "cp"), pairs)

    def key_blocks(self):
        if not self.square:
            return list(range(self.cp)), lax.axis_index("cp")
        own = 2 * self.core + self.x
        return [own ^ k for k in range(4)], own

    def gather_keys(self, a, axis=0):
        if not self.square:
            return (lax.all_gather(a, "cp", axis=axis, tiled=True),)
        from_x, from_core = self.over_x(a), self.over_core(a)
        return a, from_x, from_core, self.over_core(from_x)

    def scatter_keys_first(self, a):
        if not self.square:
            own = lax.psum_scatter(a, "cp", scatter_dimension=0, tiled=True)
            return own, jnp.zeros_like(own)
        rows = a.shape[0] // 4
        return a[: 2 * rows], self.over_core(a[2 * rows :])

    def scatter_keys_second(self, pair):
        if not self.square:
            return pair
        rows = pair[0].shape[0] // 2
        pair = add(*pair)
        return pair[:rows], self.over_x(pair[rows:])


    def gather_first(self, a):
        if not self.square:
            return (lax.all_gather(a, "cp", axis=0, tiled=True),)
        cut = -(-a.shape[0] // 32) * 16
        top, low = a[:cut], a[cut:]
        return top, low, self.over_x(top), self.over_y(low)

    def pair_up(self, spot, mine, got, axis=0):
        return jnp.where(spot == 0, jnp.stack([mine, got], axis), jnp.stack([got, mine], axis))

    def gather_pairs(self, parts):
        if not self.square:
            return parts
        top, low, from_x, from_y = parts
        return self.pair_up(self.x, top, from_x), self.pair_up(self.y, low, from_y)

    def gather_second(self, pairs):
        if not self.square:
            return pairs
        top, low = pairs
        return top, low, self.over_y(top), self.over_x(low)

    def gather_whole(self, parts):
        if not self.square:
            return parts[0]
        top, low, from_y, from_x = parts
        a = jnp.concatenate([self.pair_up(self.y, top, from_y), self.pair_up(self.x, low, from_x, 1)], axis=2)
        return a.reshape(-1, a.shape[-1])


    def halves(self, fill, lefts, rights, stride, each, n, step, extra=()):
        if self.square:
            spot = jnp.stack([lax.axis_index("cp"), self.core]).astype(jnp.int32)
            return weight_grad(spot, fill, lefts, rights, stride, each, n, step, extra)
        products = []

        def product(left, right):
            a, b = (jnp.concatenate(group, axis=0) for group in (lefts[left], rights[right]))
            return dotf(a, b, TN).astype(BF16)

        if fill is fill_rows:
            both = product(0, 0).reshape(self.cp, 2, each, n)
            products = at(both, self.core, 1), at(both, 1 - self.core, 1)
        elif fill is fill_roles:
            products = product(0, 0), product(0, 1)
        elif fill is fill_choice:
            first, second = product(0, 0), product(1, 1)
            products = self.pick(first, second), self.pick(second, first)
        else:
            kv, part = product(0, 0), n - LANES
            low, high = kv[:, :part], kv[:, kv.shape[1] - part :]
            vectors = jnp.pad(extra[0].T, ((0, 0), (0, LANES - extra[0].shape[0]))).astype(BF16)
            products = [jnp.concatenate([self.pick(*pair), vectors], axis=1) for pair in ((low, high), (high, low))]
        return [a.reshape(self.cp, each, n) for a in products]

    def scatter_ready(self, pieces, got, apart=False):
        if not self.square:
            return (add(pieces[0], got),)
        top, top_out, low, low_out = pieces[:4]
        got = got.reshape((2, 2) + got.shape[1:])
        cut = top.shape[1]
        if apart:
            over_x = [add(top_out[i], got[i, 1, :cut]) for i in range(2)]
            over_y = [add(low_out[i], got[1, i, cut:]) for i in range(2)]
            return top, low, got, over_x, over_y
        return top, low, got, add(top_out, got[:, 1, :cut]), add(low_out, got[1, :, cut:])

    def scatter_first(self, parts):
        if not self.square:
            return (lax.psum_scatter(parts[0], "cp", scatter_dimension=0, tiled=False),)
        return parts[:3] + (self.over_x(parts[3]), self.over_y(parts[4]))

    def scatter_open(self, parts):
        if not self.square:
            return self.scatter_first(parts)
        return parts + ([self.over_x(parts[3][1])], [self.over_y(parts[4][1])])

    def scatter_more(self, parts):
        if not self.square:
            return parts
        over_x, over_y, from_x, from_y = parts[3:]
        return parts[:3] + ([self.over_x(over_x[0])] + from_x, [self.over_y(over_y[0])] + from_y)

    def scatter_second(self, parts):
        if not self.square:
            return parts
        top, low, got, from_x, from_y = parts
        cut = top.shape[1]
        top_out = add(top[1], got[1, 0, :cut], from_x[1])
        low_out = add(low[1], got[0, 1, cut:], from_y[1])
        return parts + (self.over_y(top_out), self.over_x(low_out))

    def scatter_rows(self, parts):
        if not self.square:
            half = parts[0].shape[0] // 2
            return parts[0][:half], parts[0][half:]
        top, low, got, from_x, from_y, last_y, last_x = parts
        cut = top.shape[1]
        return add(top[0], got[0, 0, :cut], from_x[0], last_y), add(low[0], got[0, 0, cut:], from_y[0], last_x)

    def scatter_whole(self, parts):
        return jnp.concatenate(self.scatter_rows(parts), axis=0)


    def hop(self, a, moves):
        return lax.ppermute(a, "dp", [(2 * s + c, 2 * t + c) for s, t in moves for c in range(2)])

    def z_first(self, a):
        n, got = self.dp // 2, jnp.zeros_like(a)
        for t in range(n // 2 - 1):
            if t:
                a = add(a, got)
            got = self.hop(a, [(t, t + 1), (n - 1 - t, n - 2 - t)])
        return a, got

    def z_second(self, pair):
        n, a = self.dp // 2, add(*pair)
        return a, self.hop(a, [(n // 2 - 1, n // 2), (n // 2, n // 2 - 1)])

    def z_third(self, pair):
        n, a = self.dp // 2, add(*pair)
        back = a
        for t in reversed(range(n // 2 - 1)):
            if t < n // 2 - 2:
                a = jnp.where((self.z == t + 1) | (self.z == n - 2 - t), back, a)
            back = self.hop(a, [(t + 1, t), (n - 2 - t, n - 1 - t)])
        return a, back

    def z_whole(self, pair):
        n = self.dp // 2
        if n < 4:
            return pair[0]
        return jnp.where((self.z == 0) | (self.z == n - 1), pair[1], pair[0])

    def pick(self, a, b):
        return jnp.where(self.core == 0, a, b)


def inverse_rms(matrix):
    return lax.rsqrt(jnp.mean(matrix * matrix, axis=-1, keepdims=True) + NORM_EPSILON)


def norm_back(matrix, gain, upstream):
    factor = inverse_rms(matrix)
    unit = matrix * factor
    scaled = upstream * gain
    grad = factor * (scaled - unit * jnp.mean(scaled * unit, axis=-1, keepdims=True))
    return grad, jnp.sum(upstream * unit, axis=0, keepdims=True)


def rope_tables(places):
    half = HEAD_DIM // 2
    inverse = jnp.power(ROPE_BASE, -2.0 * jnp.arange(half, dtype=F32) / HEAD_DIM)
    angles = places.astype(F32)[:, None] * inverse[None, :]
    cos, sin = jnp.cos(angles), jnp.sin(angles)
    cos, sin = jnp.concatenate([cos, cos], 1), jnp.concatenate([-sin, sin], 1)
    one, zero = jnp.ones_like(cos), jnp.zeros_like(sin)
    both = lambda a, b: jnp.concatenate([a, b], 1)
    return both(cos, cos), both(sin, sin), both(cos, one), both(sin, zero)


class Level:
    def __init__(self, recursion, place, context):
        self.recursion, self.place = recursion, place
        self.tables, self.row_info, self.col_info, self.depth = context

    def project(self, state, w):
        self.state = state
        self.q, self.kv, self.normed = qkv_call(state, w["gain_a"], w["q"], w["kv"], self.tables)

    def attend(self, kvs, w):
        self.kvs = kvs
        self.att, self.lse = attend_call(self.recursion, self.q, kvs, self.row_info, self.col_info)
        self.attn = dotf(self.att, w["o"])
        self.after = self.state + self.attn
        self.normed2 = (self.after * inverse_rms(self.after) * w["gain_f"]).astype(BF16)

    def expand(self, w):
        mine, theirs = dotf(self.normed2, w["mine"]), dotf(self.normed2, w["theirs"])
        gate, up = self.place.pick(mine, theirs), self.place.pick(theirs, mine)
        self.inner = (jax.nn.silu(gate) * up).astype(BF16)
        self.gate, self.up = gate.astype(BF16), up.astype(BF16)

    def close(self, w):
        self.branch = self.attn + dotf(self.inner, w["down"])
        self.router_row = w["router"][self.recursion]
        self.router = jax.nn.sigmoid(jnp.sum(self.state * self.router_row, axis=-1, keepdims=True))
        self.active = (self.depth[:, None] > self.recursion).astype(F32)
        return self.state + self.active * self.router * self.branch

    def back_open(self, grad):
        self.g_branch = grad * (self.active * self.router)
        g_logit = jnp.sum(grad * self.branch, axis=-1, keepdims=True)
        g_logit = g_logit * self.active * self.router * (1.0 - self.router)
        self.g_router = jnp.sum(g_logit * self.state, axis=0, keepdims=True)
        self.g_state = grad + g_logit * self.router_row
        self.g_ffn = self.g_branch.astype(BF16)

    def back_expand(self, w):
        g_inner = dotf(self.g_ffn, w["down"], NT)
        gate, up = self.gate.astype(F32), self.up.astype(F32)
        sig = jax.nn.sigmoid(gate)
        g_gate = (g_inner * up * sig * (1.0 + gate * (1.0 - sig))).astype(BF16)
        g_up = (g_inner * gate * sig).astype(BF16)
        self.g_mine, self.g_theirs = self.place.pick(g_gate, g_up), self.place.pick(g_up, g_gate)

    def back_norm(self, w):
        g_normed2 = dotf(self.g_mine, w["mine"], NT) + dotf(self.g_theirs, w["theirs"], NT)
        g_after, self.g_gain_f = norm_back(self.after, w["gain_f"], g_normed2)
        self.g_state = self.g_state + g_after
        self.g_attn = (g_after + self.g_branch).astype(BF16)
        self.g_att = dotf(self.g_attn, w["o"], NT).astype(BF16)

    def back_attend(self):
        cos, sin = self.tables[:2]
        self.dq, dkv = attend_back_call(
            self.recursion, self.q, self.g_att, self.att, self.kvs, self.lse, self.row_info, self.col_info, cos, sin
        )
        return dkv

    def back_project(self, mine, got, w):
        cos, sin = self.tables[2:]
        self.dkv, grad, self.g_gain_a = qkv_back_call(
            self.dq, mine, got, w["q"], w["kv"], self.state, w["gain_a"], self.g_state, cos, sin
        )
        return grad


def local(tokens, recur_depth, document_ids, cotangent, *shards, dp, cp):
    place = Place(dp, cp)
    wq, wk, wv, wo, gate, up, down, router, gain_a, gain_f = shards
    rows, each = tokens.shape[1], wq.shape[0]
    width, kv_heads = each * cp, wk.shape[1] // HEAD_DIM

    wkv = jnp.stack([wk.reshape(each, kv_heads, HEAD_DIM), wv.reshape(each, kv_heads, HEAD_DIM)], axis=2)
    wkv = wkv.reshape(each, -1)
    small = jnp.concatenate([gain_a[:, None], gain_f[:, None], router.T], axis=1)
    blend = jnp.concatenate([wkv, wq, wo], axis=1)
    half, both = blend.shape[1] // 2, wkv.shape[1]
    blend = jnp.concatenate([place.pick(blend[:, :half], blend[:, half:]), small], axis=1)
    part = place.gather_first(blend)
    ids = place.move_tokens(jnp.stack([document_ids[0], recur_depth[0]]))
    state = place.move_tokens(tokens[0])
    gates = place.pick(gate, up)
    downs = place.pick(down[: down.shape[0] // 2], down[down.shape[0] // 2 :])
    part, ids, state, gates, downs = tie(part, ids, state, gates, downs)

    part = place.gather_second(place.gather_pairs(part))
    steps = jnp.arange(rows, dtype=jnp.int32)
    blocks, block = place.key_blocks()
    every = jnp.concatenate(place.gather_keys(ids, 1), axis=1)
    spots = jnp.concatenate([b * rows + steps for b in blocks])
    col_info = jnp.stack([every[0], spots, every[1]])
    row_info = jnp.stack([ids[0], block * rows + steps], axis=1)
    tables = rope_tables(row_info[:, 1])
    context = (tables, row_info, col_info, ids[1])
    part, context, state, gates = tie(part, context, state.astype(F32), gates)

    g_part = place.gather_first(gates)
    mine = place.gather_whole(part)
    theirs = place.over_core(mine)
    w = {"gain_a": mine[:, half][None, :].astype(F32), "gain_f": mine[:, half + 1][None, :].astype(F32)}
    w["router"] = mine[:, half + 2 :].T.astype(F32)
    blend = jnp.concatenate([place.pick(mine, theirs)[:, :half], place.pick(theirs, mine)[:, :half]], axis=1)
    w["kv"], w["q"], w["o"] = blend[:, :both], blend[:, both : both + width], blend[:, both + width :]
    levels = [Level(r, place, context) for r in range(RECUR)]
    first = levels[0]
    first.project(state, w)
    g_part = place.gather_pairs(g_part)
    first.kv, g_part, downs = tie(first.kv, g_part, downs)

    kvs = place.gather_keys(first.kv)
    kvs, g_part, downs = tie(kvs, g_part, downs)

    g_part = place.gather_second(g_part)
    d_part = place.gather_first(downs)
    first.attend(kvs, w)
    first.normed2, g_part, d_part = tie(first.normed2, g_part, d_part)

    d_part = place.gather_second(place.gather_pairs(d_part))
    w["mine"] = place.gather_whole(g_part)
    w["theirs"] = place.over_core(w["mine"])
    first.expand(w)
    first.inner, d_part = tie(first.inner, d_part)

    mine = place.gather_whole(d_part)
    theirs = place.over_core(mine)
    mine, theirs = (a.reshape(cp, -1, width) for a in (mine, theirs))
    w["down"] = jnp.stack([place.pick(mine, theirs), place.pick(theirs, mine)], axis=1).reshape(-1, width)
    state = first.close(w)

    for level in levels[1:]:
        level.project(state, w)
        level.attend(place.gather_keys(level.kv), w)
        level.expand(w)
        state = level.close(w)
    activations = place.move_tokens(state.astype(BF16))[None]
    grad = place.move_tokens(cotangent[0]).astype(F32)

    for level in levels[:0:-1]:
        level.back_open(grad)
        level.back_expand(w)
        level.back_norm(w)
        pair = place.scatter_keys_second(place.scatter_keys_first(level.back_attend()))
        grad = level.back_project(*pair, w)

    every = lambda name: [getattr(level, name) for level in levels]
    ff = gate.shape[1]
    part = -(-both // (2 * LANES)) * LANES

    grad, activations = tie(grad, activations)
    first.back_open(grad)
    d = place.halves(fill_rows, [every("inner")], [every("g_ffn")], ff // cp, ff // cp // 2, width, 512)
    d_got = place.over_core(d[-1])
    first.back_expand(w)
    d = place.scatter_ready(d, d_got)
    d, first.g_mine, first.g_theirs = tie(d, first.g_mine, first.g_theirs)

    d = place.scatter_first(d)
    u = place.halves(fill_roles, [every("normed2")], [every("g_mine"), every("g_theirs")], each, each, ff, 512)
    d, u = tie(d, u)

    u_got = place.over_core(u[-1])
    d = place.scatter_second(d)
    first.back_norm(w)
    u = place.scatter_ready(u, u_got, True)
    d, u, first.g_att = tie(d, u, first.g_att)

    u = place.scatter_open(u)
    d = place.z_first(place.scatter_whole(d))
    dkv = first.back_attend()
    u, d, dkv = tie(u, d, dkv)

    u = place.scatter_more(u)
    pair = place.scatter_keys_first(dkv)
    (pair,) = tie(pair)
    pair = place.scatter_keys_second(pair)
    lefts, rights = [every("att"), every("normed")], [every("g_attn"), every("dq")]
    p = place.halves(fill_choice, lefts, rights, each, each, width, 512)
    u, pair, p = tie(u, pair, p)

    u = place.scatter_second(u)
    p_got = place.over_core(p[-1])
    d = place.z_second(d)
    grad = first.back_project(*pair, w)
    vectors = every("g_router") + [sum(every("g_gain_a")), sum(every("g_gain_f"))]
    vectors = jnp.concatenate(vectors + [jnp.zeros((8 - len(vectors), width), F32)], axis=0)
    k = place.halves(fill_groups, [every("normed")], [every("dkv")], each, each, part + LANES, part + LANES, (vectors,))
    p = place.scatter_ready(p, p_got)
    u, d, p, k, grad = tie(u, d, p, k, grad)

    p = place.scatter_first(p)
    k_got = place.over_core(k[-1])
    u, v = place.scatter_rows(u)
    u = place.z_first(u)
    k = place.scatter_ready(k, k_got)
    u, v, p, k = tie(u, v, p, k)

    p, k = place.scatter_second(p), place.scatter_first(k)
    u, v = place.z_second(u), place.z_first(v)
    u, v, p, k = tie(u, v, p, k)

    k = place.scatter_second(k)
    u, v = place.z_third(u), place.z_second(v)
    a = place.z_first(jnp.concatenate([place.scatter_whole(k), place.scatter_whole(p)], axis=1))
    u, v, a = tie(u, v, a)

    a, v = place.z_second(a), place.z_third(v)
    d = place.z_third(d)
    input_grad = place.move_tokens(grad.astype(BF16))[None]
    a, v, d, input_grad = tie(a, v, d, input_grad)

    a = place.z_third(a)
    d_own = place.z_whole(d)
    d_other = place.over_core(d_own)
    u_own = jnp.concatenate([place.z_whole(u), place.z_whole(v)], axis=0)
    u_other = place.over_core(u_own)
    grad_gate, grad_up = place.pick(u_own, u_other).astype(F32), place.pick(u_other, u_own).astype(F32)
    d_own, d_other = (b.reshape(-1, width) for b in (d_own, d_other))
    grad_down = jnp.concatenate([place.pick(d_own, d_other), place.pick(d_other, d_own)], axis=0).astype(F32)
    a, grad_gate, grad_up, grad_down = tie(a, grad_gate, grad_up, grad_down)

    own = place.z_whole(a)
    other = place.over_core(own)
    low, high = place.pick(own, other).astype(F32), place.pick(other, own).astype(F32)
    grad_kv = jnp.concatenate([low[:, :part], high[:, 2 * part - both : part]], axis=1)
    grad_kv = grad_kv.reshape(each, -1, 2, HEAD_DIM)
    vectors = low[:, part : part + RECUR + 2].T
    return (
        activations,
        input_grad,
        high[:, part + LANES :],
        grad_kv[:, :, 0].reshape(each, -1),
        grad_kv[:, :, 1].reshape(each, -1),
        low[:, part + LANES :],
        grad_gate,
        grad_up,
        grad_down,
        vectors[:RECUR],
        vectors[RECUR],
        vectors[RECUR + 1],
    )


def solution(mesh):
    by_token = P("dp", "cp", None)
    by_row = P("cp", None)
    in_specs = (by_token, P("dp", "cp"), P("dp", "cp"), by_token) + (by_row,) * 7 + (P(None, "cp"), P("cp"), P("cp"))
    out_specs = (by_token, by_token) + (by_row,) * 7 + (P(None, "cp"), P("cp"), P("cp"))
    step = functools.partial(local, dp=mesh.shape["dp"], cp=mesh.shape["cp"])
    return jax.shard_map(step, mesh=mesh, in_specs=in_specs, out_specs=out_specs, check_vma=False)
```

```python
import functools

import jax
import jax.numpy as jnp
from jax import lax
from jax.experimental import pallas as pl
from jax.experimental.pallas import tpu as pltpu
from jax.sharding import PartitionSpec as P

HEAD_DIM = 64
LANES = 128
GROUP = 3
RECUR = 3
NORM_EPSILON = 1e-05
MASKED_SCORE = -1e30
ROPE_BASE = 10000.0
SCALE = HEAD_DIM ** (-0.5)
MIB = 2**20
F32, BF16 = jnp.float32, jnp.bfloat16
NN = (((1,), (0,)), ((), ()))
NT = (((1,), (1,)), ((), ()))
TN = (((0,), (0,)), ((), ()))


def dotf(a, b, dims=NN):
    return lax.dot_general(a, b, dims, preferred_element_type=F32)


def turn(u):
    lane = lax.broadcasted_iota(jnp.int32, u.shape, 1) % HEAD_DIM
    return jnp.where(lane < HEAD_DIM // 2, pltpu.roll(u, LANES - 32, 1), pltpu.roll(u, 32, 1))


def variants_of(rows, keys):
    pick = lambda count, third, unit: (count * third // 3 // unit + 1) * unit
    return tuple((pick(rows, k, 32), pick(keys, k, LANES)) for k in (1, 2)) + ((rows, keys),)


def choose(meta_ref, variants, body):
    if len(variants) == 1:
        body(*variants[0])
    else:
        for i, variant in enumerate(variants):
            pl.when(meta_ref[0] == i)(functools.partial(body, *variant))


def clear(m, *refs):
    for ref in refs:
        if m < ref.shape[0]:
            ref[m:, :] = jnp.zeros((ref.shape[0] - m, ref.shape[1]), ref.dtype)


def call(kernel, name, meta, grid, inputs, in_specs, out_specs, out_shape, scratch, vmem, flops, traffic):
    return pl.pallas_call(
        kernel,
        grid_spec=pltpu.PrefetchScalarGridSpec(
            num_scalar_prefetch=1, grid=grid, in_specs=in_specs, out_specs=out_specs, scratch_shapes=scratch
        ),
        out_shape=out_shape,
        compiler_params=pltpu.CompilerParams(vmem_limit_bytes=vmem * MIB),
        cost_estimate=pl.CostEstimate(flops=flops, bytes_accessed=traffic, transcendentals=0),
        name=name,
    )(meta, *inputs)


def whole(*shape):
    return pl.BlockSpec(shape, lambda g, s: (0,) * len(shape))


def turns(table, keys):
    cos, sin = table[:, :LANES], table[:, LANES : 2 * LANES]
    if not keys:
        return cos, sin
    lane = lax.broadcasted_iota(jnp.int32, cos.shape, 1)
    return jnp.where(lane < HEAD_DIM, cos, 1.0), jnp.where(lane < HEAD_DIM, sin, 0.0)


def qkv_kernel(
    variants, meta_ref, x_ref, gain_ref, wq_ref, wkv_ref, table_ref, q_ref, kv_ref, normed_ref
):
    width = q_ref.shape[1]

    def body(m, _):
        x = x_ref[:m]
        factor = lax.rsqrt(jnp.mean(x * x, axis=-1, keepdims=True) + NORM_EPSILON)
        normed = (x * factor * gain_ref[...]).astype(BF16)
        normed_ref[:m, :] = normed
        kv = dotf(normed, wkv_ref[...])
        cos, sin = turns(table_ref[:m], True)
        for at in range(0, kv_ref.shape[1], LANES):
            u = kv[:, at : at + LANES]
            kv_ref[:m, at : at + LANES] = (u * cos + turn(u) * sin).astype(BF16)
        q = dotf(normed, wq_ref[:, :width])
        cos, sin = turns(table_ref[:m], False)
        for at in range(0, width, LANES):
            if at + LANES <= width:
                u = q[:, at : at + LANES]
            else:
                u = jnp.concatenate([q[:, at:], jnp.zeros((m, at + LANES - width), F32)], axis=1)
            r = (u * cos + turn(u) * sin).astype(BF16)
            q_ref[:m, at : min(at + LANES, width)] = r[:, : min(LANES, width - at)]
        clear(m, q_ref, kv_ref, normed_ref)

    choose(meta_ref, variants, body)


def qkv_call(variants, meta, x, gain, wq, wkv, table):
    rows, width = x.shape
    both = wkv.shape[1]
    return call(
        functools.partial(qkv_kernel, variants),
        "norm_qkv_rope",
        meta,
        (1,),
        (x, gain, wq, wkv, table),
        [whole(rows, width), whole(1, width), whole(*wq.shape), whole(width, both), whole(*table.shape)],
        [whole(rows, width), whole(rows, both), whole(rows, width)],
        [jax.ShapeDtypeStruct((rows, k), BF16) for k in (width, both, width)],
        [],
        32,
        2 * rows * width * (width + both),
        2 * width * (width + both) + 8 * rows * width,
    )


def make_bias(row_table, col_info, recursion):
    doc_r, pos_r = (row_table[:, k : k + 1].astype(jnp.int32) for k in (2 * LANES + HEAD_DIM, 3 * LANES + HEAD_DIM))
    doc_c, pos_c, depth_c = col_info[0:1, :], col_info[1:2, :], col_info[2:3, :]
    live = (depth_c > recursion) | (pos_c == pos_r)
    allowed = (pos_c <= pos_r) & (doc_c == doc_r) & live
    return jnp.where(allowed, 0.0, MASKED_SCORE).astype(F32)


def split_pairs(packed, out, to_left):
    rows, width = packed.shape
    lane = lax.broadcasted_iota(jnp.int32, (rows, LANES), 1)
    for at in range(0, width, LANES):
        h = at // HEAD_DIM
        if at + LANES <= width:
            u = packed[:, at : at + LANES].astype(F32)
        else:
            u = jnp.concatenate([packed[:, at:].astype(F32), jnp.zeros((rows, at + LANES - width), F32)], axis=1)
        v = pltpu.roll(u, HEAD_DIM, 1)
        first, second = (u, v) if to_left else (v, u)
        keep = (lane < HEAD_DIM) if to_left else (lane >= HEAD_DIM)
        out[h] = jnp.where(keep, first, 0.0).astype(out.dtype)
        if at + LANES <= width:
            out[h + 1] = jnp.where(keep, second, 0.0).astype(out.dtype)


def join_pairs(scr, out_ref, from_left):
    heads = scr.shape[0]
    lane = lax.broadcasted_iota(jnp.int32, scr.shape[1:], 1)
    for h in range(0, heads, 2):
        at = h * HEAD_DIM
        a = scr[h] if from_left else pltpu.roll(scr[h], HEAD_DIM, 1)
        if h + 1 < heads:
            b = pltpu.roll(scr[h + 1], HEAD_DIM, 1) if from_left else scr[h + 1]
            out_ref[:, at : at + LANES] = jnp.where(lane < HEAD_DIM, a, b).astype(out_ref.dtype)
        else:
            out_ref[:, at : at + HEAD_DIM] = a[:, :HEAD_DIM].astype(out_ref.dtype)


def compact_keys(meta_ref, key_refs, rows, keys):
    block = 0
    for ref in key_refs:
        for first in range(0, ref.shape[0], rows):
            keys[pl.ds(pl.multiple_of(meta_ref[2 + 2 * block], 16), rows), :] = ref[first : first + rows, :]
            block += 1


def attend_kernel(recursion, variants, count, meta_ref, q_ref, *refs):
    key_refs, (row_ref, col_ref, att_ref, lse_ref, keys, bias, q_all, o_all) = refs[:count], refs[count:]
    g = pl.program_id(0)
    rows = q_ref.shape[0]

    @pl.when(g == 0)
    def _():
        lse_ref[...] = jnp.zeros_like(lse_ref)
        split_pairs(q_ref[...], q_all, True)

    keys[...] = jnp.zeros_like(keys)
    compact_keys(meta_ref, key_refs, rows, keys)

    def body(m, n):
        @pl.when(g == 0)
        def _():
            bias[:m, :n] = make_bias(row_ref[:m], col_ref[:, :n], recursion)

        kv = keys[:n, :]
        for j in range(GROUP):
            h = g * GROUP + j
            s = dotf(q_all[h, :m], kv, NT) * SCALE + bias[:m, :n]
            peak = jnp.max(s, axis=1, keepdims=True)
            e = jnp.exp(s - peak)
            total = jnp.sum(e, axis=1, keepdims=True)
            o_all[h, :m] = dotf(e.astype(BF16), kv) / total
            lane = lax.broadcasted_iota(jnp.int32, (m, LANES), 1)
            lse_ref[:m, :] = jnp.where(lane == h, peak + jnp.log(total), lse_ref[:m, :])
            if m < rows:
                o_all[h, m:] = jnp.zeros((rows - m, LANES), F32)

    choose(meta_ref, variants, body)

    @pl.when(g == pl.num_programs(0) - 1)
    def _():
        join_pairs(o_all, att_ref, False)


def attend_call(recursion, variants, meta, q, kvs, row_info, col_info):
    rows, width = q.shape
    keys = sum(k.shape[0] for k in kvs)
    groups = kvs[0].shape[1] // LANES
    heads = groups * GROUP
    return call(
        functools.partial(attend_kernel, recursion, variants, len(kvs)),
        "attend",
        meta,
        (groups,),
        (q, *kvs, row_info, col_info),
        [whole(rows, width)]
        + [pl.BlockSpec((k.shape[0], LANES), lambda g, s: (0, g)) for k in kvs]
        + [whole(*row_info.shape), whole(3, keys)],
        [whole(rows, width), whole(rows, LANES), pl.BlockSpec((keys, LANES), lambda g, s: (0, g))],
        [
            jax.ShapeDtypeStruct((rows, width), BF16),
            jax.ShapeDtypeStruct((rows, LANES), F32),
            jax.ShapeDtypeStruct((keys, groups * LANES), BF16),
        ],
        [
            pltpu.VMEM((rows, keys), F32),
            pltpu.VMEM((heads, rows, LANES), BF16),
            pltpu.VMEM((heads, rows, LANES), F32),
        ],
        24,
        4 * rows * keys * LANES * heads,
        4 * q.size + 2 * keys * groups * LANES,
    )


def attend_back_kernel(
    recursion, variants, meta_ref, q_ref, do_ref, att_ref, keys, lse_ref, row_ref, col_ref, dq_ref, dkv_ref,
    bias, back, q_all, do_all, dot_all, p3, ds3, dq_all,
):
    g = pl.program_id(0)
    rows, width = q_ref.shape

    @pl.when(g == 0)
    def _():
        split_pairs(q_ref[...], q_all, True)
        split_pairs(do_ref[...], do_all, False)
        prod = do_ref[...].astype(F32) * att_ref[...].astype(F32)
        for h in range(width // HEAD_DIM):
            dot_all[h] = jnp.sum(prod[:, h * HEAD_DIM : (h + 1) * HEAD_DIM], axis=1, keepdims=True)

    def body(m, n):
        @pl.when(g == 0)
        def _():
            bias[:m, :n] = make_bias(row_ref[:m], col_ref[:, :n], recursion)

        kv = keys[:n, :]
        cos, sin = turns(row_ref[:m], False)
        for j in range(GROUP):
            h = g * GROUP + j
            here = slice(j * m, (j + 1) * m)
            s = dotf(q_all[h, :m], kv, NT) * SCALE + bias[:m, :n]
            lane = lax.broadcasted_iota(jnp.int32, (m, LANES), 1)
            p = jnp.exp(s - jnp.sum(jnp.where(lane == h, lse_ref[:m], 0.0), axis=1, keepdims=True))
            dp = dotf(do_all[h, :m], kv, NT)
            ds = (p * (dp - dot_all[h, :m])).astype(BF16)
            p3[here, :n] = p.astype(BF16)
            ds3[here, :n] = ds
            dq = dotf(ds, kv) * SCALE
            dq_all[h, :m] = dq * cos - turn(dq) * sin
            if m < rows:
                dq_all[h, m:] = jnp.zeros((rows - m, LANES), F32)
        q3 = jnp.concatenate([q_all[g * GROUP + j, :m] for j in range(GROUP)], axis=0)
        do3 = jnp.concatenate([do_all[g * GROUP + j, :m] for j in range(GROUP)], axis=0)
        dkv = dotf(q3, ds3[: GROUP * m, :n], TN) * SCALE + dotf(do3, p3[: GROUP * m, :n], TN)
        back[:n, :] = dkv.T

    choose(meta_ref, variants, body)
    spot = lax.broadcasted_iota(jnp.int32, (rows, LANES), 0)
    for block in range(dkv_ref.shape[0] // rows):
        part = back[pl.ds(pl.multiple_of(meta_ref[2 + 2 * block], 16), rows), :]
        part = jnp.where(spot < meta_ref[3 + 2 * block], part, 0.0)
        dkv_ref[block * rows : (block + 1) * rows, :] = part.astype(BF16)

    @pl.when(g == pl.num_programs(0) - 1)
    def _():
        join_pairs(dq_all, dq_ref, True)


def attend_back_call(recursion, variants, meta, q, do, att, kv, lse, row_info, col_info):
    rows, width = q.shape
    keys, groups = kv.shape[0], kv.shape[1] // LANES
    heads = groups * GROUP
    return call(
        functools.partial(attend_back_kernel, recursion, variants),
        "attend_back",
        meta,
        (groups,),
        (q, do, att, kv, lse, row_info, col_info),
        [whole(rows, width)] * 3
        + [pl.BlockSpec((keys, LANES), lambda g, s: (0, g)), whole(rows, LANES), whole(*row_info.shape), whole(3, keys)],
        [whole(rows, width), pl.BlockSpec((keys, LANES), lambda g, s: (0, g))],
        [jax.ShapeDtypeStruct((rows, width), BF16), jax.ShapeDtypeStruct((keys, groups * LANES), BF16)],
        [
            pltpu.VMEM((rows, keys), F32),
            pltpu.VMEM((keys, LANES), F32),
            pltpu.VMEM((heads, rows, LANES), BF16),
            pltpu.VMEM((heads, rows, LANES), BF16),
            pltpu.VMEM((heads, rows, 1), F32),
            pltpu.VMEM((GROUP * rows, keys), BF16),
            pltpu.VMEM((GROUP * rows, keys), BF16),
            pltpu.VMEM((heads, rows, LANES), F32),
        ],
        32,
        10 * rows * keys * LANES * heads,
        8 * q.size + 4 * keys * groups * LANES,
    )


IN_VMEM = pl.BlockSpec(memory_space=pltpu.VMEM)


def inverse(x):
    return lax.rsqrt(jnp.mean(x * x, axis=-1, keepdims=True) + NORM_EPSILON)


def sigmoid(x):
    return 1.0 / (1.0 + jnp.exp(-x))


def roles(core, a, b):
    return jnp.where(core == 0, a, b), jnp.where(core == 0, b, a)


def by_steps(width, step, do):
    def one(c, _):
        do(pl.ds(pl.multiple_of(c * step, step), step))
        return 0

    lax.fori_loop(0, width // step, one, 0)


def post_kernel(variants, step, meta_ref, att, state, wo, gain, router_row, active, mine, theirs, down, *refs):
    following, after, normed2, branch, router, gate_ref, up_ref, inner_ref = refs
    core, width = meta_ref[1], state.shape[1]

    def body(m, _):
        attn = dotf(att[:m], wo[:, :width])
        x = state[:m] + attn
        after[:m, :] = x
        normed2[:m, :] = (x * inverse(x) * gain[...]).astype(BF16)
        branch[:m, :] = attn

        def part(cols):
            n2 = normed2[:m, :]
            gate, up = roles(core, dotf(n2, mine[:, cols]), dotf(n2, theirs[:, cols]))
            inner = (gate * sigmoid(gate) * up).astype(BF16)
            inner_ref[:m, cols] = inner
            gate_ref[:m, cols] = gate.astype(BF16)
            up_ref[:m, cols] = up.astype(BF16)
            branch[:m, :] += dotf(inner, down[cols, :])

        by_steps(inner_ref.shape[1], step, part)
        clear(m, after, normed2, branch, inner_ref, gate_ref, up_ref)

    choose(meta_ref, variants, body)
    x = state[...]
    router[...] = sigmoid(jnp.sum(x * router_row[...], axis=-1, keepdims=True))
    following[...] = x + active[...] * router[...] * branch[...]


def post_call(variants, meta, att, state, w, router_row, active, step=512):
    rows, width = state.shape
    ff = w["mine"].shape[1]
    shape = jax.ShapeDtypeStruct
    inputs = (att, state, w["wide_o"], w["gain_f"], router_row, active, w["mine"], w["theirs"], w["down"])
    outputs = [shape((rows, width), F32), shape((rows, width), F32), shape((rows, width), BF16), shape((rows, width), F32)]
    outputs += [shape((rows, 1), F32)] + [shape((rows, ff), BF16)] * 3
    return call(
        functools.partial(post_kernel, variants, step),
        "post",
        meta,
        (1,),
        inputs,
        [IN_VMEM] * len(inputs),
        [IN_VMEM] * len(outputs),
        outputs,
        [],
        16,
        2 * rows * width * (width + 3 * ff),
        2 * width * (width + 3 * ff),
    )


def post_back_kernel(
    variants, step, meta_ref, grad, branch, state, after, router, active, router_row, gain, wo, gate_ref, up_ref, mine, theirs,
    down, g_ffn, g_state, g_attn, g_att, g_router, g_gain, g_mine_ref, g_theirs_ref, g_branch, g_normed2,
):
    core, width = meta_ref[1], state.shape[1]

    def body(m, _):
        g = grad[:m]
        weight = active[:m] * router[:m]
        logit = jnp.sum(g * branch[:m], axis=-1, keepdims=True) * weight * (1.0 - router[:m])
        g_router[...] = jnp.sum(logit * state[:m], axis=0, keepdims=True)
        g_state[:m, :] = g + logit * router_row[...]
        if m < grad.shape[0]:
            g_state[m:, :] = grad[m:]
        low = g * weight
        g_branch[:m, :] = low
        g_ffn[:m, :] = low.astype(BF16)
        g_normed2[:m, :] = jnp.zeros((m, width), F32)

        def part(cols):
            g_inner = dotf(g_ffn[:m, :], down[cols, :], NT)
            gate, up = gate_ref[:m, cols].astype(F32), up_ref[:m, cols].astype(F32)
            sig = sigmoid(gate)
            g_gate = (g_inner * up * sig * (1.0 + gate * (1.0 - sig))).astype(BF16)
            g_up = (g_inner * gate * sig).astype(BF16)
            g_mine, g_theirs = roles(core, g_gate, g_up)
            g_mine_ref[:m, cols] = g_mine
            g_theirs_ref[:m, cols] = g_theirs
            g_normed2[:m, :] += dotf(g_mine, mine[:, cols], NT) + dotf(g_theirs, theirs[:, cols], NT)

        by_steps(gate_ref.shape[1], step, part)
        x, g = after[:m], g_normed2[:m, :]
        factor = inverse(x)
        unit = x * factor
        g_gain[...] = jnp.sum(g * unit, axis=0, keepdims=True)
        scaled = g * gain[...]
        g_after = factor * (scaled - unit * jnp.mean(scaled * unit, axis=-1, keepdims=True))
        g_state[:m, :] += g_after
        low = (g_after + g_branch[:m, :]).astype(BF16)
        g_attn[:m, :] = low
        g_att[:m, :] = dotf(low, wo[:, :width], NT).astype(BF16)
        clear(m, g_ffn, g_attn, g_att, g_mine_ref, g_theirs_ref)

    choose(meta_ref, variants, body)


def expand_back_kernel(step, meta_ref, g_ffn, gate_ref, up_ref, down, g_mine_ref, g_theirs_ref):
    core = meta_ref[1]

    def part(cols):
        g_inner = dotf(g_ffn[...], down[cols, :], NT)
        gate, up = gate_ref[:, cols].astype(F32), up_ref[:, cols].astype(F32)
        sig = sigmoid(gate)
        g_gate = (g_inner * up * sig * (1.0 + gate * (1.0 - sig))).astype(BF16)
        g_up = (g_inner * gate * sig).astype(BF16)
        g_mine_ref[:, cols], g_theirs_ref[:, cols] = roles(core, g_gate, g_up)

    by_steps(gate_ref.shape[1], step, part)


def expand_back_call(meta, g_ffn, gate, up, w, step=512):
    inputs = (g_ffn, gate, up, w["down"])
    return call(
        functools.partial(expand_back_kernel, step),
        "expand_back",
        meta,
        (1,),
        inputs,
        [IN_VMEM] * len(inputs),
        [IN_VMEM] * 2,
        [jax.ShapeDtypeStruct(gate.shape, BF16)] * 2,
        [],
        16,
        2 * gate.size * g_ffn.shape[1],
        2 * w["down"].size,
    )


def norm_back_kernel(step, meta_ref, g_mine, g_theirs, mine, theirs, after, gain, g_branch, grad, wo, g_state, g_attn, g_att, g_gain):
    width = after.shape[1]
    g = dotf(g_mine[...], mine[...], NT) + dotf(g_theirs[...], theirs[...], NT)
    x = after[...]
    factor = inverse(x)
    unit = x * factor
    g_gain[...] = jnp.sum(g * unit, axis=0, keepdims=True)
    scaled = g * gain[...]
    g_after = factor * (scaled - unit * jnp.mean(scaled * unit, axis=-1, keepdims=True))
    g_state[...] = grad[...] + g_after
    low = (g_after + g_branch[...]).astype(BF16)
    g_attn[...] = low
    g_att[...] = dotf(low, wo[:, :width], NT).astype(BF16)


def norm_back_call(meta, g_mine, g_theirs, after, g_branch, grad, w, step=512):
    rows, width = after.shape
    inputs = (g_mine, g_theirs, w["mine"], w["theirs"], after, w["gain_f"], g_branch, grad, w["wide_o"])
    shape = jax.ShapeDtypeStruct
    outputs = [shape((rows, width), k) for k in (F32, BF16, BF16)] + [shape((1, width), F32)]
    return call(
        functools.partial(norm_back_kernel, step),
        "norm_back",
        meta,
        (1,),
        inputs,
        [IN_VMEM] * len(inputs),
        [IN_VMEM] * len(outputs),
        outputs,
        [],
        16,
        2 * rows * width * (width + 2 * g_mine.shape[1]),
        2 * width * (width + 2 * g_mine.shape[1]),
    )


def post_back_call(variants, meta, grad, branch, state, after, router, active, router_row, gate, up, w, step=512):
    rows, width = state.shape
    ff = w["mine"].shape[1]
    shape = jax.ShapeDtypeStruct
    inputs = (grad, branch, state, after, router, active, router_row, w["gain_f"], w["wide_o"], gate, up)
    inputs += (w["mine"], w["theirs"], w["down"])
    outputs = [shape((rows, width), k) for k in (BF16, F32, BF16, BF16)]
    outputs += [shape((1, width), F32)] * 2 + [shape((rows, ff), BF16)] * 2
    return call(
        functools.partial(post_back_kernel, variants, step),
        "post_back",
        meta,
        (1,),
        inputs,
        [IN_VMEM] * len(inputs),
        [IN_VMEM] * len(outputs),
        outputs,
        [pltpu.VMEM((rows, width), F32)] * 2,
        16,
        2 * rows * width * (width + 3 * ff),
        2 * width * (width + 3 * ff),
    )


def qkv_back_kernel(
    variants, meta_ref, dq_ref, mine_ref, got_ref, wq_ref, wkv_ref, x_ref, gain_ref, up_ref, table_ref,
    dkv_ref, out_ref, gain_grad_ref,
):
    def body(m, _):
        cos, sin = turns(table_ref[:m], True)
        for at in range(0, dkv_ref.shape[1], LANES):
            cols = slice(at, at + LANES)
            u = mine_ref[:m, cols].astype(F32) + got_ref[:m, cols].astype(F32)
            dkv_ref[:m, cols] = (u * cos - turn(u) * sin).astype(BF16)
        clear(m, dkv_ref)
        g = dotf(dq_ref[:m], wq_ref[:, : dq_ref.shape[1]], NT) + dotf(dkv_ref[:m, :], wkv_ref[...], NT)
        x = x_ref[:m]
        factor = inverse(x)
        unit = x * factor
        gain_grad_ref[...] = jnp.sum(g * unit, axis=0, keepdims=True)
        scaled = g * gain_ref[...]
        out_ref[:m, :] = up_ref[:m] + factor * (scaled - unit * jnp.mean(scaled * unit, axis=-1, keepdims=True))
        if m < up_ref.shape[0]:
            out_ref[m:, :] = up_ref[m:]

    choose(meta_ref, variants, body)


def qkv_back_call(variants, meta, dq, mine, got, wq, wkv, x, gain, upstream, table):
    rows, width = x.shape
    both = wkv.shape[1]
    full, row, keys = whole(rows, width), whole(1, width), whole(rows, both)
    return call(
        functools.partial(qkv_back_kernel, variants),
        "qkv_back",
        meta,
        (1,),
        (dq, mine, got, wq, wkv, x, gain, upstream, table),
        [full, keys, keys, whole(*wq.shape), whole(width, both), full, row, full, whole(*table.shape)],
        [keys, full, row],
        [
            jax.ShapeDtypeStruct((rows, both), BF16),
            jax.ShapeDtypeStruct((rows, width), F32),
            jax.ShapeDtypeStruct((1, width), F32),
        ],
        [],
        32,
        2 * rows * width * (width + both),
        2 * width * (width + both) + 16 * rows * width,
    )


def weight_grad_kernel(fill, counts, stride, spot_ref, *refs):
    c = pl.program_id(0)
    n_left, n_right, n_extra, levels = counts
    sources, refs = refs[: n_left * levels], refs[n_left * levels :]
    rights, refs = refs[: n_right * levels], refs[n_right * levels :]
    extra, outs, scratch = refs[:n_extra], refs[n_extra : n_extra + 5], refs[n_extra + 5 :]
    staged, turned, values, sem = scratch[:n_left], scratch[n_left : 2 * n_left], scratch[-3:-1], scratch[-1]

    @pl.when(c == 0)
    def _():
        copies = []
        for i, source in enumerate(sources):
            rows = source.shape[0]
            target = staged[i // levels].at[pl.ds(i % levels * rows, rows), :]
            copies.append(pltpu.make_async_copy(source, target, sem.at[i]))
            copies[-1].start()
        for i, copy in enumerate(copies):
            copy.wait()
            if i % levels == levels - 1:
                turned[i // levels][...] = staged[i // levels][...].T

    def product(left, right):
        stacked = jnp.concatenate([a[...] for a in rights[right * levels : (right + 1) * levels]], axis=0)
        return dotf(turned[left][...], stacked)

    core = spot_ref[1]
    fill(core, c, product, values, extra)
    each, cut = outs[4].shape[1], outs[0].shape[1]
    kept, away = values
    for r in range(4):
        mine = other = pl.multiple_of((spot_ref[0] ^ r) * stride, 16)
        source = away
        if stride != each:
            other = pl.multiple_of(mine + (1 - core) * each, 16)
            mine = pl.multiple_of(mine + core * each, 16)
            source = kept
        outs[r % 2][r // 2] = kept[pl.ds(mine, cut), :]
        outs[2 + r // 2][r % 2] = kept[pl.ds(pl.multiple_of(mine + cut, 16), each - cut), :]
        outs[4][r] = source[pl.ds(other, each), :]


def fill_rows(core, c, product, values, extra):
    values[0][...] = product(0, 0).astype(BF16)


def fill_roles(core, c, product, values, extra):
    for i, value in enumerate(values):
        value[...] = product(0, i).astype(BF16)


def fill_choice(core, c, product, values, extra):
    kept, away = values
    first, second = product(0, 0).astype(BF16), product(1, 1).astype(BF16)
    kept[...] = jnp.where(core == 0, first, second)
    away[...] = jnp.where(core == 0, second, first)


def fill_groups(core, c, product, values, extra):
    kept, away = values
    v = product(0, 0)
    part = kept.shape[1] - LANES
    low, high = v[:, :part].astype(BF16), v[:, v.shape[1] - part :].astype(BF16)
    kept[:, :part] = jnp.where(core == 0, low, high)
    away[:, :part] = jnp.where(core == 0, high, low)
    vectors = extra[0][...].T
    rest = jnp.zeros((vectors.shape[0], LANES - vectors.shape[1]), F32)
    vectors = jnp.concatenate([vectors, rest], axis=1).astype(BF16)
    kept[:, part:] = vectors
    away[:, part:] = vectors


def weight_grad(spot, fill, lefts, rights, stride, each, n, step, extra=()):
    levels, rows = len(lefts[0]), lefts[0][0].shape[0]
    depth = levels * rows
    cut = -(-each // 32) * 16
    shapes = [(2, cut, n), (2, cut, n), (2, each - cut, n), (2, each - cut, n), (4, each, n)]
    flops = 2 * depth * 4 * stride * sum(right[0].shape[1] for right in rights)
    sources, moving = [a for group in lefts for a in group], [a for group in rights for a in group]
    by_step = pl.BlockSpec((rows, step), lambda c, s: (0, c))
    at_once = lambda a: pl.BlockSpec(a.shape, lambda c, s: (0, 0))
    return pl.pallas_call(
        functools.partial(weight_grad_kernel, fill, (len(lefts), len(rights), len(extra), levels), stride),
        grid_spec=pltpu.PrefetchScalarGridSpec(
            num_scalar_prefetch=1,
            grid=(-(-n // step),),
            in_specs=[pl.BlockSpec(memory_space=pl.ANY)] * len(sources)
            + [by_step if n > step else at_once(a) for a in moving]
            + [at_once(a) for a in extra],
            out_specs=[pl.BlockSpec(s[:2] + (step,), lambda c, s: (0, 0, c)) for s in shapes],
            scratch_shapes=[pltpu.VMEM((depth, group[0].shape[1]), BF16) for group in lefts]
            + [pltpu.VMEM((group[0].shape[1], depth), BF16) for group in lefts]
            + [pltpu.VMEM((4 * stride, step), BF16)] * 2
            + [pltpu.SemaphoreType.DMA((len(sources),))],
        ),
        out_shape=[jax.ShapeDtypeStruct(s, BF16) for s in shapes],
        compiler_params=pltpu.CompilerParams(vmem_limit_bytes=24 * MIB),
        cost_estimate=pl.CostEstimate(
            flops=flops, bytes_accessed=2 * sum(a.size for a in sources + moving) + 16 * each * n, transcendentals=0
        ),
        name="weight_grad",
    )(spot, *sources, *moving, *extra)


def settle_kernel(moves, spot_ref, *refs):
    out = refs[-1]
    for i, first, rows, place in moves:
        out[pl.ds(pl.multiple_of(place(spot_ref), 16), rows), :] = refs[i][first : first + rows, : out.shape[1]]


def copy_call(kernel, name, spot, arrays, shapes):
    return pl.pallas_call(
        kernel,
        grid_spec=pltpu.PrefetchScalarGridSpec(
            num_scalar_prefetch=1,
            grid=(1,),
            in_specs=[pl.BlockSpec(a.shape, lambda g, s: (0, 0)) for a in arrays],
            out_specs=[pl.BlockSpec(shape, lambda g, s: (0, 0)) for shape in shapes],
        ),
        out_shape=[jax.ShapeDtypeStruct(shape, arrays[0].dtype) for shape in shapes],
        compiler_params=pltpu.CompilerParams(vmem_limit_bytes=32 * MIB),
        cost_estimate=pl.CostEstimate(flops=0, bytes_accessed=4 * sum(a.size for a in arrays), transcendentals=0),
        name=name,
    )(spot, *arrays)


def settle_call(spot, arrays, moves, rows, width=None):
    shape = (rows, width or arrays[0].shape[1])
    (out,) = copy_call(functools.partial(settle_kernel, moves), "settle", spot, arrays, [shape])
    return out


def unpack_kernel(part, spot_ref, mine, theirs, q_out, o_out, kv_out, tail_out):
    both = kv_out.shape[1]
    tail_out[...] = mine[:, mine.shape[1] - LANES :]

    def go(first, second):
        q_out[...] = first[:, part:]
        o_out[...] = second[:, part:]
        kv_out[:, :part] = first[:, :part]
        kv_out[:, part:] = second[:, 2 * part - both : part]

    pl.when(spot_ref[1] == 0)(lambda: go(mine, theirs))
    pl.when(spot_ref[1] == 1)(lambda: go(theirs, mine))


def unpack_call(spot, mine, theirs, part, both):
    rows, width = mine.shape
    shapes = [(rows, width - part), (rows, width - part), (rows, both), (rows, LANES)]
    return copy_call(functools.partial(unpack_kernel, part), "unpack", spot, (mine, theirs), shapes)


def tie(*trees):
    return lax.optimization_barrier(trees)


def add(*terms):
    return sum(a.astype(F32) for a in terms).astype(BF16)


def at(a, index, axis):
    return lax.dynamic_index_in_dim(a, index, axis, keepdims=False)


class Place:
    def __init__(self, dp, cp):
        self.dp, self.cp, self.square = dp, cp, cp == 4
        dp_at, cp_at = lax.axis_index("dp"), lax.axis_index("cp")
        self.core, self.z = dp_at % 2, dp_at // 2
        self.y, self.x = cp_at // 2, cp_at % 2
        self.spot = jnp.stack([cp_at, self.core]).astype(jnp.int32)

    def over_x(self, a):
        return lax.ppermute(a, "cp", [(i, i ^ 1) for i in range(self.cp)])

    def over_y(self, a):
        return lax.ppermute(a, "cp", [(i, i ^ 2) for i in range(self.cp)])

    def over_core(self, a):
        return lax.ppermute(a, "dp", [(i, i ^ 1) for i in range(self.dp)])

    def move_tokens(self, a):
        if not self.square:
            return a
        pairs = []
        for d in range(self.dp):
            for c in range(self.cp):
                z, core, y, x = d // 2, d % 2, c // 2, c % 2
                pairs.append((d * self.cp + c, (2 * z + y) * self.cp + 2 * core + x))
        return lax.ppermute(a, ("dp", "cp"), pairs)

    def key_block(self):
        return 2 * self.core + self.x if self.square else lax.axis_index("cp")

    def gather_keys(self, a, axis=0):
        if not self.square:
            return (lax.all_gather(a, "cp", axis=axis, tiled=True),)
        from_x, from_core = self.over_x(a), self.over_core(a)
        return a, from_x, from_core, self.over_core(from_x)

    def scatter_keys_first(self, a):
        if not self.square:
            own = lax.psum_scatter(a, "cp", scatter_dimension=0, tiled=True)
            return own, jnp.zeros_like(own)
        rows = a.shape[0] // 4
        return a[: 2 * rows], self.over_core(a[2 * rows :])

    def scatter_keys_second(self, pair):
        if not self.square:
            return pair
        rows = pair[0].shape[0] // 2
        pair = add(*pair)
        return pair[:rows], self.over_x(pair[rows:])


    def gather_first(self, a):
        if not self.square:
            return (lax.all_gather(a, "cp", axis=0, tiled=True),)
        cut = -(-a.shape[0] // 32) * 16
        top, low = a[:cut], a[cut:]
        return top, low, self.over_x(top), self.over_y(low)

    def gather_second(self, parts):
        if not self.square:
            return parts
        top, low, from_x, from_y = parts
        over_y = self.over_y(jnp.concatenate([top, from_x], axis=0))
        over_x = self.over_x(jnp.concatenate([low, from_y], axis=0))
        return parts + (over_y, over_x)

    def gather_whole(self, parts):
        if not self.square:
            return parts[0]
        cut, rest = parts[0].shape[0], parts[1].shape[0]
        rows = cut + rest

        def move(i, first, count, block, offset):
            return i, first, count, lambda spot: (spot[0] ^ block) * rows + offset

        moves = [
            move(0, 0, cut, 0, 0),
            move(1, 0, rest, 0, cut),
            move(2, 0, cut, 1, 0),
            move(3, 0, rest, 2, cut),
            move(4, 0, cut, 2, 0),
            move(4, cut, cut, 3, 0),
            move(5, 0, rest, 1, cut),
            move(5, rest, rest, 3, cut),
        ]
        return settle_call(self.spot, parts, moves, 4 * rows)

    def interleave(self, mine, theirs, width):
        half = mine.shape[0] // self.cp

        def move(i, block):
            return i, block * half, half, lambda spot: (2 * block + (spot[1] if i == 0 else 1 - spot[1])) * half

        moves = [move(i, block) for block in range(self.cp) for i in range(2)]
        return settle_call(self.spot, (mine, theirs), moves, 2 * mine.shape[0], width)


    def halves(self, fill, lefts, rights, stride, each, n, step, extra=()):
        if self.square:
            return weight_grad(self.spot, fill, lefts, rights, stride, each, n, step, extra)
        products = []

        def product(left, right):
            a, b = (jnp.concatenate(group, axis=0) for group in (lefts[left], rights[right]))
            b = jnp.pad(b, ((0, 0), (0, max(n - b.shape[1], 0)))) if fill is not fill_groups else b
            return dotf(a, b, TN).astype(BF16)

        if fill is fill_rows:
            both = product(0, 0).reshape(self.cp, 2, each, n)
            products = at(both, self.core, 1), at(both, 1 - self.core, 1)
        elif fill is fill_roles:
            products = product(0, 0), product(0, 1)
        elif fill is fill_choice:
            first, second = product(0, 0), product(1, 1)
            products = self.pick(first, second), self.pick(second, first)
        else:
            kv, part = product(0, 0), n - LANES
            low, high = kv[:, :part], kv[:, kv.shape[1] - part :]
            vectors = jnp.pad(extra[0].T, ((0, 0), (0, LANES - extra[0].shape[0]))).astype(BF16)
            products = [jnp.concatenate([self.pick(*pair), vectors], axis=1) for pair in ((low, high), (high, low))]
        return [a.reshape(self.cp, each, n) for a in products]

    def scatter_ready(self, pieces, got, apart=False):
        if not self.square:
            return (add(pieces[0], got),)
        top, top_out, low, low_out = pieces[:4]
        got = got.reshape((2, 2) + got.shape[1:])
        cut = top.shape[1]
        if apart:
            over_x = [add(top_out[i], got[i, 1, :cut]) for i in range(2)]
            over_y = [add(low_out[i], got[1, i, cut:]) for i in range(2)]
            return top, low, got, over_x, over_y
        return top, low, got, add(top_out, got[:, 1, :cut]), add(low_out, got[1, :, cut:])

    def scatter_first(self, parts):
        if not self.square:
            return (lax.psum_scatter(parts[0], "cp", scatter_dimension=0, tiled=False),)
        return parts[:3] + (self.over_x(parts[3]), self.over_y(parts[4]))

    def scatter_open(self, parts):
        if not self.square:
            return self.scatter_first(parts)
        return parts + ([self.over_x(parts[3][1])], [self.over_y(parts[4][1])])

    def scatter_more(self, parts):
        if not self.square:
            return parts
        over_x, over_y, from_x, from_y = parts[3:]
        return parts[:3] + ([self.over_x(over_x[0])] + from_x, [self.over_y(over_y[0])] + from_y)

    def scatter_second(self, parts):
        if not self.square:
            return parts
        top, low, got, from_x, from_y = parts
        cut = top.shape[1]
        top_out = add(top[1], got[1, 0, :cut], from_x[1])
        low_out = add(low[1], got[0, 1, cut:], from_y[1])
        return parts + (self.over_y(top_out), self.over_x(low_out))

    def scatter_rows(self, parts):
        if not self.square:
            half = parts[0].shape[0] // 2
            return parts[0][:half], parts[0][half:]
        top, low, got, from_x, from_y, last_y, last_x = parts
        cut = top.shape[1]
        return add(top[0], got[0, 0, :cut], from_x[0], last_y), add(low[0], got[0, 0, cut:], from_y[0], last_x)

    def scatter_whole(self, parts):
        return jnp.concatenate(self.scatter_rows(parts), axis=0)


    def hop(self, a, moves):
        return lax.ppermute(a, "dp", [(2 * s + c, 2 * t + c) for s, t in moves for c in range(2)])

    def z_first(self, a):
        n, got = self.dp // 2, jnp.zeros_like(a)
        for t in range(n // 2 - 1):
            if t:
                a = add(a, got)
            got = self.hop(a, [(t, t + 1), (n - 1 - t, n - 2 - t)])
        return a, got

    def z_second(self, pair):
        n, a = self.dp // 2, add(*pair)
        return a, self.hop(a, [(n // 2 - 1, n // 2), (n // 2, n // 2 - 1)])

    def z_third(self, pair):
        n, a = self.dp // 2, add(*pair)
        back = a
        for t in reversed(range(n // 2 - 1)):
            if t < n // 2 - 2:
                a = jnp.where((self.z == t + 1) | (self.z == n - 2 - t), back, a)
            back = self.hop(a, [(t + 1, t), (n - 2 - t, n - 1 - t)])
        return a, back

    def z_whole(self, pair):
        n = self.dp // 2
        if n < 4:
            return pair[0]
        return jnp.where((self.z == 0) | (self.z == n - 1), pair[1], pair[0])

    def pick(self, a, b):
        return jnp.where(self.core == 0, a, b)


def inverse_rms(matrix):
    return lax.rsqrt(jnp.mean(matrix * matrix, axis=-1, keepdims=True) + NORM_EPSILON)


def row_table(documents, places):
    half = HEAD_DIM // 2
    inverse = jnp.power(ROPE_BASE, -2.0 * jnp.arange(half, dtype=F32) / HEAD_DIM)
    angles = places.astype(F32)[:, None] * inverse[None, :]
    cos, sin = jnp.cos(angles), jnp.sin(angles)
    spread = lambda a: jnp.broadcast_to(a.astype(F32)[:, None], (a.shape[0], LANES))
    return jnp.concatenate([cos] * 4 + [-sin, sin] * 2 + [spread(documents), spread(places)], axis=1)


def depth_order(depth):
    steps = jnp.arange(depth.shape[0])
    before = (depth[:, None] > depth[None, :]) | ((depth[:, None] == depth[None, :]) & (steps[:, None] < steps[None, :]))
    return jnp.sum(before, axis=0)[None, :] == steps[:, None]


def reorder(order, rows):
    return dotf(order.astype(BF16), rows).astype(BF16)


def all_keys(every, rows, core):
    blocks = every.shape[1] // rows
    spots = jnp.stack([rows * jnp.arange(blocks), jnp.full((blocks,), rows)], axis=1).reshape(-1)
    return jnp.concatenate([jnp.stack([0, core]), spots]).astype(jnp.int32), every


def active_keys(every, rows, core, square):
    keys = every.shape[1]
    blocks, steps = keys // rows, jnp.arange(rows)
    levels = jnp.arange(1, RECUR)[:, None]
    counts = jnp.sum((every[2][None] > levels).reshape(RECUR - 1, blocks, rows), axis=2)
    taken = (counts + 15) // 16 * 16
    ahead = jnp.arange(blocks)[:, None] < jnp.arange(blocks)[None, :]
    starts = jnp.sum(jnp.where(ahead[None], taken[:, :, None], 0), axis=1)
    target = jnp.where(steps < taken[:, :, None], starts[:, :, None] + steps, -1).reshape(RECUR - 1, 1, keys, 1)
    hit = target == jnp.arange(keys)
    cols = jnp.sum(jnp.where(hit, every[None, :, :, None] + 1, 0), axis=2) - 1
    total = jnp.sum(taken, axis=1)
    own = counts[:, 0] if square else jnp.max(counts, axis=1)
    (m, n), (wide_m, wide_n), _ = variants_of(rows, keys)
    body = jnp.where((own <= m) & (total <= n), 0, jnp.where((own <= wide_m) & (total <= wide_n), 1, 2))
    spots = jnp.stack([starts, counts], axis=2).reshape(RECUR - 1, -1)
    metas = jnp.concatenate([body[:, None], jnp.full_like(body, core)[:, None], spots], axis=1).astype(jnp.int32)
    return [(metas[i], cols[i].astype(jnp.int32)) for i in range(RECUR - 1)]


class Level:
    def __init__(self, recursion, place, context, meta, col_info):
        self.recursion, self.place, self.meta, self.col_info = recursion, place, meta, col_info
        self.table, depth = context
        rows, keys = self.table.shape[0], self.col_info.shape[1]
        self.variants = variants_of(rows, keys) if recursion else ((rows, keys),)
        self.active = (depth[:, None] > recursion).astype(F32)

    def project(self, state, w):
        self.state = state
        self.q, self.kv, self.normed = qkv_call(
            self.variants, self.meta, state, w["gain_a"], w["q"], w["kv"], self.table
        )

    def attend(self, kvs):
        self.att, self.lse, self.keys = attend_call(
            self.recursion, self.variants, self.meta, self.q, kvs, self.table, self.col_info
        )

    def post(self, w):
        self.router_row = w["router"][self.recursion][None, :]
        state, self.after, self.normed2, self.branch, self.router, self.gate, self.up, self.inner = post_call(
            self.variants, self.meta, self.att, self.state, w, self.router_row, self.active
        )
        return state

    def widen(self, w):
        self.attn = dotf(self.att, w["o"])
        self.after = self.state + self.attn
        self.normed2 = (self.after * inverse_rms(self.after) * w["gain_f"]).astype(BF16)

    def expand(self, w):
        mine, theirs = dotf(self.normed2, w["mine"]), dotf(self.normed2, w["theirs"])
        gate, up = self.place.pick(mine, theirs), self.place.pick(theirs, mine)
        self.inner = (jax.nn.silu(gate) * up).astype(BF16)
        self.gate, self.up = gate.astype(BF16), up.astype(BF16)

    def close(self, w):
        self.branch = self.attn + dotf(self.inner, w["down"])
        self.router_row = w["router"][self.recursion][None, :]
        self.router = jax.nn.sigmoid(jnp.sum(self.state * self.router_row, axis=-1, keepdims=True))
        return self.state + self.active * self.router * self.branch

    def back_open(self, grad):
        self.g_branch = grad * (self.active * self.router)
        g_logit = jnp.sum(grad * self.branch, axis=-1, keepdims=True)
        g_logit = g_logit * self.active * self.router * (1.0 - self.router)
        self.g_router = jnp.sum(g_logit * self.state, axis=0, keepdims=True)
        self.g_state = grad + g_logit * self.router_row
        self.g_ffn = self.g_branch.astype(BF16)

    def back_expand(self, w):
        self.g_mine, self.g_theirs = expand_back_call(self.meta, self.g_ffn, self.gate, self.up, w)

    def back_norm(self, w):
        self.g_state, self.g_attn, self.g_att, self.g_gain_f = norm_back_call(
            self.meta, self.g_mine, self.g_theirs, self.after, self.g_branch, self.g_state, w
        )

    def post_back(self, grad, w):
        out = post_back_call(
            self.variants, self.meta, grad, self.branch, self.state, self.after, self.router, self.active, self.router_row,
            self.gate, self.up, w,
        )
        self.g_ffn, self.g_state, self.g_attn, self.g_att, self.g_router, self.g_gain_f, self.g_mine, self.g_theirs = out

    def back_attend(self):
        self.dq, dkv = attend_back_call(
            self.recursion, self.variants, self.meta, self.q, self.g_att, self.att, self.keys, self.lse, self.table,
            self.col_info,
        )
        return dkv

    def back_project(self, mine, got, w):
        self.dkv, grad, self.g_gain_a = qkv_back_call(
            self.variants, self.meta, self.dq, mine, got, w["q"], w["kv"], self.state, w["gain_a"], self.g_state, self.table
        )
        return grad


def local(tokens, recur_depth, document_ids, cotangent, *shards, dp, cp):
    place = Place(dp, cp)
    wq, wk, wv, wo, gate, up, down, router, gain_a, gain_f = shards
    rows, each = tokens.shape[1], wq.shape[0]
    width, kv_heads = each * cp, wk.shape[1] // HEAD_DIM

    wkv = jnp.stack([wk.reshape(each, kv_heads, HEAD_DIM), wv.reshape(each, kv_heads, HEAD_DIM)], axis=2)
    wkv = wkv.reshape(each, -1)
    small = jnp.concatenate([gain_a[:, None], gain_f[:, None], router.T], axis=1)
    both = wkv.shape[1]
    part = -(-both // (2 * LANES)) * LANES
    spare = -(part + width + small.shape[1]) % LANES
    blend = [place.pick(wkv[:, :part], wkv[:, both - part :]), place.pick(wq, wo), small, jnp.zeros((each, spare), BF16)]
    blend = place.gather_first(jnp.concatenate(blend, axis=1))
    ids = place.move_tokens(jnp.stack([document_ids[0], recur_depth[0]]))
    state = place.move_tokens(tokens[0])
    gates = place.pick(gate, up)
    downs = place.pick(down[: down.shape[0] // 2], down[down.shape[0] // 2 :])
    padded = -(-width // LANES) * LANES
    downs = jnp.pad(downs, ((0, 0), (0, padded - width)))
    blend, ids, state, gates, downs = tie(blend, ids, state, gates, downs)

    blend = place.gather_second(blend)
    steps = jnp.arange(rows, dtype=jnp.int32)
    order = depth_order(ids[1])
    ids = jnp.stack([ids[0], place.key_block() * rows + steps, ids[1]])
    ids = jnp.sum(jnp.where(order[None], ids[:, None, :], 0), axis=2)
    every = jnp.concatenate(place.gather_keys(ids, 1), axis=1)
    table = row_table(ids[0], ids[1])
    state = reorder(order, state)
    context = (table, ids[2])
    blend, context, order, state, gates, every = tie(blend, context, order, state.astype(F32), gates, every)

    g_part = place.gather_first(gates)
    mine = place.gather_whole(blend)
    theirs = place.over_core(mine)
    w = dict(zip(("q", "o", "kv", "tail"), unpack_call(place.spot, mine, theirs, part, both)))
    edge = width % LANES
    small = w["tail"][:, edge : edge + small.shape[1]].T.astype(F32)
    w["wide_o"], w["o"] = w["o"], w["o"][:, :width]
    w["gain_a"], w["gain_f"], w["router"] = small[:1], small[1:2], small[2:]
    first = Level(0, place, context, *all_keys(every, rows, place.core))
    first.project(state, w)
    first.kv, g_part, downs = tie(first.kv, g_part, downs)

    kvs = place.gather_keys(first.kv)
    kvs, g_part, downs, every = tie(kvs, g_part, downs, every)

    g_part = place.gather_second(g_part)
    d_part = place.gather_first(downs)
    first.attend(kvs)
    first.widen(w)
    later = active_keys(every, rows, place.core, place.square)
    first.normed2, g_part, d_part, later = tie(first.normed2, g_part, d_part, later)
    levels = [first] + [Level(r + 1, place, context, *found) for r, found in enumerate(later)]

    d_part = place.gather_second(d_part)
    w["mine"] = place.gather_whole(g_part)
    w["theirs"] = place.over_core(w["mine"])
    first.expand(w)
    first.inner, d_part = tie(first.inner, d_part)

    mine = place.gather_whole(d_part)
    w["down"] = place.interleave(mine, place.over_core(mine), width)
    state = first.close(w)

    for level in levels[1:]:
        level.project(state, w)
        level.attend(place.gather_keys(level.kv))
        state = level.post(w)
    activations = place.move_tokens(reorder(order.T, state.astype(BF16)))[None]
    grad = reorder(order, place.move_tokens(cotangent[0])).astype(F32)

    for level in levels[:0:-1]:
        level.post_back(grad, w)
        pair = place.scatter_keys_second(place.scatter_keys_first(level.back_attend()))
        grad = level.back_project(*pair, w)

    every = lambda name: [getattr(level, name) for level in levels]
    ff = gate.shape[1]

    grad, activations = tie(grad, activations)
    first.back_open(grad)
    d = place.halves(fill_rows, [every("inner")], [every("g_ffn")], ff // cp, ff // cp // 2, padded, 512)
    d_got = place.over_core(d[-1])
    first.back_expand(w)
    d = place.scatter_ready(d, d_got)
    d, first.g_mine, first.g_theirs = tie(d, first.g_mine, first.g_theirs)

    d = place.scatter_first(d)
    u = place.halves(fill_roles, [every("normed2")], [every("g_mine"), every("g_theirs")], each, each, ff, 512)
    d, u = tie(d, u)

    u_got = place.over_core(u[-1])
    d = place.scatter_second(d)
    first.back_norm(w)
    u = place.scatter_ready(u, u_got, True)
    d, u, first.g_att = tie(d, u, first.g_att)

    u = place.scatter_open(u)
    d = place.z_first(place.scatter_whole(d))
    dkv = first.back_attend()
    u, d, dkv = tie(u, d, dkv)

    u = place.scatter_more(u)
    pair = place.scatter_keys_first(dkv)
    (pair,) = tie(pair)
    pair = place.scatter_keys_second(pair)
    lefts, rights = [every("att"), every("normed")], [every("g_attn"), every("dq")]
    p = place.halves(fill_choice, lefts, rights, each, each, padded, 512)
    u, pair, p = tie(u, pair, p)

    u = place.scatter_second(u)
    p_got = place.over_core(p[-1])
    d = place.z_second(d)
    grad = first.back_project(*pair, w)
    vectors = every("g_router") + [sum(every("g_gain_a")), sum(every("g_gain_f"))]
    vectors = jnp.concatenate(vectors + [jnp.zeros((8 - len(vectors), width), F32)], axis=0)
    k = place.halves(fill_groups, [every("normed")], [every("dkv")], each, each, part + LANES, part + LANES, (vectors,))
    p = place.scatter_ready(p, p_got)
    u, d, p, k, grad = tie(u, d, p, k, grad)

    p = place.scatter_first(p)
    k_got = place.over_core(k[-1])
    u, v = place.scatter_rows(u)
    u = place.z_first(u)
    k = place.scatter_ready(k, k_got)
    u, v, p, k = tie(u, v, p, k)

    p, k = place.scatter_second(p), place.scatter_first(k)
    u, v = place.z_second(u), place.z_first(v)
    u, v, p, k = tie(u, v, p, k)

    k = place.scatter_second(k)
    u, v = place.z_third(u), place.z_second(v)
    a = place.z_first(jnp.concatenate([place.scatter_whole(k), place.scatter_whole(p)], axis=1))
    u, v, a = tie(u, v, a)

    a, v = place.z_second(a), place.z_third(v)
    d = place.z_third(d)
    input_grad = place.move_tokens(reorder(order.T, grad.astype(BF16)))[None]
    a, v, d, input_grad = tie(a, v, d, input_grad)

    a = place.z_third(a)
    d_own = place.z_whole(d)
    d_other = place.over_core(d_own)
    u_own = jnp.concatenate([place.z_whole(u), place.z_whole(v)], axis=0)
    u_other = place.over_core(u_own)
    grad_gate, grad_up = place.pick(u_own, u_other).astype(F32), place.pick(u_other, u_own).astype(F32)
    d_own, d_other = d_own[:, :width], d_other[:, :width]
    grad_down = jnp.concatenate([place.pick(d_own, d_other), place.pick(d_other, d_own)], axis=0).astype(F32)
    a, grad_gate, grad_up, grad_down = tie(a, grad_gate, grad_up, grad_down)

    own = place.z_whole(a)
    other = place.over_core(own)
    low, high = place.pick(own, other).astype(F32), place.pick(other, own).astype(F32)
    grad_kv = jnp.concatenate([low[:, :part], high[:, 2 * part - both : part]], axis=1)
    grad_kv = grad_kv.reshape(each, -1, 2, HEAD_DIM)
    vectors = low[:, part : part + RECUR + 2].T
    return (
        activations,
        input_grad,
        high[:, part + LANES : part + LANES + width],
        grad_kv[:, :, 0].reshape(each, -1),
        grad_kv[:, :, 1].reshape(each, -1),
        low[:, part + LANES : part + LANES + width],
        grad_gate,
        grad_up,
        grad_down,
        vectors[:RECUR],
        vectors[RECUR],
        vectors[RECUR + 1],
    )


def solution(mesh):
    by_token = P("dp", "cp", None)
    by_row = P("cp", None)
    in_specs = (by_token, P("dp", "cp"), P("dp", "cp"), by_token) + (by_row,) * 7 + (P(None, "cp"), P("cp"), P("cp"))
    out_specs = (by_token, by_token) + (by_row,) * 7 + (P(None, "cp"), P("cp"), P("cp"))
    step = functools.partial(local, dp=mesh.shape["dp"], cp=mesh.shape["cp"])
    return jax.shard_map(step, mesh=mesh, in_specs=in_specs, out_specs=out_specs, check_vma=False)
```

```python
import functools

import jax
import jax.numpy as jnp
from jax import lax
from jax.experimental import pallas as pl
from jax.experimental.pallas import tpu as pltpu
from jax.sharding import PartitionSpec as P

HEAD_DIM = 64
LANES = 128
GROUP = 3
RECUR = 3
NORM_EPSILON = 1e-05
MASKED_SCORE = -1e30
ROPE_BASE = 10000.0
SCALE = HEAD_DIM ** (-0.5)
MIB = 2**20
F32, BF16 = jnp.float32, jnp.bfloat16
NN = (((1,), (0,)), ((), ()))
NT = (((1,), (1,)), ((), ()))
TN = (((0,), (0,)), ((), ()))


def dotf(a, b, dims=NN):
    return lax.dot_general(a, b, dims, preferred_element_type=F32)


def turn(u):
    lane = lax.broadcasted_iota(jnp.int32, u.shape, 1) % HEAD_DIM
    return jnp.where(lane < HEAD_DIM // 2, pltpu.roll(u, LANES - 32, 1), pltpu.roll(u, 32, 1))


def variants_of(rows, keys):
    pick = lambda count, third, unit: (count * third // 3 // unit + 1) * unit
    return tuple((pick(rows, k, 32), pick(keys, k, LANES)) for k in (1, 2)) + ((rows, keys),)


def choose(meta_ref, variants, body):
    if len(variants) == 1:
        body(*variants[0])
    else:
        for i, variant in enumerate(variants):
            pl.when(meta_ref[0] == i)(functools.partial(body, *variant))


def clear(m, *refs):
    for ref in refs:
        if m < ref.shape[0]:
            ref[m:, :] = jnp.zeros((ref.shape[0] - m, ref.shape[1]), ref.dtype)


def call(kernel, name, meta, grid, inputs, in_specs, out_specs, out_shape, scratch, vmem, flops, traffic):
    return pl.pallas_call(
        kernel,
        grid_spec=pltpu.PrefetchScalarGridSpec(
            num_scalar_prefetch=1, grid=grid, in_specs=in_specs, out_specs=out_specs, scratch_shapes=scratch
        ),
        out_shape=out_shape,
        compiler_params=pltpu.CompilerParams(vmem_limit_bytes=vmem * MIB),
        cost_estimate=pl.CostEstimate(flops=flops, bytes_accessed=traffic, transcendentals=0),
        name=name,
    )(meta, *inputs)


def whole(*shape):
    return pl.BlockSpec(shape, lambda g, s: (0,) * len(shape))


IN_VMEM = pl.BlockSpec(memory_space=pltpu.VMEM)


def turns(table, keys):
    cos, sin = table[:, :LANES], table[:, LANES : 2 * LANES]
    if not keys:
        return cos, sin
    lane = lax.broadcasted_iota(jnp.int32, cos.shape, 1)
    return jnp.where(lane < HEAD_DIM, cos, 1.0), jnp.where(lane < HEAD_DIM, sin, 0.0)


def qkv_kernel(
    variants, meta_ref, x_ref, gain_ref, wq_ref, wkv_ref, table_ref, q_ref, kv_ref, normed_ref
):
    width = q_ref.shape[1]

    def body(m, _):
        x = x_ref[:m]
        factor = lax.rsqrt(jnp.mean(x * x, axis=-1, keepdims=True) + NORM_EPSILON)
        normed = (x * factor * gain_ref[...]).astype(BF16)
        normed_ref[:m, :] = normed
        kv = dotf(normed, wkv_ref[...])
        cos, sin = turns(table_ref[:m], True)
        for at in range(0, kv_ref.shape[1], LANES):
            u = kv[:, at : at + LANES]
            kv_ref[:m, at : at + LANES] = (u * cos + turn(u) * sin).astype(BF16)
        q = dotf(normed, wq_ref[:, :width])
        cos, sin = turns(table_ref[:m], False)
        for at in range(0, width, LANES):
            if at + LANES <= width:
                u = q[:, at : at + LANES]
            else:
                u = jnp.concatenate([q[:, at:], jnp.zeros((m, at + LANES - width), F32)], axis=1)
            r = (u * cos + turn(u) * sin).astype(BF16)
            q_ref[:m, at : min(at + LANES, width)] = r[:, : min(LANES, width - at)]
        clear(m, q_ref, kv_ref, normed_ref)

    choose(meta_ref, variants, body)


def qkv_call(variants, meta, x, gain, wq, wkv, table):
    rows, width = x.shape
    both = wkv.shape[1]
    return call(
        functools.partial(qkv_kernel, variants),
        "norm_qkv_rope",
        meta,
        (1,),
        (x, gain, wq, wkv, table),
        [IN_VMEM] * 5,
        [IN_VMEM] * 3,
        [jax.ShapeDtypeStruct((rows, k), BF16) for k in (width, both, width)],
        [],
        16,
        2 * rows * width * (width + both),
        2 * width * (width + both) + 8 * rows * width,
    )


def make_bias(row_table, col_info, recursion):
    doc_r, pos_r = (row_table[:, k : k + 1].astype(jnp.int32) for k in (2 * LANES + HEAD_DIM, 3 * LANES + HEAD_DIM))
    doc_c, pos_c, depth_c = col_info[0:1, :], col_info[1:2, :], col_info[2:3, :]
    live = (depth_c > recursion) | (pos_c == pos_r)
    allowed = (pos_c <= pos_r) & (doc_c == doc_r) & live
    return jnp.where(allowed, 0.0, MASKED_SCORE).astype(F32)


def split_pairs(packed, out, to_left):
    m, width = packed.shape
    lane = lax.broadcasted_iota(jnp.int32, (m, LANES), 1)
    for at in range(0, width, LANES):
        h = at // HEAD_DIM
        if at + LANES <= width:
            u = packed[:, at : at + LANES].astype(F32)
        else:
            u = jnp.concatenate([packed[:, at:].astype(F32), jnp.zeros((m, at + LANES - width), F32)], axis=1)
        v = pltpu.roll(u, HEAD_DIM, 1)
        first, second = (u, v) if to_left else (v, u)
        keep = (lane < HEAD_DIM) if to_left else (lane >= HEAD_DIM)
        out[h, :m] = jnp.where(keep, first, 0.0).astype(out.dtype)
        if at + LANES <= width:
            out[h + 1, :m] = jnp.where(keep, second, 0.0).astype(out.dtype)


def join_pairs(scr, out_ref, from_left, m):
    heads = scr.shape[0]
    lane = lax.broadcasted_iota(jnp.int32, (m, LANES), 1)
    for h in range(0, heads, 2):
        at = h * HEAD_DIM
        a = scr[h, :m] if from_left else pltpu.roll(scr[h, :m], HEAD_DIM, 1)
        if h + 1 < heads:
            b = pltpu.roll(scr[h + 1, :m], HEAD_DIM, 1) if from_left else scr[h + 1, :m]
            out_ref[:m, at : at + LANES] = jnp.where(lane < HEAD_DIM, a, b).astype(out_ref.dtype)
        else:
            out_ref[:m, at : at + HEAD_DIM] = a[:, :HEAD_DIM].astype(out_ref.dtype)


def compact_keys(meta_ref, key_refs, rows, keys):
    keys[...] = jnp.zeros_like(keys)
    block = 0
    for ref in key_refs:
        for first in range(0, ref.shape[0], rows):
            keys[pl.ds(pl.multiple_of(meta_ref[2 + 2 * block], 16), rows), :] = ref[first : first + rows, :]
            block += 1


def by_group(count, do):
    def one(g, _):
        do(g, pl.ds(pl.multiple_of(g * LANES, LANES), LANES))
        return 0

    lax.fori_loop(0, count, one, 0)


def stacked(m):
    return GROUP if GROUP * m <= 400 else 1


def attend_kernel(recursion, variants, count, meta_ref, q_ref, *refs):
    key_refs, (row_ref, col_ref, att_ref, lse_ref, keys, bias, q_all, o_all) = refs[:count], refs[count:]
    rows, groups = q_ref.shape[0], keys.shape[1] // LANES
    compact_keys(meta_ref, key_refs, rows, keys)
    lse_ref[...] = jnp.zeros_like(lse_ref)

    def body(m, n):
        bias[:m, :n] = make_bias(row_ref[:m], col_ref[:, :n], recursion)
        split_pairs(q_ref[:m] * jnp.bfloat16(SCALE), q_all, True)
        at_once = stacked(m)

        def group(g, cols):
            kv = keys[:n, cols]
            lane = lax.broadcasted_iota(jnp.int32, (m, LANES), 1)
            for first in range(0, GROUP, at_once):
                heads = [g * GROUP + first + j for j in range(at_once)]
                queries = jnp.concatenate([q_all[h, :m] for h in heads], axis=0)
                s = dotf(queries, kv, NT) + jnp.concatenate([bias[:m, :n]] * at_once, axis=0)
                peak = jnp.max(s, axis=1, keepdims=True)
                e = jnp.exp(s - peak)
                total = jnp.sum(e, axis=1, keepdims=True)
                o = dotf(e.astype(BF16), kv) / total
                log = peak + jnp.log(total)
                for j, h in enumerate(heads):
                    here = slice(j * m, (j + 1) * m)
                    o_all[h, :m] = o[here]
                    lse_ref[:m, :] = jnp.where(lane == h, log[here], lse_ref[:m, :])

        by_group(groups, group)
        join_pairs(o_all, att_ref, False, m)
        clear(m, att_ref)

    choose(meta_ref, variants, body)


def attend_call(recursion, variants, meta, q, kvs, row_info, col_info):
    rows, width = q.shape
    keys, both = sum(k.shape[0] for k in kvs), kvs[0].shape[1]
    heads = both // LANES * GROUP
    shape = jax.ShapeDtypeStruct
    inputs = (q, *kvs, row_info, col_info)
    return call(
        functools.partial(attend_kernel, recursion, variants, len(kvs)),
        "attend",
        meta,
        (1,),
        inputs,
        [IN_VMEM] * len(inputs),
        [IN_VMEM] * 3,
        [shape((rows, width), BF16), shape((rows, LANES), F32), shape((keys, both), BF16)],
        [
            pltpu.VMEM((rows, keys), F32),
            pltpu.VMEM((heads, rows, LANES), BF16),
            pltpu.VMEM((heads, rows, LANES), F32),
        ],
        16,
        4 * rows * keys * LANES * heads,
        4 * q.size + 2 * keys * both,
    )


def attend_back_kernel(
    recursion, variants, meta_ref, q_ref, do_ref, att_ref, keys, lse_ref, row_ref, col_ref, dq_ref, dkv_ref,
    bias, back, q_all, do_all, p3, ds3, dq_all,
):
    rows, groups = q_ref.shape[0], keys.shape[1] // LANES

    def body(m, n):
        bias[:m, :n] = make_bias(row_ref[:m], col_ref[:, :n], recursion)
        split_pairs(q_ref[:m] * jnp.bfloat16(SCALE), q_all, True)
        split_pairs(do_ref[:m], do_all, False)
        split_pairs(do_ref[:m].astype(F32) * att_ref[:m].astype(F32), dq_all, True)
        at_once = stacked(m)

        def group(g, cols):
            kv = keys[:n, cols]
            cos, sin = turns(row_ref[:m], False)
            lane = lax.broadcasted_iota(jnp.int32, (m, LANES), 1)
            for first in range(0, GROUP, at_once):
                heads = [g * GROUP + first + j for j in range(at_once)]
                here = slice(first * m, (first + at_once) * m)
                stack = lambda parts: jnp.concatenate(parts, axis=0)
                logs = stack([jnp.sum(jnp.where(lane == h, lse_ref[:m], 0.0), axis=1, keepdims=True) for h in heads])
                dots = stack([jnp.sum(dq_all[h, :m], axis=1, keepdims=True) for h in heads])
                s = dotf(stack([q_all[h, :m] for h in heads]), kv, NT) + stack([bias[:m, :n]] * at_once)
                p = jnp.exp(s - logs)
                dp = dotf(stack([do_all[h, :m] for h in heads]), kv, NT)
                ds = (p * (dp - dots)).astype(BF16)
                p3[here, :n] = p.astype(BF16)
                ds3[here, :n] = ds
                dq = dotf(ds, kv) * SCALE
                for j, h in enumerate(heads):
                    one = dq[j * m : (j + 1) * m]
                    dq_all[h, :m] = one * cos - turn(one) * sin
            q3 = jnp.concatenate([q_all[g * GROUP + j, :m] for j in range(GROUP)], axis=0)
            do3 = jnp.concatenate([do_all[g * GROUP + j, :m] for j in range(GROUP)], axis=0)
            dkv = dotf(q3, ds3[: GROUP * m, :n], TN) + dotf(do3, p3[: GROUP * m, :n], TN)
            back[:n, cols] = dkv.T

        by_group(groups, group)
        join_pairs(dq_all, dq_ref, True, m)
        clear(m, dq_ref)

    choose(meta_ref, variants, body)
    spot = lax.broadcasted_iota(jnp.int32, (rows, back.shape[1]), 0)
    for block in range(dkv_ref.shape[0] // rows):
        part = back[pl.ds(pl.multiple_of(meta_ref[2 + 2 * block], 16), rows), :]
        part = jnp.where(spot < meta_ref[3 + 2 * block], part, 0.0)
        dkv_ref[block * rows : (block + 1) * rows, :] = part.astype(BF16)


def attend_back_call(recursion, variants, meta, q, do, att, kv, lse, row_info, col_info):
    rows, width = q.shape
    keys, both = kv.shape
    heads = both // LANES * GROUP
    inputs = (q, do, att, kv, lse, row_info, col_info)
    return call(
        functools.partial(attend_back_kernel, recursion, variants),
        "attend_back",
        meta,
        (1,),
        inputs,
        [IN_VMEM] * len(inputs),
        [IN_VMEM] * 2,
        [jax.ShapeDtypeStruct((rows, width), BF16), jax.ShapeDtypeStruct((keys, both), BF16)],
        [
            pltpu.VMEM((rows, keys), F32),
            pltpu.VMEM((keys, both), F32),
            pltpu.VMEM((heads, rows, LANES), BF16),
            pltpu.VMEM((heads, rows, LANES), BF16),
            pltpu.VMEM((GROUP * rows, keys), BF16),
            pltpu.VMEM((GROUP * rows, keys), BF16),
            pltpu.VMEM((heads, rows, LANES), F32),
        ],
        24,
        10 * rows * keys * LANES * heads,
        8 * q.size + 4 * keys * both,
    )


def inverse(x):
    return lax.rsqrt(jnp.mean(x * x, axis=-1, keepdims=True) + NORM_EPSILON)


def sigmoid(x):
    return 1.0 / (1.0 + jnp.exp(-x))


def roles(core, a, b):
    return jnp.where(core == 0, a, b), jnp.where(core == 0, b, a)


def by_steps(width, step, do):
    def one(c, _):
        do(pl.ds(pl.multiple_of(c * step, step), step))
        return 0

    lax.fori_loop(0, width // step, one, 0)


def post_kernel(variants, step, meta_ref, att, state, wo, gain, router_row, active, mine, theirs, down, *refs):
    following, after, normed2, branch, router, gate_ref, up_ref, inner_ref = refs
    core, width = meta_ref[1], state.shape[1]

    def body(m, _):
        attn = dotf(att[:m], wo[:, :width])
        x = state[:m] + attn
        after[:m, :] = x
        normed2[:m, :] = (x * inverse(x) * gain[...]).astype(BF16)
        branch[:m, :] = attn

        def part(cols):
            n2 = normed2[:m, :]
            gate, up = roles(core, dotf(n2, mine[:, cols]), dotf(n2, theirs[:, cols]))
            inner = (gate * sigmoid(gate) * up).astype(BF16)
            inner_ref[:m, cols] = inner
            gate_ref[:m, cols] = gate.astype(BF16)
            up_ref[:m, cols] = up.astype(BF16)
            branch[:m, :] += dotf(inner, down[cols, :])

        by_steps(inner_ref.shape[1], step, part)
        clear(m, after, normed2, branch, inner_ref, gate_ref, up_ref)

    choose(meta_ref, variants, body)
    x = state[...]
    router[...] = sigmoid(jnp.sum(x * router_row[...], axis=-1, keepdims=True))
    following[...] = x + active[...] * router[...] * branch[...]


def post_call(variants, meta, att, state, w, router_row, active, step=512):
    rows, width = state.shape
    ff = w["mine"].shape[1]
    shape = jax.ShapeDtypeStruct
    inputs = (att, state, w["wide_o"], w["gain_f"], router_row, active, w["mine"], w["theirs"], w["down"])
    outputs = [shape((rows, width), F32), shape((rows, width), F32), shape((rows, width), BF16), shape((rows, width), F32)]
    outputs += [shape((rows, 1), F32)] + [shape((rows, ff), BF16)] * 3
    return call(
        functools.partial(post_kernel, variants, step),
        "post",
        meta,
        (1,),
        inputs,
        [IN_VMEM] * len(inputs),
        [IN_VMEM] * len(outputs),
        outputs,
        [],
        16,
        2 * rows * width * (width + 3 * ff),
        2 * width * (width + 3 * ff),
    )


def post_back_kernel(
    variants, step, meta_ref, grad, branch, state, after, router, active, router_row, gain, wo, gate_ref, up_ref, mine, theirs,
    down, g_ffn, g_state, g_attn, g_att, g_router, g_gain, g_mine_ref, g_theirs_ref, g_branch, g_normed2,
):
    core, width = meta_ref[1], state.shape[1]

    def body(m, _):
        g = grad[:m]
        weight = active[:m] * router[:m]
        logit = jnp.sum(g * branch[:m], axis=-1, keepdims=True) * weight * (1.0 - router[:m])
        g_router[...] = jnp.sum(logit * state[:m], axis=0, keepdims=True)
        g_state[:m, :] = g + logit * router_row[...]
        if m < grad.shape[0]:
            g_state[m:, :] = grad[m:]
        low = g * weight
        g_branch[:m, :] = low
        g_ffn[:m, :] = low.astype(BF16)
        g_normed2[:m, :] = jnp.zeros((m, width), F32)

        def part(cols):
            g_inner = dotf(g_ffn[:m, :], down[cols, :], NT)
            gate, up = gate_ref[:m, cols].astype(F32), up_ref[:m, cols].astype(F32)
            sig = sigmoid(gate)
            g_gate = (g_inner * up * sig * (1.0 + gate * (1.0 - sig))).astype(BF16)
            g_up = (g_inner * gate * sig).astype(BF16)
            g_mine, g_theirs = roles(core, g_gate, g_up)
            g_mine_ref[:m, cols] = g_mine
            g_theirs_ref[:m, cols] = g_theirs
            g_normed2[:m, :] += dotf(g_mine, mine[:, cols], NT) + dotf(g_theirs, theirs[:, cols], NT)

        by_steps(gate_ref.shape[1], step, part)
        x, g = after[:m], g_normed2[:m, :]
        factor = inverse(x)
        unit = x * factor
        g_gain[...] = jnp.sum(g * unit, axis=0, keepdims=True)
        scaled = g * gain[...]
        g_after = factor * (scaled - unit * jnp.mean(scaled * unit, axis=-1, keepdims=True))
        g_state[:m, :] += g_after
        low = (g_after + g_branch[:m, :]).astype(BF16)
        g_attn[:m, :] = low
        g_att[:m, :] = dotf(low, wo[:, :width], NT).astype(BF16)
        clear(m, g_ffn, g_attn, g_att, g_mine_ref, g_theirs_ref)

    choose(meta_ref, variants, body)


def expand_back_kernel(step, meta_ref, g_ffn, gate_ref, up_ref, down, g_mine_ref, g_theirs_ref):
    core = meta_ref[1]

    def part(cols):
        g_inner = dotf(g_ffn[...], down[cols, :], NT)
        gate, up = gate_ref[:, cols].astype(F32), up_ref[:, cols].astype(F32)
        sig = sigmoid(gate)
        g_gate = (g_inner * up * sig * (1.0 + gate * (1.0 - sig))).astype(BF16)
        g_up = (g_inner * gate * sig).astype(BF16)
        g_mine_ref[:, cols], g_theirs_ref[:, cols] = roles(core, g_gate, g_up)

    by_steps(gate_ref.shape[1], step, part)


def expand_back_call(meta, g_ffn, gate, up, w, step=512):
    inputs = (g_ffn, gate, up, w["down"])
    return call(
        functools.partial(expand_back_kernel, step),
        "expand_back",
        meta,
        (1,),
        inputs,
        [IN_VMEM] * len(inputs),
        [IN_VMEM] * 2,
        [jax.ShapeDtypeStruct(gate.shape, BF16)] * 2,
        [],
        16,
        2 * gate.size * g_ffn.shape[1],
        2 * w["down"].size,
    )


def norm_back_kernel(step, meta_ref, g_mine, g_theirs, mine, theirs, after, gain, g_branch, grad, wo, g_state, g_attn, g_att, g_gain):
    width = after.shape[1]
    g = dotf(g_mine[...], mine[...], NT) + dotf(g_theirs[...], theirs[...], NT)
    x = after[...]
    factor = inverse(x)
    unit = x * factor
    g_gain[...] = jnp.sum(g * unit, axis=0, keepdims=True)
    scaled = g * gain[...]
    g_after = factor * (scaled - unit * jnp.mean(scaled * unit, axis=-1, keepdims=True))
    g_state[...] = grad[...] + g_after
    low = (g_after + g_branch[...]).astype(BF16)
    g_attn[...] = low
    g_att[...] = dotf(low, wo[:, :width], NT).astype(BF16)


def norm_back_call(meta, g_mine, g_theirs, after, g_branch, grad, w, step=512):
    rows, width = after.shape
    inputs = (g_mine, g_theirs, w["mine"], w["theirs"], after, w["gain_f"], g_branch, grad, w["wide_o"])
    shape = jax.ShapeDtypeStruct
    outputs = [shape((rows, width), k) for k in (F32, BF16, BF16)] + [shape((1, width), F32)]
    return call(
        functools.partial(norm_back_kernel, step),
        "norm_back",
        meta,
        (1,),
        inputs,
        [IN_VMEM] * len(inputs),
        [IN_VMEM] * len(outputs),
        outputs,
        [],
        16,
        2 * rows * width * (width + 2 * g_mine.shape[1]),
        2 * width * (width + 2 * g_mine.shape[1]),
    )


def post_back_call(variants, meta, grad, branch, state, after, router, active, router_row, gate, up, w, step=512):
    rows, width = state.shape
    ff = w["mine"].shape[1]
    shape = jax.ShapeDtypeStruct
    inputs = (grad, branch, state, after, router, active, router_row, w["gain_f"], w["wide_o"], gate, up)
    inputs += (w["mine"], w["theirs"], w["down"])
    outputs = [shape((rows, width), k) for k in (BF16, F32, BF16, BF16)]
    outputs += [shape((1, width), F32)] * 2 + [shape((rows, ff), BF16)] * 2
    return call(
        functools.partial(post_back_kernel, variants, step),
        "post_back",
        meta,
        (1,),
        inputs,
        [IN_VMEM] * len(inputs),
        [IN_VMEM] * len(outputs),
        outputs,
        [pltpu.VMEM((rows, width), F32)] * 2,
        16,
        2 * rows * width * (width + 3 * ff),
        2 * width * (width + 3 * ff),
    )


def qkv_back_kernel(
    variants, meta_ref, dq_ref, mine_ref, got_ref, wq_ref, wkv_ref, x_ref, gain_ref, up_ref, table_ref,
    dkv_ref, out_ref, gain_grad_ref,
):
    def body(m, _):
        cos, sin = turns(table_ref[:m], True)
        for at in range(0, dkv_ref.shape[1], LANES):
            cols = slice(at, at + LANES)
            u = mine_ref[:m, cols].astype(F32) + got_ref[:m, cols].astype(F32)
            dkv_ref[:m, cols] = (u * cos - turn(u) * sin).astype(BF16)
        clear(m, dkv_ref)
        g = dotf(dq_ref[:m], wq_ref[:, : dq_ref.shape[1]], NT) + dotf(dkv_ref[:m, :], wkv_ref[...], NT)
        x = x_ref[:m]
        factor = inverse(x)
        unit = x * factor
        gain_grad_ref[...] = jnp.sum(g * unit, axis=0, keepdims=True)
        scaled = g * gain_ref[...]
        out_ref[:m, :] = up_ref[:m] + factor * (scaled - unit * jnp.mean(scaled * unit, axis=-1, keepdims=True))
        if m < up_ref.shape[0]:
            out_ref[m:, :] = up_ref[m:]

    choose(meta_ref, variants, body)


def qkv_back_call(variants, meta, dq, mine, got, wq, wkv, x, gain, upstream, table):
    rows, width = x.shape
    both = wkv.shape[1]
    return call(
        functools.partial(qkv_back_kernel, variants),
        "qkv_back",
        meta,
        (1,),
        (dq, mine, got, wq, wkv, x, gain, upstream, table),
        [IN_VMEM] * 9,
        [IN_VMEM] * 3,
        [
            jax.ShapeDtypeStruct((rows, both), BF16),
            jax.ShapeDtypeStruct((rows, width), F32),
            jax.ShapeDtypeStruct((1, width), F32),
        ],
        [],
        16,
        2 * rows * width * (width + both),
        2 * width * (width + both) + 16 * rows * width,
    )


def weight_grad_kernel(fill, counts, hand, choices, stride, spot_ref, *refs):
    c = pl.program_id(0)
    n_left, n_right, n_extra, n_ready, levels = counts
    sources, refs = refs[: n_left * levels], refs[n_left * levels :]
    rights, refs = refs[: n_right * levels], refs[n_right * levels :]
    extra, ready, refs = refs[:n_extra], refs[n_extra : n_extra + n_ready], refs[n_extra + n_ready :]
    outs, handed = refs[:5], refs[5 : 5 + (hand is not None)]
    scratch = refs[5 + len(handed) :]
    staged, turned, values, sem = scratch[:n_left], list(scratch[n_left : 2 * n_left]), scratch[-3:-1], scratch[-1]
    if handed:
        turned[hand] = handed[0]
    turned += ready

    def run(sizes):
        starts = [sum(sizes[:i]) for i in range(levels)]
        depth = sum(sizes)

        @pl.when(c == 0)
        def _():
            copies = []
            for i, source in enumerate(sources):
                size = sizes[i % levels]
                target = staged[i // levels].at[pl.ds(starts[i % levels], size), :]
                copies.append(pltpu.make_async_copy(source.at[pl.ds(0, size), :], target, sem.at[i]))
                copies[-1].start()
            for i, copy in enumerate(copies):
                copy.wait()
                if i % levels == levels - 1:
                    turned[i // levels][:, :depth] = staged[i // levels][:depth, :].T

        def product(left, right):
            group = rights[right * levels : (right + 1) * levels]
            stacked = jnp.concatenate([a[:size, :] for a, size in zip(group, sizes)], axis=0)
            return dotf(turned[left][:, :depth], stacked)

        fill(spot_ref[1], c, product, values, extra)

    core = spot_ref[1]
    for i, sizes in enumerate(choices):
        pl.when(spot_ref[2] == i)(functools.partial(run, sizes))
    each, cut = outs[4].shape[1], outs[0].shape[1]
    kept, away = values
    for r in range(4):
        mine = other = pl.multiple_of((spot_ref[0] ^ r) * stride, 16)
        source = away
        if stride != each:
            other = pl.multiple_of(mine + (1 - core) * each, 16)
            mine = pl.multiple_of(mine + core * each, 16)
            source = kept
        outs[r % 2][r // 2] = kept[pl.ds(mine, cut), :]
        outs[2 + r // 2][r % 2] = kept[pl.ds(pl.multiple_of(mine + cut, 16), each - cut), :]
        outs[4][r] = source[pl.ds(other, each), :]


def fill_rows(core, c, product, values, extra):
    values[0][...] = product(0, 0).astype(BF16)


def fill_roles(core, c, product, values, extra):
    for i, value in enumerate(values):
        value[...] = product(0, i).astype(BF16)


def fill_choice(core, c, product, values, extra):
    kept, away = values
    first, second = product(0, 0).astype(BF16), product(1, 1).astype(BF16)
    kept[...] = jnp.where(core == 0, first, second)
    away[...] = jnp.where(core == 0, second, first)


def fill_groups(core, c, product, values, extra):
    kept, away = values
    v = product(0, 0)
    part = kept.shape[1] - LANES
    low, high = v[:, :part].astype(BF16), v[:, v.shape[1] - part :].astype(BF16)
    kept[:, :part] = jnp.where(core == 0, low, high)
    away[:, :part] = jnp.where(core == 0, high, low)
    vectors = extra[0][...].T
    rest = jnp.zeros((vectors.shape[0], LANES - vectors.shape[1]), F32)
    vectors = jnp.concatenate([vectors, rest], axis=1).astype(BF16)
    kept[:, part:] = vectors
    away[:, part:] = vectors


def weight_grad(spot, fill, lefts, rights, stride, each, n, step, choices, extra=(), ready=(), hand=None):
    levels, rows = len(rights[0]), rights[0][0].shape[0]
    depth = levels * rows
    cut = -(-each // 32) * 16
    shapes = [(2, cut, n), (2, cut, n), (2, each - cut, n), (2, each - cut, n), (4, each, n)]
    flops = 2 * depth * 4 * stride * sum(right[0].shape[1] for right in rights)
    sources, moving = [a for group in lefts for a in group], [a for group in rights for a in group]
    by_step = pl.BlockSpec((rows, step), lambda c, s: (0, c))
    given = [] if hand is None else [(lefts[hand][0].shape[1], depth)]
    at_once = lambda a: pl.BlockSpec(a.shape, lambda c, s: (0, 0))
    return pl.pallas_call(
        functools.partial(weight_grad_kernel, fill, (len(lefts), len(rights), len(extra), len(ready), levels), hand, choices, stride),
        grid_spec=pltpu.PrefetchScalarGridSpec(
            num_scalar_prefetch=1,
            grid=(-(-n // step),),
            in_specs=[pl.BlockSpec(memory_space=pl.ANY)] * len(sources)
            + [by_step if n > step else at_once(a) for a in moving]
            + [at_once(a) for a in extra]
            + [IN_VMEM] * len(ready),
            out_specs=[pl.BlockSpec(s[:2] + (step,), lambda c, s: (0, 0, c)) for s in shapes] + [IN_VMEM] * len(given),
            scratch_shapes=[pltpu.VMEM((depth, group[0].shape[1]), BF16) for group in lefts]
            + [pltpu.VMEM((group[0].shape[1], depth), BF16) for group in lefts]
            + [pltpu.VMEM((4 * stride, step), BF16)] * 2
            + [pltpu.SemaphoreType.DMA((max(len(sources), 1),))],
        ),
        out_shape=[jax.ShapeDtypeStruct(s, BF16) for s in shapes + given],
        compiler_params=pltpu.CompilerParams(vmem_limit_bytes=24 * MIB),
        cost_estimate=pl.CostEstimate(
            flops=flops, bytes_accessed=2 * sum(a.size for a in sources + moving) + 16 * each * n, transcendentals=0
        ),
        name="weight_grad",
    )(spot, *sources, *moving, *extra, *ready)


def settle_kernel(moves, spot_ref, *refs):
    out = refs[-1]
    for i, first, rows, place in moves:
        out[pl.ds(pl.multiple_of(place(spot_ref), 16), rows), :] = refs[i][first : first + rows, : out.shape[1]]


def copy_call(kernel, name, spot, arrays, shapes):
    return pl.pallas_call(
        kernel,
        grid_spec=pltpu.PrefetchScalarGridSpec(
            num_scalar_prefetch=1,
            grid=(1,),
            in_specs=[IN_VMEM] * len(arrays),
            out_specs=[IN_VMEM] * len(shapes),
        ),
        out_shape=[jax.ShapeDtypeStruct(shape, arrays[0].dtype) for shape in shapes],
        compiler_params=pltpu.CompilerParams(vmem_limit_bytes=16 * MIB),
        cost_estimate=pl.CostEstimate(flops=0, bytes_accessed=4 * sum(a.size for a in arrays), transcendentals=0),
        name=name,
    )(spot, *arrays)


def settle_call(spot, arrays, moves, rows, width=None):
    shape = (rows, width or arrays[0].shape[1])
    (out,) = copy_call(functools.partial(settle_kernel, moves), "settle", spot, arrays, [shape])
    return out


def unpack_kernel(part, spot_ref, mine, theirs, q_out, o_out, kv_out, tail_out):
    both = kv_out.shape[1]
    tail_out[...] = mine[:, mine.shape[1] - LANES :]

    def go(first, second):
        q_out[...] = first[:, part:]
        o_out[...] = second[:, part:]
        kv_out[:, :part] = first[:, :part]
        kv_out[:, part:] = second[:, 2 * part - both : part]

    pl.when(spot_ref[1] == 0)(lambda: go(mine, theirs))
    pl.when(spot_ref[1] == 1)(lambda: go(theirs, mine))


def unpack_call(spot, mine, theirs, part, both):
    rows, width = mine.shape
    shapes = [(rows, width - part), (rows, width - part), (rows, both), (rows, LANES)]
    return copy_call(functools.partial(unpack_kernel, part), "unpack", spot, (mine, theirs), shapes)


def finish_kernel(part, both, spot_ref, own, other, query, key, value, out, vectors):
    width = query.shape[1]

    def go(low, high):
        out[...] = low[:, part + LANES : part + LANES + width].astype(F32)
        query[...] = high[:, part + LANES : part + LANES + width].astype(F32)
        vectors[...] = low[:, part : part + LANES].astype(F32).T[: vectors.shape[0], :]
        groups = [low[:, at : at + LANES] for at in range(0, part, LANES)]
        groups += [high[:, at : at + LANES] for at in range(2 * part - both, part, LANES)]
        groups = [group.astype(F32) for group in groups]
        lane = lax.broadcasted_iota(jnp.int32, groups[0].shape, 1)
        for i in range(0, len(groups), 2):
            at = i * HEAD_DIM
            a, turned = groups[i], pltpu.roll(groups[i], HEAD_DIM, 1)
            if i + 1 < len(groups):
                b = groups[i + 1]
                key[at : at + LANES, :] = jnp.where(lane < HEAD_DIM, a, pltpu.roll(b, HEAD_DIM, 1)).T
                value[at : at + LANES, :] = jnp.where(lane < HEAD_DIM, turned, b).T
            else:
                key[at : at + HEAD_DIM, :] = a.T[:HEAD_DIM, :]
                value[at : at + HEAD_DIM, :] = turned.T[:HEAD_DIM, :]

    pl.when(spot_ref[1] == 0)(lambda: go(own, other))
    pl.when(spot_ref[1] == 1)(lambda: go(other, own))


def finish_rows_kernel(spot_ref, own, other, out):
    half, width = own.shape[0], out.shape[0]

    def go(low, high):
        out[:, :half] = low[:, :width].astype(F32).T
        out[:, half:] = high[:, :width].astype(F32).T

    pl.when(spot_ref[1] == 0)(lambda: go(own, other))
    pl.when(spot_ref[1] == 1)(lambda: go(other, own))


def finish_rows_call(spot, own, other, width):
    shape = jax.ShapeDtypeStruct((width, 2 * own.shape[0]), F32)
    return call(
        finish_rows_kernel, "finish_rows", spot, (1,), (own, other), [IN_VMEM] * 2, IN_VMEM, shape, [], 16, 0, 8 * own.size
    )


def finish_call(spot, own, other, part, both, width):
    rows = own.shape[0]
    shapes = [(rows, width), (both // 2, rows), (both // 2, rows), (rows, width), (8, rows)]
    return call(
        functools.partial(finish_kernel, part, both),
        "finish",
        spot,
        (1,),
        (own, other),
        [IN_VMEM] * 2,
        [IN_VMEM] * len(shapes),
        [jax.ShapeDtypeStruct(shape, F32) for shape in shapes],
        [],
        16,
        0,
        8 * own.size,
    )


def tie(*trees):
    return lax.optimization_barrier(trees)


def add(*terms):
    return sum(a.astype(F32) for a in terms).astype(BF16)


def at(a, index, axis):
    return lax.dynamic_index_in_dim(a, index, axis, keepdims=False)


class Place:
    def __init__(self, dp, cp):
        self.dp, self.cp, self.square = dp, cp, cp == 4
        dp_at, cp_at = lax.axis_index("dp"), lax.axis_index("cp")
        self.core, self.z = dp_at % 2, dp_at // 2
        self.y, self.x = cp_at // 2, cp_at % 2
        self.spot = jnp.stack([cp_at, self.core]).astype(jnp.int32)

    def over_x(self, a):
        return lax.ppermute(a, "cp", [(i, i ^ 1) for i in range(self.cp)])

    def over_y(self, a):
        return lax.ppermute(a, "cp", [(i, i ^ 2) for i in range(self.cp)])

    def over_core(self, a):
        return lax.ppermute(a, "dp", [(i, i ^ 1) for i in range(self.dp)])

    def move_tokens(self, a):
        if not self.square:
            return a
        pairs = []
        for d in range(self.dp):
            for c in range(self.cp):
                z, core, y, x = d // 2, d % 2, c // 2, c % 2
                pairs.append((d * self.cp + c, (2 * z + y) * self.cp + 2 * core + x))
        return lax.ppermute(a, ("dp", "cp"), pairs)

    def move_wide(self, a):
        return self.move_tokens(jnp.pad(a, ((0, 0), (0, -a.shape[1] % LANES))))

    def fit(self, rows, later):
        sizes = [m for m, _ in variants_of(rows, later[0][1].shape[1])]
        self.choices = (tuple(reversed(sizes)), (rows,) * RECUR)
        fits = jnp.bool_(True)
        for r, (meta, _) in enumerate(later):
            fits = fits & (meta[0] <= RECUR - 2 - r)
        self.grad_spot = jnp.concatenate([self.spot, jnp.where(fits, 0, 1)[None].astype(jnp.int32)])

    def key_block(self):
        return 2 * self.core + self.x if self.square else lax.axis_index("cp")

    def gather_keys(self, a, axis=0):
        if not self.square:
            return (lax.all_gather(a, "cp", axis=axis, tiled=True),)
        from_x, from_core = self.over_x(a), self.over_core(a)
        return a, from_x, from_core, self.over_core(from_x)

    def scatter_keys_first(self, a):
        if not self.square:
            own = lax.psum_scatter(a, "cp", scatter_dimension=0, tiled=True)
            return own, jnp.zeros_like(own)
        rows = a.shape[0] // 4
        return a[: 2 * rows], self.over_core(a[2 * rows :])

    def scatter_keys_second(self, pair):
        if not self.square:
            return pair
        rows = pair[0].shape[0] // 2
        pair = add(*pair)
        return pair[:rows], self.over_x(pair[rows:])


    def gather_first(self, a):
        if not self.square:
            return (lax.all_gather(a, "cp", axis=0, tiled=True),)
        return a, self.over_x(a), self.over_y(a)

    def gather_second(self, parts):
        if not self.square:
            return parts
        own, from_x, from_y = parts
        cut = -(-own.shape[0] // 32) * 16
        return parts + (self.over_y(from_x[:cut]), self.over_x(from_y[cut:]))

    def gather_whole(self, parts):
        if not self.square:
            return parts[0]
        rows, cut = parts[0].shape[0], parts[3].shape[0]

        def move(i, count, block, offset):
            return i, 0, count, lambda spot: (spot[0] ^ block) * rows + offset

        moves = [move(0, rows, 0, 0), move(1, rows, 1, 0), move(2, rows, 2, 0)]
        moves += [move(3, cut, 3, 0), move(4, rows - cut, 3, cut)]
        return settle_call(self.spot, parts, moves, 4 * rows)

    def interleave(self, mine, theirs, width):
        half = mine.shape[0] // self.cp

        def move(i, block):
            return i, block * half, half, lambda spot: (2 * block + (spot[1] if i == 0 else 1 - spot[1])) * half

        moves = [move(i, block) for block in range(self.cp) for i in range(2)]
        return settle_call(self.spot, (mine, theirs), moves, 2 * mine.shape[0], width)


    def halves(self, fill, lefts, rights, stride, each, n, step, extra=(), ready=(), hand=None):
        if self.square:
            return weight_grad(
                self.grad_spot, fill, [] if ready else lefts, rights, stride, each, n, step, self.choices, extra, ready, hand
            )
        products = []

        def product(left, right):
            a, b = (jnp.concatenate(group, axis=0) for group in (lefts[left], rights[right]))
            b = jnp.pad(b, ((0, 0), (0, max(n - b.shape[1], 0)))) if fill is not fill_groups else b
            return dotf(a, b, TN).astype(BF16)

        if fill is fill_rows:
            both = product(0, 0).reshape(self.cp, 2, each, n)
            products = at(both, self.core, 1), at(both, 1 - self.core, 1)
        elif fill is fill_roles:
            products = product(0, 0), product(0, 1)
        elif fill is fill_choice:
            first, second = product(0, 0), product(1, 1)
            products = self.pick(first, second), self.pick(second, first)
        else:
            kv, part = product(0, 0), n - LANES
            low, high = kv[:, :part], kv[:, kv.shape[1] - part :]
            vectors = jnp.pad(extra[0].T, ((0, 0), (0, LANES - extra[0].shape[0]))).astype(BF16)
            products = [jnp.concatenate([self.pick(*pair), vectors], axis=1) for pair in ((low, high), (high, low))]
        return [a.reshape(self.cp, each, n) for a in products]

    def scatter_ready(self, pieces, got, apart=False):
        if not self.square:
            return (add(pieces[0], got),)
        top, top_out, low, low_out = pieces[:4]
        got = got.reshape((2, 2) + got.shape[1:])
        cut = top.shape[1]
        if apart:
            over_x = [add(top_out[i], got[i, 1, :cut]) for i in range(2)]
            over_y = [add(low_out[i], got[1, i, cut:]) for i in range(2)]
            return top, low, got, over_x, over_y
        return top, low, got, add(top_out, got[:, 1, :cut]), add(low_out, got[1, :, cut:])

    def scatter_first(self, parts):
        if not self.square:
            return (lax.psum_scatter(parts[0], "cp", scatter_dimension=0, tiled=False),)
        return parts[:3] + (self.over_x(parts[3]), self.over_y(parts[4]))

    def scatter_open(self, parts):
        if not self.square:
            return self.scatter_first(parts)
        return parts + ([self.over_x(parts[3][1])], [self.over_y(parts[4][1])])

    def scatter_more(self, parts):
        if not self.square:
            return parts
        over_x, over_y, from_x, from_y = parts[3:]
        return parts[:3] + ([self.over_x(over_x[0])] + from_x, [self.over_y(over_y[0])] + from_y)

    def scatter_second(self, parts):
        if not self.square:
            return parts
        top, low, got, from_x, from_y = parts
        cut = top.shape[1]
        top_out = add(top[1], got[1, 0, :cut], from_x[1])
        low_out = add(low[1], got[0, 1, cut:], from_y[1])
        return parts + (self.over_y(top_out), self.over_x(low_out))

    def scatter_rows(self, parts):
        if not self.square:
            half = parts[0].shape[0] // 2
            return parts[0][:half], parts[0][half:]
        top, low, got, from_x, from_y, last_y, last_x = parts
        cut = top.shape[1]
        return add(top[0], got[0, 0, :cut], from_x[0], last_y), add(low[0], got[0, 0, cut:], from_y[0], last_x)

    def scatter_whole(self, parts):
        return jnp.concatenate(self.scatter_rows(parts), axis=0)


    def hop(self, a, moves):
        return lax.ppermute(a, "dp", [(2 * s + c, 2 * t + c) for s, t in moves for c in range(2)])

    def z_first(self, a):
        n, got = self.dp // 2, jnp.zeros_like(a)
        for t in range(n // 2 - 1):
            if t:
                a = add(a, got)
            got = self.hop(a, [(t, t + 1), (n - 1 - t, n - 2 - t)])
        return a, got

    def z_second(self, pair):
        n, a = self.dp // 2, add(*pair)
        return a, self.hop(a, [(n // 2 - 1, n // 2), (n // 2, n // 2 - 1)])

    def z_third(self, pair):
        n, a = self.dp // 2, add(*pair)
        back = a
        for t in reversed(range(n // 2 - 1)):
            if t < n // 2 - 2:
                a = jnp.where((self.z == t + 1) | (self.z == n - 2 - t), back, a)
            back = self.hop(a, [(t + 1, t), (n - 2 - t, n - 1 - t)])
        return a, back

    def z_whole(self, pair):
        n = self.dp // 2
        if n < 4:
            return pair[0]
        return jnp.where((self.z == 0) | (self.z == n - 1), pair[1], pair[0])

    def pick(self, a, b):
        return jnp.where(self.core == 0, a, b)


def inverse_rms(matrix):
    return lax.rsqrt(jnp.mean(matrix * matrix, axis=-1, keepdims=True) + NORM_EPSILON)


def row_table(documents, places):
    half = HEAD_DIM // 2
    inverse = jnp.power(ROPE_BASE, -2.0 * jnp.arange(half, dtype=F32) / HEAD_DIM)
    angles = places.astype(F32)[:, None] * inverse[None, :]
    cos, sin = jnp.cos(angles), jnp.sin(angles)
    spread = lambda a: jnp.broadcast_to(a.astype(F32)[:, None], (a.shape[0], LANES))
    return jnp.concatenate([cos] * 4 + [-sin, sin] * 2 + [spread(documents), spread(places)], axis=1)


def depth_order(depth):
    steps = jnp.arange(depth.shape[0])
    before = (depth[:, None] > depth[None, :]) | ((depth[:, None] == depth[None, :]) & (steps[:, None] < steps[None, :]))
    return jnp.sum(before, axis=0)[None, :] == steps[:, None]


def reorder(order, rows):
    return dotf(order.astype(BF16), rows).astype(BF16)


def all_keys(every, rows, core):
    blocks = every.shape[1] // rows
    spots = jnp.stack([rows * jnp.arange(blocks), jnp.full((blocks,), rows)], axis=1).reshape(-1)
    return jnp.concatenate([jnp.stack([0, core]), spots]).astype(jnp.int32), every


def active_keys(every, rows, core, square):
    keys = every.shape[1]
    blocks, steps = keys // rows, jnp.arange(rows)
    levels = jnp.arange(1, RECUR)[:, None]
    counts = jnp.sum((every[2][None] > levels).reshape(RECUR - 1, blocks, rows), axis=2)
    taken = (counts + 15) // 16 * 16
    ahead = jnp.arange(blocks)[:, None] < jnp.arange(blocks)[None, :]
    starts = jnp.sum(jnp.where(ahead[None], taken[:, :, None], 0), axis=1)
    target = jnp.where(steps < taken[:, :, None], starts[:, :, None] + steps, -1).reshape(RECUR - 1, 1, keys, 1)
    hit = target == jnp.arange(keys)
    cols = jnp.sum(jnp.where(hit, every[None, :, :, None] + 1, 0), axis=2) - 1
    total = jnp.sum(taken, axis=1)
    own = counts[:, 0] if square else jnp.max(counts, axis=1)
    (m, n), (wide_m, wide_n), _ = variants_of(rows, keys)
    body = jnp.where((own <= m) & (total <= n), 0, jnp.where((own <= wide_m) & (total <= wide_n), 1, 2))
    spots = jnp.stack([starts, counts], axis=2).reshape(RECUR - 1, -1)
    metas = jnp.concatenate([body[:, None], jnp.full_like(body, core)[:, None], spots], axis=1).astype(jnp.int32)
    return [(metas[i], cols[i].astype(jnp.int32)) for i in range(RECUR - 1)]


class Level:
    def __init__(self, recursion, place, context, meta, col_info):
        self.recursion, self.place, self.meta, self.col_info = recursion, place, meta, col_info
        self.table, depth = context
        rows, keys = self.table.shape[0], self.col_info.shape[1]
        self.variants = variants_of(rows, keys) if recursion else ((rows, keys),)
        self.active = (depth[:, None] > recursion).astype(F32)

    def project(self, state, w):
        self.state = state
        self.q, self.kv, self.normed = qkv_call(
            self.variants, self.meta, state, w["gain_a"], w["q"], w["kv"], self.table
        )

    def attend(self, kvs):
        self.att, self.lse, self.keys = attend_call(
            self.recursion, self.variants, self.meta, self.q, kvs, self.table, self.col_info
        )

    def post(self, w):
        self.router_row = w["router"][self.recursion][None, :]
        state, self.after, self.normed2, self.branch, self.router, self.gate, self.up, self.inner = post_call(
            self.variants, self.meta, self.att, self.state, w, self.router_row, self.active
        )
        return state

    def widen(self, w):
        self.attn = dotf(self.att, w["o"])
        self.after = self.state + self.attn
        self.normed2 = (self.after * inverse_rms(self.after) * w["gain_f"]).astype(BF16)

    def expand(self, w):
        mine, theirs = dotf(self.normed2, w["mine"]), dotf(self.normed2, w["theirs"])
        gate, up = self.place.pick(mine, theirs), self.place.pick(theirs, mine)
        self.inner = (jax.nn.silu(gate) * up).astype(BF16)
        self.gate, self.up = gate.astype(BF16), up.astype(BF16)

    def close(self, w):
        self.branch = self.attn + dotf(self.inner, w["down"])
        self.router_row = w["router"][self.recursion][None, :]
        self.router = jax.nn.sigmoid(jnp.sum(self.state * self.router_row, axis=-1, keepdims=True))
        return self.state + self.active * self.router * self.branch

    def back_open(self, grad):
        self.g_branch = grad * (self.active * self.router)
        g_logit = jnp.sum(grad * self.branch, axis=-1, keepdims=True)
        g_logit = g_logit * self.active * self.router * (1.0 - self.router)
        self.g_router = jnp.sum(g_logit * self.state, axis=0, keepdims=True)
        self.g_state = grad + g_logit * self.router_row
        self.g_ffn = self.g_branch.astype(BF16)

    def back_expand(self, w):
        self.g_mine, self.g_theirs = expand_back_call(self.meta, self.g_ffn, self.gate, self.up, w)

    def back_norm(self, w):
        self.g_state, self.g_attn, self.g_att, self.g_gain_f = norm_back_call(
            self.meta, self.g_mine, self.g_theirs, self.after, self.g_branch, self.g_state, w
        )

    def post_back(self, grad, w):
        out = post_back_call(
            self.variants, self.meta, grad, self.branch, self.state, self.after, self.router, self.active, self.router_row,
            self.gate, self.up, w,
        )
        self.g_ffn, self.g_state, self.g_attn, self.g_att, self.g_router, self.g_gain_f, self.g_mine, self.g_theirs = out

    def back_attend(self):
        self.dq, dkv = attend_back_call(
            self.recursion, self.variants, self.meta, self.q, self.g_att, self.att, self.keys, self.lse, self.table,
            self.col_info,
        )
        return dkv

    def back_project(self, mine, got, w):
        self.dkv, grad, self.g_gain_a = qkv_back_call(
            self.variants, self.meta, self.dq, mine, got, w["q"], w["kv"], self.state, w["gain_a"], self.g_state, self.table
        )
        return grad


def local(tokens, recur_depth, document_ids, cotangent, *shards, dp, cp):
    place = Place(dp, cp)
    wq, wk, wv, wo, gate, up, down, router, gain_a, gain_f = shards
    rows, each = tokens.shape[1], wq.shape[0]
    width, kv_heads = each * cp, wk.shape[1] // HEAD_DIM

    wkv = jnp.stack([wk.reshape(each, kv_heads, HEAD_DIM), wv.reshape(each, kv_heads, HEAD_DIM)], axis=2)
    wkv = wkv.reshape(each, -1)
    small = jnp.concatenate([gain_a[:, None], gain_f[:, None], router.T], axis=1)
    both = wkv.shape[1]
    part = -(-both // (2 * LANES)) * LANES
    spare = -(part + width + small.shape[1]) % LANES
    blend = [place.pick(wkv[:, :part], wkv[:, both - part :]), place.pick(wq, wo), small, jnp.zeros((each, spare), BF16)]
    blend = place.gather_first(jnp.concatenate(blend, axis=1))
    ids = place.move_tokens(jnp.stack([document_ids[0], recur_depth[0]]))
    state = place.move_tokens(tokens[0])
    gates = place.pick(gate, up)
    downs = place.pick(down[: down.shape[0] // 2], down[down.shape[0] // 2 :])
    padded = -(-width // LANES) * LANES
    downs = jnp.pad(downs, ((0, 0), (0, padded - width)))
    blend, ids, state, gates, downs = tie(blend, ids, state, gates, downs)

    blend = place.gather_second(blend)
    steps = jnp.arange(rows, dtype=jnp.int32)
    order = depth_order(ids[1])
    ids = jnp.stack([ids[0], place.key_block() * rows + steps, ids[1]])
    ids = jnp.sum(jnp.where(order[None], ids[:, None, :], 0), axis=2)
    every = jnp.concatenate(place.gather_keys(ids, 1), axis=1)
    table = row_table(ids[0], ids[1])
    state = reorder(order, state)
    context = (table, ids[2])
    blend, context, order, state, gates, every = tie(blend, context, order, state.astype(F32), gates, every)

    g_part = place.gather_first(gates)
    mine = place.gather_whole(blend)
    theirs = place.over_core(mine)
    w = dict(zip(("q", "o", "kv", "tail"), unpack_call(place.spot, mine, theirs, part, both)))
    edge = width % LANES
    small = w["tail"][:, edge : edge + small.shape[1]].T.astype(F32)
    w["wide_o"], w["o"] = w["o"], w["o"][:, :width]
    w["gain_a"], w["gain_f"], w["router"] = small[:1], small[1:2], small[2:]
    first = Level(0, place, context, *all_keys(every, rows, place.core))
    first.project(state, w)
    first.kv, downs, every = tie(first.kv, downs, every)

    kvs = place.gather_keys(first.kv)
    later = active_keys(every, rows, place.core, place.square)
    kvs, g_part, downs, later = tie(kvs, g_part, downs, later)

    g_part = place.gather_second(g_part)
    d_part = place.gather_first(downs)
    first.attend(kvs)
    first.widen(w)
    first.normed2, g_part, d_part = tie(first.normed2, g_part, d_part)
    place.fit(rows, later)
    levels = [first] + [Level(r + 1, place, context, *found) for r, found in enumerate(later)]

    d_part = place.gather_second(d_part)
    w["mine"] = place.gather_whole(g_part)
    w["theirs"] = place.over_core(w["mine"])
    first.expand(w)
    first.inner, d_part = tie(first.inner, d_part)

    mine = place.gather_whole(d_part)
    w["down"] = place.interleave(mine, place.over_core(mine), width)
    state = first.close(w)

    for level in levels[1:]:
        level.project(state, w)
        level.attend(place.gather_keys(level.kv))
        state = level.post(w)
    activations = place.move_wide(reorder(order.T, state.astype(BF16)))
    grad = reorder(order, place.move_tokens(cotangent[0])).astype(F32)

    for level in levels[:0:-1]:
        level.post_back(grad, w)
        pair = place.scatter_keys_second(place.scatter_keys_first(level.back_attend()))
        grad = level.back_project(*pair, w)

    every = lambda name: [getattr(level, name) for level in levels]
    ff = gate.shape[1]

    grad, activations = tie(grad, activations)
    first.back_open(grad)
    d = place.halves(fill_rows, [every("inner")], [every("g_ffn")], ff // cp, ff // cp // 2, padded, 512)
    d_got = place.over_core(d[-1])
    first.back_expand(w)
    d = place.scatter_ready(d, d_got)
    d, first.g_mine, first.g_theirs = tie(d, first.g_mine, first.g_theirs)

    d = place.scatter_first(d)
    u = place.halves(fill_roles, [every("normed2")], [every("g_mine"), every("g_theirs")], each, each, ff, 512)
    d, u = tie(d, u)

    u_got = place.over_core(u[-1])
    d = place.scatter_second(d)
    first.back_norm(w)
    u = place.scatter_ready(u, u_got, True)
    d, u, first.g_att = tie(d, u, first.g_att)

    u = place.scatter_open(u)
    d = place.z_first(place.scatter_whole(d))
    dkv = first.back_attend()
    u, d, dkv = tie(u, d, dkv)

    pair = place.scatter_keys_first(dkv)
    (pair,) = tie(pair)
    pair = place.scatter_keys_second(pair)
    u = place.scatter_more(u)
    lefts, rights = [every("att"), every("normed")], [every("g_attn"), every("dq")]
    p = place.halves(fill_choice, lefts, rights, each, each, padded, 512, hand=1)
    u, pair, p = tie(u, pair, p)

    u = place.scatter_second(u)
    p_got = place.over_core(p[4] if place.square else p[1])
    grad = first.back_project(*pair, w)
    vectors = every("g_router") + [sum(every("g_gain_a")), sum(every("g_gain_f"))]
    vectors = jnp.concatenate(vectors + [jnp.zeros((8 - len(vectors), width), F32)], axis=0)
    ready = p[5:] if place.square else ()
    k = place.halves(
        fill_groups, [every("normed")], [every("dkv")], each, each, part + LANES, part + LANES, (vectors,), ready=ready
    )
    p = place.scatter_ready(p, p_got)
    u, p, k, grad = tie(u, p, k, grad)

    k_got = place.over_core(k[-1])
    u, v = place.scatter_rows(u)
    u = place.z_first(u)
    p = place.scatter_first(p)
    k = place.scatter_first(place.scatter_ready(k, k_got))
    d = place.z_second(d)
    u, v, p, k, d = tie(u, v, p, k, d)

    p, k = place.scatter_second(p), place.scatter_second(k)
    u, v = place.z_second(u), place.z_first(v)
    d = place.z_third(d)
    input_grad = place.move_wide(reorder(order.T, grad.astype(BF16)))
    u, v, p, k, d, input_grad, activations = tie(u, v, p, k, d, input_grad, activations)

    u, v = place.z_third(u), place.z_second(v)
    a = place.z_first(jnp.concatenate([place.scatter_whole(k), place.scatter_whole(p)], axis=1))
    u, v, a = tie(u, v, a)

    a, v = place.z_second(a), place.z_third(v)
    d_own = place.z_whole(d)
    grad_down = finish_rows_call(place.spot, d_own, place.over_core(d_own), width).T
    input_grad, activations = (b[None, :, :width] for b in (input_grad, activations))
    a, v, grad_down, input_grad, activations = tie(a, v, grad_down, input_grad, activations)

    a = place.z_third(a)
    u_own = jnp.concatenate([place.z_whole(u), place.z_whole(v)], axis=0)
    u_other = place.over_core(u_own)
    grad_gate, grad_up = place.pick(u_own, u_other).astype(F32), place.pick(u_other, u_own).astype(F32)
    a, grad_gate, grad_up = tie(a, grad_gate, grad_up)

    own = place.z_whole(a)
    other = place.over_core(own)
    grad_query, grad_key, grad_value, grad_out, vectors = finish_call(place.spot, own, other, part, both, width)
    return (
        activations,
        input_grad,
        grad_query,
        grad_key.T,
        grad_value.T,
        grad_out,
        grad_gate,
        grad_up,
        grad_down,
        vectors[:RECUR],
        vectors[RECUR],
        vectors[RECUR + 1],
    )


def solution(mesh):
    by_token = P("dp", "cp", None)
    by_row = P("cp", None)
    in_specs = (by_token, P("dp", "cp"), P("dp", "cp"), by_token) + (by_row,) * 7 + (P(None, "cp"), P("cp"), P("cp"))
    out_specs = (by_token, by_token) + (by_row,) * 7 + (P(None, "cp"), P("cp"), P("cp"))
    step = functools.partial(local, dp=mesh.shape["dp"], cp=mesh.shape["cp"])
    return jax.shard_map(step, mesh=mesh, in_specs=in_specs, out_specs=out_specs, check_vma=False)
```

```python
import functools

import jax
import jax.numpy as jnp
from jax import lax
from jax.experimental import pallas as pl
from jax.experimental.pallas import tpu as pltpu
from jax.sharding import PartitionSpec as P

HEAD_DIM = 64
LANES = 128
GROUP = 3
RECUR = 3
NORM_EPSILON = 1e-05
MASKED_SCORE = -1e30
ROPE_BASE = 10000.0
SCALE = HEAD_DIM ** (-0.5)
MIB = 2**20
F32, BF16 = jnp.float32, jnp.bfloat16
NN = (((1,), (0,)), ((), ()))
NT = (((1,), (1,)), ((), ()))
TN = (((0,), (0,)), ((), ()))


def dotf(a, b, dims=NN):
    return lax.dot_general(a, b, dims, preferred_element_type=F32)


def turn(u):
    lane = lax.broadcasted_iota(jnp.int32, u.shape, 1) % HEAD_DIM
    return jnp.where(lane < HEAD_DIM // 2, pltpu.roll(u, LANES - 32, 1), pltpu.roll(u, 32, 1))


def variants_of(rows, keys):
    pick = lambda count, third, unit: (count * third // 3 // unit + 1) * unit
    return tuple((pick(rows, k, 32), pick(keys, k, LANES)) for k in (1, 2)) + ((rows, keys),)


def choose(meta_ref, variants, body):
    if len(variants) == 1:
        body(*variants[0])
    else:
        for i, variant in enumerate(variants):
            pl.when(meta_ref[0] == i)(functools.partial(body, *variant))


def clear(m, *refs):
    for ref in refs:
        if m < ref.shape[0]:
            ref[m:, :] = jnp.zeros((ref.shape[0] - m, ref.shape[1]), ref.dtype)


def call(kernel, name, meta, grid, inputs, in_specs, out_specs, out_shape, scratch, vmem, flops, traffic):
    return pl.pallas_call(
        kernel,
        grid_spec=pltpu.PrefetchScalarGridSpec(
            num_scalar_prefetch=1, grid=grid, in_specs=in_specs, out_specs=out_specs, scratch_shapes=scratch
        ),
        out_shape=out_shape,
        compiler_params=pltpu.CompilerParams(vmem_limit_bytes=vmem * MIB),
        cost_estimate=pl.CostEstimate(flops=flops, bytes_accessed=traffic, transcendentals=0),
        name=name,
    )(meta, *inputs)


def whole(*shape):
    return pl.BlockSpec(shape, lambda g, s: (0,) * len(shape))


IN_VMEM = pl.BlockSpec(memory_space=pltpu.VMEM)


def turns(table, keys):
    cos, sin = table[:, :LANES], table[:, LANES : 2 * LANES]
    if not keys:
        return cos, sin
    lane = lax.broadcasted_iota(jnp.int32, cos.shape, 1)
    return jnp.where(lane < HEAD_DIM, cos, 1.0), jnp.where(lane < HEAD_DIM, sin, 0.0)


def qkv_kernel(
    variants, meta_ref, x_ref, gain_ref, wq_ref, wkv_ref, table_ref, q_ref, kv_ref, normed_ref
):
    width = q_ref.shape[1]

    def body(m, _):
        x = x_ref[:m]
        factor = lax.rsqrt(jnp.mean(x * x, axis=-1, keepdims=True) + NORM_EPSILON)
        normed = (x * factor * gain_ref[...]).astype(BF16)
        normed_ref[:m, :] = normed
        kv = dotf(normed, wkv_ref[...])
        cos, sin = turns(table_ref[:m], True)
        for at in range(0, kv_ref.shape[1], LANES):
            u = kv[:, at : at + LANES]
            kv_ref[:m, at : at + LANES] = (u * cos + turn(u) * sin).astype(BF16)
        q = dotf(normed, wq_ref[:, :width])
        cos, sin = turns(table_ref[:m], False)
        for at in range(0, width, LANES):
            if at + LANES <= width:
                u = q[:, at : at + LANES]
            else:
                u = jnp.concatenate([q[:, at:], jnp.zeros((m, at + LANES - width), F32)], axis=1)
            r = (u * cos + turn(u) * sin).astype(BF16)
            q_ref[:m, at : min(at + LANES, width)] = r[:, : min(LANES, width - at)]
        clear(m, q_ref, kv_ref, normed_ref)

    choose(meta_ref, variants, body)


def qkv_call(variants, meta, x, gain, wq, wkv, table):
    rows, width = x.shape
    both = wkv.shape[1]
    return call(
        functools.partial(qkv_kernel, variants),
        "norm_qkv_rope",
        meta,
        (1,),
        (x, gain, wq, wkv, table),
        [IN_VMEM] * 5,
        [IN_VMEM] * 3,
        [jax.ShapeDtypeStruct((rows, k), BF16) for k in (width, both, width)],
        [],
        16,
        2 * rows * width * (width + both),
        2 * width * (width + both) + 8 * rows * width,
    )


def make_bias(row_table, col_info, recursion):
    doc_r, pos_r = (row_table[:, k : k + 1].astype(jnp.int32) for k in (2 * LANES + HEAD_DIM, 3 * LANES + HEAD_DIM))
    doc_c, pos_c, depth_c = col_info[0:1, :], col_info[1:2, :], col_info[2:3, :]
    live = (depth_c > recursion) | (pos_c == pos_r)
    allowed = (pos_c <= pos_r) & (doc_c == doc_r) & live
    return jnp.where(allowed, 0.0, MASKED_SCORE).astype(F32)


def split_pairs(packed, out, to_left):
    m, width = packed.shape
    lane = lax.broadcasted_iota(jnp.int32, (m, LANES), 1)
    for at in range(0, width, LANES):
        h = at // HEAD_DIM
        if at + LANES <= width:
            u = packed[:, at : at + LANES].astype(F32)
        else:
            u = jnp.concatenate([packed[:, at:].astype(F32), jnp.zeros((m, at + LANES - width), F32)], axis=1)
        v = pltpu.roll(u, HEAD_DIM, 1)
        first, second = (u, v) if to_left else (v, u)
        keep = (lane < HEAD_DIM) if to_left else (lane >= HEAD_DIM)
        out[h, :m] = jnp.where(keep, first, 0.0).astype(out.dtype)
        if at + LANES <= width:
            out[h + 1, :m] = jnp.where(keep, second, 0.0).astype(out.dtype)


def join_pairs(scr, out_ref, from_left, m):
    heads = scr.shape[0]
    lane = lax.broadcasted_iota(jnp.int32, (m, LANES), 1)
    for h in range(0, heads, 2):
        at = h * HEAD_DIM
        a = scr[h, :m] if from_left else pltpu.roll(scr[h, :m], HEAD_DIM, 1)
        if h + 1 < heads:
            b = pltpu.roll(scr[h + 1, :m], HEAD_DIM, 1) if from_left else scr[h + 1, :m]
            out_ref[:m, at : at + LANES] = jnp.where(lane < HEAD_DIM, a, b).astype(out_ref.dtype)
        else:
            out_ref[:m, at : at + HEAD_DIM] = a[:, :HEAD_DIM].astype(out_ref.dtype)


def compact_keys(meta_ref, key_refs, rows, keys):
    keys[...] = jnp.zeros_like(keys)
    block = 0
    for ref in key_refs:
        for first in range(0, ref.shape[0], rows):
            keys[pl.ds(pl.multiple_of(meta_ref[2 + 2 * block], 16), rows), :] = ref[first : first + rows, :]
            block += 1


def by_group(count, do, unroll=False):
    def one(g, _):
        do(g, pl.ds(pl.multiple_of(g * LANES, LANES), LANES))
        return 0

    lax.fori_loop(0, count, one, 0, unroll=unroll)


def stacked(m):
    return GROUP if GROUP * m <= 400 else 1


def attend_kernel(recursion, variants, count, meta_ref, q_ref, *refs):
    key_refs, (row_ref, col_ref, att_ref, lse_ref, keys, bias, q_all, o_all) = refs[:count], refs[count:]
    rows, groups = q_ref.shape[0], keys.shape[1] // LANES
    compact_keys(meta_ref, key_refs, rows, keys)
    lse_ref[...] = jnp.zeros_like(lse_ref)

    def body(m, n):
        bias[:m, :n] = make_bias(row_ref[:m], col_ref[:, :n], recursion)
        split_pairs(q_ref[:m] * jnp.bfloat16(SCALE), q_all, True)
        at_once = stacked(m)

        def group(g, cols):
            kv = keys[:n, cols]
            lane = lax.broadcasted_iota(jnp.int32, (m, LANES), 1)
            sets = [[g * GROUP + first + j for j in range(at_once)] for first in range(0, GROUP, at_once)]

            def score(heads):
                queries = jnp.concatenate([q_all[h, :m] for h in heads], axis=0)
                return dotf(queries, kv, NT) + jnp.concatenate([bias[:m, :n]] * at_once, axis=0)

            s = score(sets[0])
            for i, heads in enumerate(sets):
                following = score(sets[i + 1]) if i + 1 < len(sets) else None
                peak = jnp.max(s, axis=1, keepdims=True)
                e = jnp.exp(s - peak)
                total = jnp.sum(e, axis=1, keepdims=True)
                o = dotf(e.astype(BF16), kv) / total
                log = peak + jnp.log(total)
                for j, h in enumerate(heads):
                    here = slice(j * m, (j + 1) * m)
                    o_all[h, :m] = o[here]
                    lse_ref[:m, :] = jnp.where(lane == h, log[here], lse_ref[:m, :])
                s = following

        by_group(groups, group, True)
        join_pairs(o_all, att_ref, False, m)
        clear(m, att_ref)

    choose(meta_ref, variants, body)


def attend_call(recursion, variants, meta, q, kvs, row_info, col_info):
    rows, width = q.shape
    keys, both = sum(k.shape[0] for k in kvs), kvs[0].shape[1]
    heads = both // LANES * GROUP
    shape = jax.ShapeDtypeStruct
    inputs = (q, *kvs, row_info, col_info)
    return call(
        functools.partial(attend_kernel, recursion, variants, len(kvs)),
        "attend",
        meta,
        (1,),
        inputs,
        [IN_VMEM] * len(inputs),
        [IN_VMEM] * 3,
        [shape((rows, width), BF16), shape((rows, LANES), F32), shape((keys, both), BF16)],
        [
            pltpu.VMEM((rows, keys), F32),
            pltpu.VMEM((heads, rows, LANES), BF16),
            pltpu.VMEM((heads, rows, LANES), F32),
        ],
        24,
        4 * rows * keys * LANES * heads,
        4 * q.size + 2 * keys * both,
    )


def attend_back_kernel(
    recursion, variants, meta_ref, q_ref, do_ref, att_ref, keys, lse_ref, row_ref, col_ref, dq_ref, dkv_ref,
    bias, back, q_all, do_all, p3, ds3, dq_all,
):
    rows, groups = q_ref.shape[0], keys.shape[1] // LANES

    def body(m, n):
        bias[:m, :n] = make_bias(row_ref[:m], col_ref[:, :n], recursion)
        split_pairs(q_ref[:m] * jnp.bfloat16(SCALE), q_all, True)
        split_pairs(do_ref[:m], do_all, False)
        split_pairs(do_ref[:m].astype(F32) * att_ref[:m].astype(F32), dq_all, True)
        at_once = stacked(m)

        def group(g, cols):
            kv = keys[:n, cols]
            cos, sin = turns(row_ref[:m], False)
            lane = lax.broadcasted_iota(jnp.int32, (m, LANES), 1)
            stack = lambda parts: jnp.concatenate(parts, axis=0)
            sets = [[g * GROUP + first + j for j in range(at_once)] for first in range(0, GROUP, at_once)]

            def score(heads):
                s = dotf(stack([q_all[h, :m] for h in heads]), kv, NT) + stack([bias[:m, :n]] * at_once)
                return s, dotf(stack([do_all[h, :m] for h in heads]), kv, NT)

            s, dp = score(sets[0])
            for i, heads in enumerate(sets):
                following = score(sets[i + 1]) if i + 1 < len(sets) else (None, None)
                here = slice(i * at_once * m, (i + 1) * at_once * m)
                logs = stack([jnp.sum(jnp.where(lane == h, lse_ref[:m], 0.0), axis=1, keepdims=True) for h in heads])
                dots = stack([jnp.sum(dq_all[h, :m], axis=1, keepdims=True) for h in heads])
                p = jnp.exp(s - logs)
                ds = (p * (dp - dots)).astype(BF16)
                p3[here, :n] = p.astype(BF16)
                ds3[here, :n] = ds
                dq = dotf(ds, kv) * SCALE
                for j, h in enumerate(heads):
                    one = dq[j * m : (j + 1) * m]
                    dq_all[h, :m] = one * cos - turn(one) * sin
                s, dp = following
            q3 = jnp.concatenate([q_all[g * GROUP + j, :m] for j in range(GROUP)], axis=0)
            do3 = jnp.concatenate([do_all[g * GROUP + j, :m] for j in range(GROUP)], axis=0)
            dkv = dotf(q3, ds3[: GROUP * m, :n], TN) + dotf(do3, p3[: GROUP * m, :n], TN)
            back[:n, cols] = dkv.T

        by_group(groups, group, False)
        join_pairs(dq_all, dq_ref, True, m)
        clear(m, dq_ref)

    choose(meta_ref, variants, body)
    spot = lax.broadcasted_iota(jnp.int32, (rows, back.shape[1]), 0)
    for block in range(dkv_ref.shape[0] // rows):
        part = back[pl.ds(pl.multiple_of(meta_ref[2 + 2 * block], 16), rows), :]
        part = jnp.where(spot < meta_ref[3 + 2 * block], part, 0.0)
        dkv_ref[block * rows : (block + 1) * rows, :] = part.astype(BF16)


def attend_back_call(recursion, variants, meta, q, do, att, kv, lse, row_info, col_info):
    rows, width = q.shape
    keys, both = kv.shape
    heads = both // LANES * GROUP
    inputs = (q, do, att, kv, lse, row_info, col_info)
    return call(
        functools.partial(attend_back_kernel, recursion, variants),
        "attend_back",
        meta,
        (1,),
        inputs,
        [IN_VMEM] * len(inputs),
        [IN_VMEM] * 2,
        [jax.ShapeDtypeStruct((rows, width), BF16), jax.ShapeDtypeStruct((keys, both), BF16)],
        [
            pltpu.VMEM((rows, keys), F32),
            pltpu.VMEM((keys, both), F32),
            pltpu.VMEM((heads, rows, LANES), BF16),
            pltpu.VMEM((heads, rows, LANES), BF16),
            pltpu.VMEM((GROUP * rows, keys), BF16),
            pltpu.VMEM((GROUP * rows, keys), BF16),
            pltpu.VMEM((heads, rows, LANES), F32),
        ],
        32,
        10 * rows * keys * LANES * heads,
        8 * q.size + 4 * keys * both,
    )


def inverse(x):
    return lax.rsqrt(jnp.mean(x * x, axis=-1, keepdims=True) + NORM_EPSILON)


def sigmoid(x):
    return 1.0 / (1.0 + jnp.exp(-x))


def roles(core, a, b):
    return jnp.where(core == 0, a, b), jnp.where(core == 0, b, a)


def by_steps(width, step, do):
    def one(c, _):
        do(pl.ds(pl.multiple_of(c * step, step), step))
        return 0

    lax.fori_loop(0, width // step, one, 0)


def post_kernel(variants, step, meta_ref, att, state, wo, gain, router_row, active, mine, theirs, down, *refs):
    following, after, normed2, branch, router, gate_ref, up_ref, inner_ref = refs
    core, width = meta_ref[1], state.shape[1]

    def body(m, _):
        attn = dotf(att[:m], wo[:, :width])
        x = state[:m] + attn
        after[:m, :] = x
        normed2[:m, :] = (x * inverse(x) * gain[...]).astype(BF16)
        branch[:m, :] = attn

        def part(cols):
            n2 = normed2[:m, :]
            gate, up = roles(core, dotf(n2, mine[:, cols]), dotf(n2, theirs[:, cols]))
            inner = (gate * sigmoid(gate) * up).astype(BF16)
            inner_ref[:m, cols] = inner
            gate_ref[:m, cols] = gate.astype(BF16)
            up_ref[:m, cols] = up.astype(BF16)
            branch[:m, :] += dotf(inner, down[cols, :])

        by_steps(inner_ref.shape[1], step, part)
        clear(m, after, normed2, branch, inner_ref, gate_ref, up_ref)

    choose(meta_ref, variants, body)
    x = state[...]
    router[...] = sigmoid(jnp.sum(x * router_row[...], axis=-1, keepdims=True))
    following[...] = x + active[...] * router[...] * branch[...]


def post_call(variants, meta, att, state, w, router_row, active, step=512):
    rows, width = state.shape
    ff = w["mine"].shape[1]
    shape = jax.ShapeDtypeStruct
    inputs = (att, state, w["wide_o"], w["gain_f"], router_row, active, w["mine"], w["theirs"], w["down"])
    outputs = [shape((rows, width), F32), shape((rows, width), F32), shape((rows, width), BF16), shape((rows, width), F32)]
    outputs += [shape((rows, 1), F32)] + [shape((rows, ff), BF16)] * 3
    return call(
        functools.partial(post_kernel, variants, step),
        "post",
        meta,
        (1,),
        inputs,
        [IN_VMEM] * len(inputs),
        [IN_VMEM] * len(outputs),
        outputs,
        [],
        16,
        2 * rows * width * (width + 3 * ff),
        2 * width * (width + 3 * ff),
    )


def post_back_kernel(
    variants, step, meta_ref, grad, branch, state, after, router, active, router_row, gain, wo, gate_ref, up_ref, mine, theirs,
    down, g_ffn, g_state, g_attn, g_att, g_router, g_gain, g_mine_ref, g_theirs_ref, g_branch, g_normed2,
):
    core, width = meta_ref[1], state.shape[1]

    def body(m, _):
        g = grad[:m]
        weight = active[:m] * router[:m]
        logit = jnp.sum(g * branch[:m], axis=-1, keepdims=True) * weight * (1.0 - router[:m])
        g_router[...] = jnp.sum(logit * state[:m], axis=0, keepdims=True)
        g_state[:m, :] = g + logit * router_row[...]
        if m < grad.shape[0]:
            g_state[m:, :] = grad[m:]
        low = g * weight
        g_branch[:m, :] = low
        g_ffn[:m, :] = low.astype(BF16)
        g_normed2[:m, :] = jnp.zeros((m, width), F32)

        def part(cols):
            g_inner = dotf(g_ffn[:m, :], down[cols, :], NT)
            gate, up = gate_ref[:m, cols].astype(F32), up_ref[:m, cols].astype(F32)
            sig = sigmoid(gate)
            g_gate = (g_inner * up * sig * (1.0 + gate * (1.0 - sig))).astype(BF16)
            g_up = (g_inner * gate * sig).astype(BF16)
            g_mine, g_theirs = roles(core, g_gate, g_up)
            g_mine_ref[:m, cols] = g_mine
            g_theirs_ref[:m, cols] = g_theirs
            g_normed2[:m, :] += dotf(g_mine, mine[:, cols], NT) + dotf(g_theirs, theirs[:, cols], NT)

        by_steps(gate_ref.shape[1], step, part)
        x, g = after[:m], g_normed2[:m, :]
        factor = inverse(x)
        unit = x * factor
        g_gain[...] = jnp.sum(g * unit, axis=0, keepdims=True)
        scaled = g * gain[...]
        g_after = factor * (scaled - unit * jnp.mean(scaled * unit, axis=-1, keepdims=True))
        g_state[:m, :] += g_after
        low = (g_after + g_branch[:m, :]).astype(BF16)
        g_attn[:m, :] = low
        g_att[:m, :] = dotf(low, wo[:, :width], NT).astype(BF16)
        clear(m, g_ffn, g_attn, g_att, g_mine_ref, g_theirs_ref)

    choose(meta_ref, variants, body)


def expand_back_kernel(step, meta_ref, g_ffn, gate_ref, up_ref, down, g_mine_ref, g_theirs_ref):
    core = meta_ref[1]

    def part(cols):
        g_inner = dotf(g_ffn[...], down[cols, :], NT)
        gate, up = gate_ref[:, cols].astype(F32), up_ref[:, cols].astype(F32)
        sig = sigmoid(gate)
        g_gate = (g_inner * up * sig * (1.0 + gate * (1.0 - sig))).astype(BF16)
        g_up = (g_inner * gate * sig).astype(BF16)
        g_mine_ref[:, cols], g_theirs_ref[:, cols] = roles(core, g_gate, g_up)

    by_steps(gate_ref.shape[1], step, part)


def expand_back_call(meta, g_ffn, gate, up, w, step=512):
    inputs = (g_ffn, gate, up, w["down"])
    return call(
        functools.partial(expand_back_kernel, step),
        "expand_back",
        meta,
        (1,),
        inputs,
        [IN_VMEM] * len(inputs),
        [IN_VMEM] * 2,
        [jax.ShapeDtypeStruct(gate.shape, BF16)] * 2,
        [],
        16,
        2 * gate.size * g_ffn.shape[1],
        2 * w["down"].size,
    )


def norm_back_kernel(step, meta_ref, g_mine, g_theirs, mine, theirs, after, gain, g_branch, grad, wo, g_state, g_attn, g_att, g_gain):
    width = after.shape[1]
    g = dotf(g_mine[...], mine[...], NT) + dotf(g_theirs[...], theirs[...], NT)
    x = after[...]
    factor = inverse(x)
    unit = x * factor
    g_gain[...] = jnp.sum(g * unit, axis=0, keepdims=True)
    scaled = g * gain[...]
    g_after = factor * (scaled - unit * jnp.mean(scaled * unit, axis=-1, keepdims=True))
    g_state[...] = grad[...] + g_after
    low = (g_after + g_branch[...]).astype(BF16)
    g_attn[...] = low
    g_att[...] = dotf(low, wo[:, :width], NT).astype(BF16)


def norm_back_call(meta, g_mine, g_theirs, after, g_branch, grad, w, step=512):
    rows, width = after.shape
    inputs = (g_mine, g_theirs, w["mine"], w["theirs"], after, w["gain_f"], g_branch, grad, w["wide_o"])
    shape = jax.ShapeDtypeStruct
    outputs = [shape((rows, width), k) for k in (F32, BF16, BF16)] + [shape((1, width), F32)]
    return call(
        functools.partial(norm_back_kernel, step),
        "norm_back",
        meta,
        (1,),
        inputs,
        [IN_VMEM] * len(inputs),
        [IN_VMEM] * len(outputs),
        outputs,
        [],
        16,
        2 * rows * width * (width + 2 * g_mine.shape[1]),
        2 * width * (width + 2 * g_mine.shape[1]),
    )


def post_back_call(variants, meta, grad, branch, state, after, router, active, router_row, gate, up, w, step=512):
    rows, width = state.shape
    ff = w["mine"].shape[1]
    shape = jax.ShapeDtypeStruct
    inputs = (grad, branch, state, after, router, active, router_row, w["gain_f"], w["wide_o"], gate, up)
    inputs += (w["mine"], w["theirs"], w["down"])
    outputs = [shape((rows, width), k) for k in (BF16, F32, BF16, BF16)]
    outputs += [shape((1, width), F32)] * 2 + [shape((rows, ff), BF16)] * 2
    return call(
        functools.partial(post_back_kernel, variants, step),
        "post_back",
        meta,
        (1,),
        inputs,
        [IN_VMEM] * len(inputs),
        [IN_VMEM] * len(outputs),
        outputs,
        [pltpu.VMEM((rows, width), F32)] * 2,
        16,
        2 * rows * width * (width + 3 * ff),
        2 * width * (width + 3 * ff),
    )


def qkv_back_kernel(
    variants, meta_ref, dq_ref, mine_ref, got_ref, wq_ref, wkv_ref, x_ref, gain_ref, up_ref, table_ref,
    dkv_ref, out_ref, gain_grad_ref,
):
    def body(m, _):
        cos, sin = turns(table_ref[:m], True)
        for at in range(0, dkv_ref.shape[1], LANES):
            cols = slice(at, at + LANES)
            u = mine_ref[:m, cols].astype(F32) + got_ref[:m, cols].astype(F32)
            dkv_ref[:m, cols] = (u * cos - turn(u) * sin).astype(BF16)
        clear(m, dkv_ref)
        g = dotf(dq_ref[:m], wq_ref[:, : dq_ref.shape[1]], NT) + dotf(dkv_ref[:m, :], wkv_ref[...], NT)
        x = x_ref[:m]
        factor = inverse(x)
        unit = x * factor
        gain_grad_ref[...] = jnp.sum(g * unit, axis=0, keepdims=True)
        scaled = g * gain_ref[...]
        out_ref[:m, :] = up_ref[:m] + factor * (scaled - unit * jnp.mean(scaled * unit, axis=-1, keepdims=True))
        if m < up_ref.shape[0]:
            out_ref[m:, :] = up_ref[m:]

    choose(meta_ref, variants, body)


def qkv_back_call(variants, meta, dq, mine, got, wq, wkv, x, gain, upstream, table):
    rows, width = x.shape
    both = wkv.shape[1]
    return call(
        functools.partial(qkv_back_kernel, variants),
        "qkv_back",
        meta,
        (1,),
        (dq, mine, got, wq, wkv, x, gain, upstream, table),
        [IN_VMEM] * 9,
        [IN_VMEM] * 3,
        [
            jax.ShapeDtypeStruct((rows, both), BF16),
            jax.ShapeDtypeStruct((rows, width), F32),
            jax.ShapeDtypeStruct((1, width), F32),
        ],
        [],
        16,
        2 * rows * width * (width + both),
        2 * width * (width + both) + 16 * rows * width,
    )


def weight_grad_kernel(fill, counts, hand, choices, stride, spot_ref, *refs):
    c = pl.program_id(0)
    n_left, n_right, n_extra, n_ready, levels = counts
    sources, refs = refs[: n_left * levels], refs[n_left * levels :]
    rights, refs = refs[: n_right * levels], refs[n_right * levels :]
    extra, ready, refs = refs[:n_extra], refs[n_extra : n_extra + n_ready], refs[n_extra + n_ready :]
    outs, handed = refs[:5], refs[5 : 5 + (hand is not None)]
    scratch = refs[5 + len(handed) :]
    staged, turned, values, sem = scratch[:n_left], list(scratch[n_left : 2 * n_left]), scratch[-3:-1], scratch[-1]
    if handed:
        turned[hand] = handed[0]
    turned += ready

    def run(sizes):
        starts = [sum(sizes[:i]) for i in range(levels)]
        depth = sum(sizes)

        @pl.when(c == 0)
        def _():
            copies = []
            for i, source in enumerate(sources):
                size = sizes[i % levels]
                target = staged[i // levels].at[pl.ds(starts[i % levels], size), :]
                copies.append(pltpu.make_async_copy(source.at[pl.ds(0, size), :], target, sem.at[i]))
                copies[-1].start()
            for i, copy in enumerate(copies):
                copy.wait()
                if i % levels == levels - 1:
                    turned[i // levels][:, :depth] = staged[i // levels][:depth, :].T

        def product(left, right):
            group = rights[right * levels : (right + 1) * levels]
            stacked = jnp.concatenate([a[:size, :] for a, size in zip(group, sizes)], axis=0)
            return dotf(turned[left][:, :depth], stacked)

        fill(spot_ref[1], c, product, values, extra)

    core = spot_ref[1]
    for i, sizes in enumerate(choices):
        pl.when(spot_ref[2] == i)(functools.partial(run, sizes))
    each, cut = outs[4].shape[1], outs[0].shape[1]
    kept, away = values
    for r in range(4):
        mine = other = pl.multiple_of((spot_ref[0] ^ r) * stride, 16)
        source = away
        if stride != each:
            other = pl.multiple_of(mine + (1 - core) * each, 16)
            mine = pl.multiple_of(mine + core * each, 16)
            source = kept
        outs[r % 2][r // 2] = kept[pl.ds(mine, cut), :]
        outs[2 + r // 2][r % 2] = kept[pl.ds(pl.multiple_of(mine + cut, 16), each - cut), :]
        outs[4][r] = source[pl.ds(other, each), :]


def fill_rows(core, c, product, values, extra):
    values[0][...] = product(0, 0).astype(BF16)


def fill_roles(core, c, product, values, extra):
    for i, value in enumerate(values):
        value[...] = product(0, i).astype(BF16)


def fill_choice(core, c, product, values, extra):
    kept, away = values
    first, second = product(0, 0).astype(BF16), product(1, 1).astype(BF16)
    kept[...] = jnp.where(core == 0, first, second)
    away[...] = jnp.where(core == 0, second, first)


def fill_groups(core, c, product, values, extra):
    kept, away = values
    v = product(0, 0)
    part = kept.shape[1] - LANES
    low, high = v[:, :part].astype(BF16), v[:, v.shape[1] - part :].astype(BF16)
    kept[:, :part] = jnp.where(core == 0, low, high)
    away[:, :part] = jnp.where(core == 0, high, low)
    vectors = extra[0][...].T
    rest = jnp.zeros((vectors.shape[0], LANES - vectors.shape[1]), F32)
    vectors = jnp.concatenate([vectors, rest], axis=1).astype(BF16)
    kept[:, part:] = vectors
    away[:, part:] = vectors


def weight_grad(spot, fill, lefts, rights, stride, each, n, step, choices, extra=(), ready=(), hand=None):
    levels, rows = len(rights[0]), rights[0][0].shape[0]
    depth = levels * rows
    cut = -(-each // 32) * 16
    shapes = [(2, cut, n), (2, cut, n), (2, each - cut, n), (2, each - cut, n), (4, each, n)]
    flops = 2 * depth * 4 * stride * sum(right[0].shape[1] for right in rights)
    sources, moving = [a for group in lefts for a in group], [a for group in rights for a in group]
    by_step = pl.BlockSpec((rows, step), lambda c, s: (0, c))
    given = [] if hand is None else [(lefts[hand][0].shape[1], depth)]
    at_once = lambda a: pl.BlockSpec(a.shape, lambda c, s: (0, 0))
    return pl.pallas_call(
        functools.partial(weight_grad_kernel, fill, (len(lefts), len(rights), len(extra), len(ready), levels), hand, choices, stride),
        grid_spec=pltpu.PrefetchScalarGridSpec(
            num_scalar_prefetch=1,
            grid=(-(-n // step),),
            in_specs=[pl.BlockSpec(memory_space=pl.ANY)] * len(sources)
            + [by_step if n > step else at_once(a) for a in moving]
            + [at_once(a) for a in extra]
            + [IN_VMEM] * len(ready),
            out_specs=[pl.BlockSpec(s[:2] + (step,), lambda c, s: (0, 0, c)) for s in shapes] + [IN_VMEM] * len(given),
            scratch_shapes=[pltpu.VMEM((depth, group[0].shape[1]), BF16) for group in lefts]
            + [pltpu.VMEM((group[0].shape[1], depth), BF16) for group in lefts]
            + [pltpu.VMEM((4 * stride, step), BF16)] * 2
            + [pltpu.SemaphoreType.DMA((max(len(sources), 1),))],
        ),
        out_shape=[jax.ShapeDtypeStruct(s, BF16) for s in shapes + given],
        compiler_params=pltpu.CompilerParams(vmem_limit_bytes=24 * MIB),
        cost_estimate=pl.CostEstimate(
            flops=flops, bytes_accessed=2 * sum(a.size for a in sources + moving) + 16 * each * n, transcendentals=0
        ),
        name="weight_grad",
    )(spot, *sources, *moving, *extra, *ready)


def settle_kernel(moves, spot_ref, *refs):
    out = refs[-1]
    for i, first, rows, place in moves:
        out[pl.ds(pl.multiple_of(place(spot_ref), 16), rows), :] = refs[i][first : first + rows, : out.shape[1]]


def copy_call(kernel, name, spot, arrays, shapes):
    return pl.pallas_call(
        kernel,
        grid_spec=pltpu.PrefetchScalarGridSpec(
            num_scalar_prefetch=1,
            grid=(1,),
            in_specs=[IN_VMEM] * len(arrays),
            out_specs=[IN_VMEM] * len(shapes),
        ),
        out_shape=[jax.ShapeDtypeStruct(shape, arrays[0].dtype) for shape in shapes],
        compiler_params=pltpu.CompilerParams(vmem_limit_bytes=16 * MIB),
        cost_estimate=pl.CostEstimate(flops=0, bytes_accessed=4 * sum(a.size for a in arrays), transcendentals=0),
        name=name,
    )(spot, *arrays)


def settle_call(spot, arrays, moves, rows, width=None):
    shape = (rows, width or arrays[0].shape[1])
    (out,) = copy_call(functools.partial(settle_kernel, moves), "settle", spot, arrays, [shape])
    return out


def unpack_kernel(part, spot_ref, mine, theirs, q_out, o_out, kv_out, tail_out):
    both = kv_out.shape[1]
    tail_out[...] = mine[:, mine.shape[1] - LANES :]

    def go(first, second):
        q_out[...] = first[:, part:]
        o_out[...] = second[:, part:]
        kv_out[:, :part] = first[:, :part]
        kv_out[:, part:] = second[:, 2 * part - both : part]

    pl.when(spot_ref[1] == 0)(lambda: go(mine, theirs))
    pl.when(spot_ref[1] == 1)(lambda: go(theirs, mine))


def unpack_call(spot, mine, theirs, part, both):
    rows, width = mine.shape
    shapes = [(rows, width - part), (rows, width - part), (rows, both), (rows, LANES)]
    return copy_call(functools.partial(unpack_kernel, part), "unpack", spot, (mine, theirs), shapes)


def finish_kernel(part, both, spot_ref, own, other, query, key, value, out, vectors):
    width = query.shape[1]

    def go(low, high):
        out[...] = low[:, part + LANES : part + LANES + width].astype(F32)
        query[...] = high[:, part + LANES : part + LANES + width].astype(F32)
        vectors[...] = low[:, part : part + LANES].astype(F32).T[: vectors.shape[0], :]
        groups = [low[:, at : at + LANES] for at in range(0, part, LANES)]
        groups += [high[:, at : at + LANES] for at in range(2 * part - both, part, LANES)]
        groups = [group.astype(F32) for group in groups]
        lane = lax.broadcasted_iota(jnp.int32, groups[0].shape, 1)
        for i in range(0, len(groups), 2):
            at = i * HEAD_DIM
            a, turned = groups[i], pltpu.roll(groups[i], HEAD_DIM, 1)
            if i + 1 < len(groups):
                b = groups[i + 1]
                key[at : at + LANES, :] = jnp.where(lane < HEAD_DIM, a, pltpu.roll(b, HEAD_DIM, 1)).T
                value[at : at + LANES, :] = jnp.where(lane < HEAD_DIM, turned, b).T
            else:
                key[at : at + HEAD_DIM, :] = a.T[:HEAD_DIM, :]
                value[at : at + HEAD_DIM, :] = turned.T[:HEAD_DIM, :]

    pl.when(spot_ref[1] == 0)(lambda: go(own, other))
    pl.when(spot_ref[1] == 1)(lambda: go(other, own))


def finish_rows_kernel(spot_ref, own, other, out):
    half, width = own.shape[0], out.shape[0]

    def go(low, high):
        out[:, :half] = low[:, :width].astype(F32).T
        out[:, half:] = high[:, :width].astype(F32).T

    pl.when(spot_ref[1] == 0)(lambda: go(own, other))
    pl.when(spot_ref[1] == 1)(lambda: go(other, own))


def finish_rows_call(spot, own, other, width):
    shape = jax.ShapeDtypeStruct((width, 2 * own.shape[0]), F32)
    return call(
        finish_rows_kernel, "finish_rows", spot, (1,), (own, other), [IN_VMEM] * 2, IN_VMEM, shape, [], 16, 0, 8 * own.size
    )


def finish_call(spot, own, other, part, both, width):
    rows = own.shape[0]
    shapes = [(rows, width), (both // 2, rows), (both // 2, rows), (rows, width), (8, rows)]
    return call(
        functools.partial(finish_kernel, part, both),
        "finish",
        spot,
        (1,),
        (own, other),
        [IN_VMEM] * 2,
        [IN_VMEM] * len(shapes),
        [jax.ShapeDtypeStruct(shape, F32) for shape in shapes],
        [],
        16,
        0,
        8 * own.size,
    )


def tie(*trees):
    return lax.optimization_barrier(trees)


def add(*terms):
    return sum(a.astype(F32) for a in terms).astype(BF16)


def at(a, index, axis):
    return lax.dynamic_index_in_dim(a, index, axis, keepdims=False)


class Place:
    def __init__(self, dp, cp):
        self.dp, self.cp, self.square = dp, cp, cp == 4
        dp_at, cp_at = lax.axis_index("dp"), lax.axis_index("cp")
        self.core, self.z = dp_at % 2, dp_at // 2
        self.y, self.x = cp_at // 2, cp_at % 2
        self.spot = jnp.stack([cp_at, self.core]).astype(jnp.int32)

    def over_x(self, a):
        return lax.ppermute(a, "cp", [(i, i ^ 1) for i in range(self.cp)])

    def over_y(self, a):
        return lax.ppermute(a, "cp", [(i, i ^ 2) for i in range(self.cp)])

    def over_core(self, a):
        return lax.ppermute(a, "dp", [(i, i ^ 1) for i in range(self.dp)])

    def move_tokens(self, a):
        if not self.square:
            return a
        pairs = []
        for d in range(self.dp):
            for c in range(self.cp):
                z, core, y, x = d // 2, d % 2, c // 2, c % 2
                pairs.append((d * self.cp + c, (2 * z + y) * self.cp + 2 * core + x))
        return lax.ppermute(a, ("dp", "cp"), pairs)

    def move_wide(self, a):
        return self.move_tokens(jnp.pad(a, ((0, 0), (0, -a.shape[1] % LANES))))

    def fit(self, rows, later):
        sizes = [m for m, _ in variants_of(rows, later[0][1].shape[1])]
        self.choices = (tuple(reversed(sizes)), (rows,) * RECUR)
        fits = jnp.bool_(True)
        for r, (meta, _) in enumerate(later):
            fits = fits & (meta[0] <= RECUR - 2 - r)
        self.grad_spot = jnp.concatenate([self.spot, jnp.where(fits, 0, 1)[None].astype(jnp.int32)])

    def key_block(self):
        return 2 * self.core + self.x if self.square else lax.axis_index("cp")

    def gather_keys(self, a, axis=0):
        if not self.square:
            return (lax.all_gather(a, "cp", axis=axis, tiled=True),)
        from_x, from_core = self.over_x(a), self.over_core(a)
        return a, from_x, from_core, self.over_core(from_x)

    def scatter_keys_first(self, a):
        if not self.square:
            own = lax.psum_scatter(a, "cp", scatter_dimension=0, tiled=True)
            return own, jnp.zeros_like(own)
        rows = a.shape[0] // 4
        return a[: 2 * rows], self.over_core(a[2 * rows :])

    def scatter_keys_second(self, pair):
        if not self.square:
            return pair
        rows = pair[0].shape[0] // 2
        pair = add(*pair)
        return pair[:rows], self.over_x(pair[rows:])


    def gather_first(self, a):
        if not self.square:
            return (lax.all_gather(a, "cp", axis=0, tiled=True),)
        return a, self.over_x(a), self.over_y(a)

    def gather_second(self, parts):
        if not self.square:
            return parts
        own, from_x, from_y = parts
        cut = -(-own.shape[0] // 32) * 16
        return parts + (self.over_y(from_x[:cut]), self.over_x(from_y[cut:]))

    def gather_whole(self, parts):
        if not self.square:
            return parts[0]
        rows, cut = parts[0].shape[0], parts[3].shape[0]

        def move(i, count, block, offset):
            return i, 0, count, lambda spot: (spot[0] ^ block) * rows + offset

        moves = [move(0, rows, 0, 0), move(1, rows, 1, 0), move(2, rows, 2, 0)]
        moves += [move(3, cut, 3, 0), move(4, rows - cut, 3, cut)]
        return settle_call(self.spot, parts, moves, 4 * rows)

    def interleave(self, mine, theirs, width):
        half = mine.shape[0] // self.cp

        def move(i, block):
            return i, block * half, half, lambda spot: (2 * block + (spot[1] if i == 0 else 1 - spot[1])) * half

        moves = [move(i, block) for block in range(self.cp) for i in range(2)]
        return settle_call(self.spot, (mine, theirs), moves, 2 * mine.shape[0], width)


    def halves(self, fill, lefts, rights, stride, each, n, step, extra=(), ready=(), hand=None):
        if self.square:
            return weight_grad(
                self.grad_spot, fill, [] if ready else lefts, rights, stride, each, n, step, self.choices, extra, ready, hand
            )
        products = []

        def product(left, right):
            a, b = (jnp.concatenate(group, axis=0) for group in (lefts[left], rights[right]))
            b = jnp.pad(b, ((0, 0), (0, max(n - b.shape[1], 0)))) if fill is not fill_groups else b
            return dotf(a, b, TN).astype(BF16)

        if fill is fill_rows:
            both = product(0, 0).reshape(self.cp, 2, each, n)
            products = at(both, self.core, 1), at(both, 1 - self.core, 1)
        elif fill is fill_roles:
            products = product(0, 0), product(0, 1)
        elif fill is fill_choice:
            first, second = product(0, 0), product(1, 1)
            products = self.pick(first, second), self.pick(second, first)
        else:
            kv, part = product(0, 0), n - LANES
            low, high = kv[:, :part], kv[:, kv.shape[1] - part :]
            vectors = jnp.pad(extra[0].T, ((0, 0), (0, LANES - extra[0].shape[0]))).astype(BF16)
            products = [jnp.concatenate([self.pick(*pair), vectors], axis=1) for pair in ((low, high), (high, low))]
        return [a.reshape(self.cp, each, n) for a in products]

    def scatter_ready(self, pieces, got, apart=False):
        if not self.square:
            return (add(pieces[0], got),)
        top, top_out, low, low_out = pieces[:4]
        got = got.reshape((2, 2) + got.shape[1:])
        cut = top.shape[1]
        if apart:
            over_x = [add(top_out[i], got[i, 1, :cut]) for i in range(2)]
            over_y = [add(low_out[i], got[1, i, cut:]) for i in range(2)]
            return top, low, got, over_x, over_y
        return top, low, got, add(top_out, got[:, 1, :cut]), add(low_out, got[1, :, cut:])

    def scatter_first(self, parts):
        if not self.square:
            return (lax.psum_scatter(parts[0], "cp", scatter_dimension=0, tiled=False),)
        return parts[:3] + (self.over_x(parts[3]), self.over_y(parts[4]))

    def scatter_open(self, parts):
        if not self.square:
            return self.scatter_first(parts)
        return parts + ([self.over_x(parts[3][1])], [self.over_y(parts[4][1])])

    def scatter_more(self, parts):
        if not self.square:
            return parts
        over_x, over_y, from_x, from_y = parts[3:]
        return parts[:3] + ([self.over_x(over_x[0])] + from_x, [self.over_y(over_y[0])] + from_y)

    def scatter_next(self, parts):
        if not self.square:
            return parts
        top, low, got, from_x, from_y = parts
        cut = top.shape[1]
        top_out = add(top[1], got[1, 0, :cut], from_x[1])
        low_out = add(low[1], got[0, 1, cut:], from_y[1])
        return parts + (top_out, low_out)

    def scatter_second(self, parts):
        if not self.square:
            return parts
        return parts[:5] + (self.over_y(parts[5]), self.over_x(parts[6]))

    def scatter_rows(self, parts):
        if not self.square:
            half = parts[0].shape[0] // 2
            return parts[0][:half], parts[0][half:]
        top, low, got, from_x, from_y, last_y, last_x = parts
        cut = top.shape[1]
        return add(top[0], got[0, 0, :cut], from_x[0], last_y), add(low[0], got[0, 0, cut:], from_y[0], last_x)

    def scatter_whole(self, parts):
        return jnp.concatenate(self.scatter_rows(parts), axis=0)


    def hop(self, a, moves):
        return lax.ppermute(a, "dp", [(2 * s + c, 2 * t + c) for s, t in moves for c in range(2)])

    def z_first(self, a):
        n, got = self.dp // 2, jnp.zeros_like(a)
        for t in range(n // 2 - 1):
            if t:
                a = add(a, got)
            got = self.hop(a, [(t, t + 1), (n - 1 - t, n - 2 - t)])
        return a, got

    def z_second(self, pair):
        n, a = self.dp // 2, add(*pair)
        return a, self.hop(a, [(n // 2 - 1, n // 2), (n // 2, n // 2 - 1)])

    def z_third(self, pair):
        n, a = self.dp // 2, add(*pair)
        back = a
        for t in reversed(range(n // 2 - 1)):
            if t < n // 2 - 2:
                a = jnp.where((self.z == t + 1) | (self.z == n - 2 - t), back, a)
            back = self.hop(a, [(t + 1, t), (n - 2 - t, n - 1 - t)])
        return a, back

    def z_whole(self, pair):
        n = self.dp // 2
        if n < 4:
            return pair[0]
        return jnp.where((self.z == 0) | (self.z == n - 1), pair[1], pair[0])

    def pick(self, a, b):
        return jnp.where(self.core == 0, a, b)


def inverse_rms(matrix):
    return lax.rsqrt(jnp.mean(matrix * matrix, axis=-1, keepdims=True) + NORM_EPSILON)


def row_table(documents, places):
    half = HEAD_DIM // 2
    inverse = jnp.power(ROPE_BASE, -2.0 * jnp.arange(half, dtype=F32) / HEAD_DIM)
    angles = places.astype(F32)[:, None] * inverse[None, :]
    cos, sin = jnp.cos(angles), jnp.sin(angles)
    spread = lambda a: jnp.broadcast_to(a.astype(F32)[:, None], (a.shape[0], LANES))
    return jnp.concatenate([cos] * 4 + [-sin, sin] * 2 + [spread(documents), spread(places)], axis=1)


def depth_order(depth):
    steps = jnp.arange(depth.shape[0])
    before = (depth[:, None] > depth[None, :]) | ((depth[:, None] == depth[None, :]) & (steps[:, None] < steps[None, :]))
    return jnp.sum(before, axis=0)[None, :] == steps[:, None]


def reorder(order, rows):
    return dotf(order.astype(BF16), rows).astype(BF16)


def all_keys(every, rows, core):
    blocks = every.shape[1] // rows
    spots = jnp.stack([rows * jnp.arange(blocks), jnp.full((blocks,), rows)], axis=1).reshape(-1)
    return jnp.concatenate([jnp.stack([0, core]), spots]).astype(jnp.int32), every


def active_keys(every, rows, core, square):
    keys = every.shape[1]
    blocks, steps = keys // rows, jnp.arange(rows)
    levels = jnp.arange(1, RECUR)[:, None]
    counts = jnp.sum((every[2][None] > levels).reshape(RECUR - 1, blocks, rows), axis=2)
    taken = (counts + 15) // 16 * 16
    ahead = jnp.arange(blocks)[:, None] < jnp.arange(blocks)[None, :]
    starts = jnp.sum(jnp.where(ahead[None], taken[:, :, None], 0), axis=1)
    target = jnp.where(steps < taken[:, :, None], starts[:, :, None] + steps, -1).reshape(RECUR - 1, 1, keys, 1)
    hit = target == jnp.arange(keys)
    cols = jnp.sum(jnp.where(hit, every[None, :, :, None] + 1, 0), axis=2) - 1
    total = jnp.sum(taken, axis=1)
    own = counts[:, 0] if square else jnp.max(counts, axis=1)
    (m, n), (wide_m, wide_n), _ = variants_of(rows, keys)
    body = jnp.where((own <= m) & (total <= n), 0, jnp.where((own <= wide_m) & (total <= wide_n), 1, 2))
    spots = jnp.stack([starts, counts], axis=2).reshape(RECUR - 1, -1)
    metas = jnp.concatenate([body[:, None], jnp.full_like(body, core)[:, None], spots], axis=1).astype(jnp.int32)
    return [(metas[i], cols[i].astype(jnp.int32)) for i in range(RECUR - 1)]


class Level:
    def __init__(self, recursion, place, context, meta, col_info):
        self.recursion, self.place, self.meta, self.col_info = recursion, place, meta, col_info
        self.table, depth = context
        rows, keys = self.table.shape[0], self.col_info.shape[1]
        self.variants = variants_of(rows, keys) if recursion else ((rows, keys),)
        self.active = (depth[:, None] > recursion).astype(F32)

    def project(self, state, w):
        self.state = state
        self.q, self.kv, self.normed = qkv_call(
            self.variants, self.meta, state, w["gain_a"], w["q"], w["kv"], self.table
        )

    def attend(self, kvs):
        self.att, self.lse, self.keys = attend_call(
            self.recursion, self.variants, self.meta, self.q, kvs, self.table, self.col_info
        )

    def post(self, w):
        self.router_row = w["router"][self.recursion][None, :]
        state, self.after, self.normed2, self.branch, self.router, self.gate, self.up, self.inner = post_call(
            self.variants, self.meta, self.att, self.state, w, self.router_row, self.active
        )
        return state

    def widen(self, w):
        self.attn = dotf(self.att, w["o"])
        self.after = self.state + self.attn
        self.normed2 = (self.after * inverse_rms(self.after) * w["gain_f"]).astype(BF16)

    def expand(self, w):
        mine, theirs = dotf(self.normed2, w["mine"]), dotf(self.normed2, w["theirs"])
        gate, up = self.place.pick(mine, theirs), self.place.pick(theirs, mine)
        self.inner = (jax.nn.silu(gate) * up).astype(BF16)
        self.gate, self.up = gate.astype(BF16), up.astype(BF16)

    def close(self, w):
        self.branch = self.attn + dotf(self.inner, w["down"])
        self.router_row = w["router"][self.recursion][None, :]
        self.router = jax.nn.sigmoid(jnp.sum(self.state * self.router_row, axis=-1, keepdims=True))
        return self.state + self.active * self.router * self.branch

    def back_open(self, grad):
        self.g_branch = grad * (self.active * self.router)
        g_logit = jnp.sum(grad * self.branch, axis=-1, keepdims=True)
        g_logit = g_logit * self.active * self.router * (1.0 - self.router)
        self.g_router = jnp.sum(g_logit * self.state, axis=0, keepdims=True)
        self.g_state = grad + g_logit * self.router_row
        self.g_ffn = self.g_branch.astype(BF16)

    def back_expand(self, w):
        self.g_mine, self.g_theirs = expand_back_call(self.meta, self.g_ffn, self.gate, self.up, w)

    def back_norm(self, w):
        self.g_state, self.g_attn, self.g_att, self.g_gain_f = norm_back_call(
            self.meta, self.g_mine, self.g_theirs, self.after, self.g_branch, self.g_state, w
        )

    def post_back(self, grad, w):
        out = post_back_call(
            self.variants, self.meta, grad, self.branch, self.state, self.after, self.router, self.active, self.router_row,
            self.gate, self.up, w,
        )
        self.g_ffn, self.g_state, self.g_attn, self.g_att, self.g_router, self.g_gain_f, self.g_mine, self.g_theirs = out

    def back_attend(self):
        self.dq, dkv = attend_back_call(
            self.recursion, self.variants, self.meta, self.q, self.g_att, self.att, self.keys, self.lse, self.table,
            self.col_info,
        )
        return dkv

    def back_project(self, mine, got, w):
        self.dkv, grad, self.g_gain_a = qkv_back_call(
            self.variants, self.meta, self.dq, mine, got, w["q"], w["kv"], self.state, w["gain_a"], self.g_state, self.table
        )
        return grad


def local(tokens, recur_depth, document_ids, cotangent, *shards, dp, cp):
    place = Place(dp, cp)
    wq, wk, wv, wo, gate, up, down, router, gain_a, gain_f = shards
    rows, each = tokens.shape[1], wq.shape[0]
    width, kv_heads = each * cp, wk.shape[1] // HEAD_DIM

    wkv = jnp.stack([wk.reshape(each, kv_heads, HEAD_DIM), wv.reshape(each, kv_heads, HEAD_DIM)], axis=2)
    wkv = wkv.reshape(each, -1)
    small = jnp.concatenate([gain_a[:, None], gain_f[:, None], router.T], axis=1)
    both = wkv.shape[1]
    part = -(-both // (2 * LANES)) * LANES
    spare = -(part + width + small.shape[1]) % LANES
    blend = [place.pick(wkv[:, :part], wkv[:, both - part :]), place.pick(wq, wo), small, jnp.zeros((each, spare), BF16)]
    blend = place.gather_first(jnp.concatenate(blend, axis=1))
    ids = place.move_tokens(jnp.stack([document_ids[0], recur_depth[0]]))
    state = place.move_tokens(tokens[0])
    gates = place.pick(gate, up)
    downs = place.pick(down[: down.shape[0] // 2], down[down.shape[0] // 2 :])
    padded = -(-width // LANES) * LANES
    downs = jnp.pad(downs, ((0, 0), (0, padded - width)))
    blend, ids, state, gates, downs = tie(blend, ids, state, gates, downs)

    blend = place.gather_second(blend)
    steps = jnp.arange(rows, dtype=jnp.int32)
    order = depth_order(ids[1])
    ids = jnp.stack([ids[0], place.key_block() * rows + steps, ids[1]])
    ids = jnp.sum(jnp.where(order[None], ids[:, None, :], 0), axis=2)
    every = jnp.concatenate(place.gather_keys(ids, 1), axis=1)
    table = row_table(ids[0], ids[1])
    state = reorder(order, state)
    context = (table, ids[2])
    blend, context, order, state, gates, every = tie(blend, context, order, state.astype(F32), gates, every)

    g_part = place.gather_first(gates)
    mine = place.gather_whole(blend)
    theirs = place.over_core(mine)
    w = dict(zip(("q", "o", "kv", "tail"), unpack_call(place.spot, mine, theirs, part, both)))
    edge = width % LANES
    small = w["tail"][:, edge : edge + small.shape[1]].T.astype(F32)
    w["wide_o"], w["o"] = w["o"], w["o"][:, :width]
    w["gain_a"], w["gain_f"], w["router"] = small[:1], small[1:2], small[2:]
    first = Level(0, place, context, *all_keys(every, rows, place.core))
    first.project(state, w)
    first.kv, downs, every = tie(first.kv, downs, every)

    kvs = place.gather_keys(first.kv)
    later = active_keys(every, rows, place.core, place.square)
    kvs, g_part, downs, later = tie(kvs, g_part, downs, later)

    g_part = place.gather_second(g_part)
    d_part = place.gather_first(downs)
    first.attend(kvs)
    first.widen(w)
    first.normed2, g_part, d_part = tie(first.normed2, g_part, d_part)
    place.fit(rows, later)
    levels = [first] + [Level(r + 1, place, context, *found) for r, found in enumerate(later)]

    d_part = place.gather_second(d_part)
    w["mine"] = place.gather_whole(g_part)
    w["theirs"] = place.over_core(w["mine"])
    first.expand(w)
    first.inner, d_part = tie(first.inner, d_part)

    mine = place.gather_whole(d_part)
    w["down"] = place.interleave(mine, place.over_core(mine), width)
    state = first.close(w)

    for level in levels[1:]:
        level.project(state, w)
        level.attend(place.gather_keys(level.kv))
        state = level.post(w)
    activations = place.move_wide(reorder(order.T, state.astype(BF16)))
    grad = reorder(order, place.move_tokens(cotangent[0])).astype(F32)

    for level in levels[:0:-1]:
        level.post_back(grad, w)
        pair = place.scatter_keys_second(place.scatter_keys_first(level.back_attend()))
        grad = level.back_project(*pair, w)

    every = lambda name: [getattr(level, name) for level in levels]
    ff = gate.shape[1]

    grad, activations = tie(grad, activations)
    first.back_open(grad)
    d = place.halves(fill_rows, [every("inner")], [every("g_ffn")], ff // cp, ff // cp // 2, padded, 512)
    d_got = place.over_core(d[-1])
    first.back_expand(w)
    d = place.scatter_ready(d, d_got)
    d, first.g_mine, first.g_theirs = tie(d, first.g_mine, first.g_theirs)

    d = place.scatter_first(d)
    u = place.halves(fill_roles, [every("normed2")], [every("g_mine"), every("g_theirs")], each, each, ff, 512)
    d, u = tie(d, u)

    u_got = place.over_core(u[-1])
    d = place.scatter_next(d)
    d, first.g_mine, first.g_theirs = tie(d, first.g_mine, first.g_theirs)
    d = place.scatter_second(d)
    first.back_norm(w)
    u = place.scatter_ready(u, u_got, True)
    d, u, first.g_att = tie(d, u, first.g_att)

    u = place.scatter_open(u)
    d = place.z_first(place.scatter_whole(d))
    dkv = first.back_attend()
    u, d, dkv = tie(u, d, dkv)

    pair = place.scatter_keys_first(dkv)
    (pair,) = tie(pair)
    pair = place.scatter_keys_second(pair)
    u = place.scatter_more(u)
    lefts, rights = [every("att"), every("normed")], [every("g_attn"), every("dq")]
    p = place.halves(fill_choice, lefts, rights, each, each, padded, 512, hand=1)
    u, pair, p = tie(u, pair, p)

    u = place.scatter_next(u)
    u, pair = tie(u, pair)
    u = place.scatter_second(u)
    p_got = place.over_core(p[4] if place.square else p[1])
    grad = first.back_project(*pair, w)
    vectors = every("g_router") + [sum(every("g_gain_a")), sum(every("g_gain_f"))]
    vectors = jnp.concatenate(vectors + [jnp.zeros((8 - len(vectors), width), F32)], axis=0)
    ready = p[5:] if place.square else ()
    k = place.halves(
        fill_groups, [every("normed")], [every("dkv")], each, each, part + LANES, part + LANES, (vectors,), ready=ready
    )
    p = place.scatter_ready(p, p_got)
    u, p, k, grad = tie(u, p, k, grad)

    k_got = place.over_core(k[-1])
    u, v = place.scatter_rows(u)
    u = place.z_first(u)
    p = place.scatter_first(p)
    k = place.scatter_first(place.scatter_ready(k, k_got))
    d = place.z_second(d)
    u, v, p, k, d = tie(u, v, p, k, d)

    p, k = place.scatter_next(p), place.scatter_next(k)
    u, v, p, k, d = tie(u, v, p, k, d)
    p, k = place.scatter_second(p), place.scatter_second(k)
    u, v = place.z_second(u), place.z_first(v)
    d = place.z_third(d)
    input_grad = place.move_wide(reorder(order.T, grad.astype(BF16)))
    u, v, p, k, d, input_grad, activations = tie(u, v, p, k, d, input_grad, activations)

    a = jnp.concatenate([place.scatter_whole(k), place.scatter_whole(p)], axis=1)
    u, v, a = tie(u, v, a)
    u, v, a = place.z_third(u), place.z_second(v), place.z_first(a)
    u, v, a = tie(u, v, a)

    a, v = place.z_second(a), place.z_third(v)
    d_own = place.z_whole(d)
    grad_down = finish_rows_call(place.spot, d_own, place.over_core(d_own), width).T
    input_grad, activations = (b[None, :, :width] for b in (input_grad, activations))
    a, v, grad_down, input_grad, activations = tie(a, v, grad_down, input_grad, activations)

    a = place.z_third(a)
    u_own = jnp.concatenate([place.z_whole(u), place.z_whole(v)], axis=0)
    u_other = place.over_core(u_own)
    grad_gate, grad_up = place.pick(u_own, u_other).astype(F32), place.pick(u_other, u_own).astype(F32)
    a, grad_gate, grad_up = tie(a, grad_gate, grad_up)

    own = place.z_whole(a)
    other = place.over_core(own)
    grad_query, grad_key, grad_value, grad_out, vectors = finish_call(place.spot, own, other, part, both, width)
    return (
        activations,
        input_grad,
        grad_query,
        grad_key.T,
        grad_value.T,
        grad_out,
        grad_gate,
        grad_up,
        grad_down,
        vectors[:RECUR],
        vectors[RECUR],
        vectors[RECUR + 1],
    )


def solution(mesh):
    by_token = P("dp", "cp", None)
    by_row = P("cp", None)
    in_specs = (by_token, P("dp", "cp"), P("dp", "cp"), by_token) + (by_row,) * 7 + (P(None, "cp"), P("cp"), P("cp"))
    out_specs = (by_token, by_token) + (by_row,) * 7 + (P(None, "cp"), P("cp"), P("cp"))
    step = functools.partial(local, dp=mesh.shape["dp"], cp=mesh.shape["cp"])
    return jax.shard_map(step, mesh=mesh, in_specs=in_specs, out_specs=out_specs, check_vma=False)
```

```python
import functools

import jax
import jax.numpy as jnp
from jax import lax
from jax.experimental import pallas as pl
from jax.experimental.pallas import tpu as pltpu
from jax.sharding import PartitionSpec as P

HEAD_DIM = 64
LANES = 128
GROUP = 3
RECUR = 3
NORM_EPSILON = 1e-05
MASKED_SCORE = -1e30
ROPE_BASE = 10000.0
SCALE = HEAD_DIM ** (-0.5)
MIB = 2**20
F32, BF16 = jnp.float32, jnp.bfloat16
NN = (((1,), (0,)), ((), ()))
NT = (((1,), (1,)), ((), ()))
TN = (((0,), (0,)), ((), ()))


def dotf(a, b, dims=NN):
    return lax.dot_general(a, b, dims, preferred_element_type=F32)


def turn(u):
    lane = lax.broadcasted_iota(jnp.int32, u.shape, 1) % HEAD_DIM
    return jnp.where(lane < HEAD_DIM // 2, pltpu.roll(u, LANES - 32, 1), pltpu.roll(u, 32, 1))


def variants_of(rows, keys):
    pick = lambda count, third, unit: (count * third // 3 // unit + 1) * unit
    return tuple((pick(rows, k, 32), pick(keys, k, LANES)) for k in (1, 2)) + ((rows, keys),)


def choose(meta_ref, variants, body):
    if len(variants) == 1:
        body(*variants[0])
    else:
        for i, variant in enumerate(variants):
            pl.when(meta_ref[0] == i)(functools.partial(body, *variant))


def clear(m, *refs):
    for ref in refs:
        if m < ref.shape[0]:
            ref[m:, :] = jnp.zeros((ref.shape[0] - m, ref.shape[1]), ref.dtype)


def call(kernel, name, meta, grid, inputs, in_specs, out_specs, out_shape, scratch, vmem, flops, traffic):
    return pl.pallas_call(
        kernel,
        grid_spec=pltpu.PrefetchScalarGridSpec(
            num_scalar_prefetch=1, grid=grid, in_specs=in_specs, out_specs=out_specs, scratch_shapes=scratch
        ),
        out_shape=out_shape,
        compiler_params=pltpu.CompilerParams(vmem_limit_bytes=vmem * MIB),
        cost_estimate=pl.CostEstimate(flops=flops, bytes_accessed=traffic, transcendentals=0),
        name=name,
    )(meta, *inputs)


def whole(*shape):
    return pl.BlockSpec(shape, lambda g, s: (0,) * len(shape))


IN_VMEM = pl.BlockSpec(memory_space=pltpu.VMEM)


def turns(table, keys):
    cos, sin = table[:, :LANES], table[:, LANES : 2 * LANES]
    if not keys:
        return cos, sin
    lane = lax.broadcasted_iota(jnp.int32, cos.shape, 1)
    return jnp.where(lane < HEAD_DIM, cos, 1.0), jnp.where(lane < HEAD_DIM, sin, 0.0)


def qkv_kernel(
    variants, meta_ref, x_ref, gain_ref, wq_ref, wkv_ref, table_ref, q_ref, kv_ref, normed_ref
):
    width = q_ref.shape[1]

    def body(m, _):
        x = x_ref[:m]
        factor = lax.rsqrt(jnp.mean(x * x, axis=-1, keepdims=True) + NORM_EPSILON)
        normed = (x * factor * gain_ref[...]).astype(BF16)
        normed_ref[:m, :] = normed
        kv = dotf(normed, wkv_ref[...])
        cos, sin = turns(table_ref[:m], True)
        for at in range(0, kv_ref.shape[1], LANES):
            u = kv[:, at : at + LANES]
            kv_ref[:m, at : at + LANES] = (u * cos + turn(u) * sin).astype(BF16)
        q = dotf(normed, wq_ref[:, :width])
        cos, sin = turns(table_ref[:m], False)
        for at in range(0, width, LANES):
            if at + LANES <= width:
                u = q[:, at : at + LANES]
            else:
                u = jnp.concatenate([q[:, at:], jnp.zeros((m, at + LANES - width), F32)], axis=1)
            r = (u * cos + turn(u) * sin).astype(BF16)
            q_ref[:m, at : min(at + LANES, width)] = r[:, : min(LANES, width - at)]
        clear(m, q_ref, kv_ref, normed_ref)

    choose(meta_ref, variants, body)


def qkv_call(variants, meta, x, gain, wq, wkv, table):
    rows, width = x.shape
    both = wkv.shape[1]
    return call(
        functools.partial(qkv_kernel, variants),
        "norm_qkv_rope",
        meta,
        (1,),
        (x, gain, wq, wkv, table),
        [IN_VMEM] * 5,
        [IN_VMEM] * 3,
        [jax.ShapeDtypeStruct((rows, k), BF16) for k in (width, both, width)],
        [],
        16,
        2 * rows * width * (width + both),
        2 * width * (width + both) + 8 * rows * width,
    )


def make_bias(row_table, col_info, recursion):
    doc_r, pos_r = (row_table[:, k : k + 1].astype(jnp.int32) for k in (2 * LANES + HEAD_DIM, 3 * LANES + HEAD_DIM))
    doc_c, pos_c, depth_c = col_info[0:1, :], col_info[1:2, :], col_info[2:3, :]
    live = (depth_c > recursion) | (pos_c == pos_r)
    allowed = (pos_c <= pos_r) & (doc_c == doc_r) & live
    return jnp.where(allowed, 0.0, MASKED_SCORE).astype(F32)


def split_pairs(packed, out, to_left):
    m, width = packed.shape
    lane = lax.broadcasted_iota(jnp.int32, (m, LANES), 1)
    for at in range(0, width, LANES):
        h = at // HEAD_DIM
        if at + LANES <= width:
            u = packed[:, at : at + LANES].astype(F32)
        else:
            u = jnp.concatenate([packed[:, at:].astype(F32), jnp.zeros((m, at + LANES - width), F32)], axis=1)
        v = pltpu.roll(u, HEAD_DIM, 1)
        first, second = (u, v) if to_left else (v, u)
        keep = (lane < HEAD_DIM) if to_left else (lane >= HEAD_DIM)
        out[h, :m] = jnp.where(keep, first, 0.0).astype(out.dtype)
        if at + LANES <= width:
            out[h + 1, :m] = jnp.where(keep, second, 0.0).astype(out.dtype)


def join_pairs(scr, out_ref, from_left, m):
    heads = scr.shape[0]
    lane = lax.broadcasted_iota(jnp.int32, (m, LANES), 1)
    for h in range(0, heads, 2):
        at = h * HEAD_DIM
        a = scr[h, :m] if from_left else pltpu.roll(scr[h, :m], HEAD_DIM, 1)
        if h + 1 < heads:
            b = pltpu.roll(scr[h + 1, :m], HEAD_DIM, 1) if from_left else scr[h + 1, :m]
            out_ref[:m, at : at + LANES] = jnp.where(lane < HEAD_DIM, a, b).astype(out_ref.dtype)
        else:
            out_ref[:m, at : at + HEAD_DIM] = a[:, :HEAD_DIM].astype(out_ref.dtype)


def compact_keys(meta_ref, key_refs, rows, keys):
    keys[...] = jnp.zeros_like(keys)
    block = 0
    for ref in key_refs:
        for first in range(0, ref.shape[0], rows):
            keys[pl.ds(pl.multiple_of(meta_ref[2 + 2 * block], 16), rows), :] = ref[first : first + rows, :]
            block += 1


def by_group(count, do):
    def one(g, _):
        do(g, pl.ds(pl.multiple_of(g * LANES, LANES), LANES))
        return 0

    lax.fori_loop(0, count, one, 0)


def stacked(m):
    return GROUP if GROUP * m <= 400 else 1


def attend_kernel(recursion, variants, count, meta_ref, q_ref, *refs):
    key_refs, (row_ref, col_ref, att_ref, lse_ref, keys, bias, q_all, o_all) = refs[:count], refs[count:]
    rows, groups = q_ref.shape[0], keys.shape[1] // LANES
    compact_keys(meta_ref, key_refs, rows, keys)
    lse_ref[...] = jnp.zeros_like(lse_ref)

    def body(m, n):
        bias[:m, :n] = make_bias(row_ref[:m], col_ref[:, :n], recursion)
        split_pairs(q_ref[:m] * jnp.bfloat16(SCALE), q_all, True)
        at_once = stacked(m)

        def group(g, cols):
            kv = keys[:n, cols]
            lane = lax.broadcasted_iota(jnp.int32, (m, LANES), 1)
            sets = [[g * GROUP + first + j for j in range(at_once)] for first in range(0, GROUP, at_once)]

            def score(heads):
                queries = jnp.concatenate([q_all[h, :m] for h in heads], axis=0)
                return dotf(queries, kv, NT) + jnp.concatenate([bias[:m, :n]] * at_once, axis=0)

            s = score(sets[0])
            for i, heads in enumerate(sets):
                following = score(sets[i + 1]) if i + 1 < len(sets) else None
                peak = jnp.max(s, axis=1, keepdims=True)
                e = jnp.exp(s - peak)
                total = jnp.sum(e, axis=1, keepdims=True)
                o = dotf(e.astype(BF16), kv) / total
                log = peak + jnp.log(total)
                for j, h in enumerate(heads):
                    here = slice(j * m, (j + 1) * m)
                    o_all[h, :m] = o[here]
                    lse_ref[:m, :] = jnp.where(lane == h, log[here], lse_ref[:m, :])
                s = following

        by_group(groups, group)
        join_pairs(o_all, att_ref, False, m)
        clear(m, att_ref)

    choose(meta_ref, variants, body)


def attend_call(recursion, variants, meta, q, kvs, row_info, col_info):
    rows, width = q.shape
    keys, both = sum(k.shape[0] for k in kvs), kvs[0].shape[1]
    heads = both // LANES * GROUP
    shape = jax.ShapeDtypeStruct
    inputs = (q, *kvs, row_info, col_info)
    return call(
        functools.partial(attend_kernel, recursion, variants, len(kvs)),
        "attend",
        meta,
        (1,),
        inputs,
        [IN_VMEM] * len(inputs),
        [IN_VMEM] * 3,
        [shape((rows, width), BF16), shape((rows, LANES), F32), shape((keys, both), BF16)],
        [
            pltpu.VMEM((rows, keys), F32),
            pltpu.VMEM((heads, rows, LANES), BF16),
            pltpu.VMEM((heads, rows, LANES), F32),
        ],
        16,
        4 * rows * keys * LANES * heads,
        4 * q.size + 2 * keys * both,
    )


def attend_back_kernel(
    recursion, variants, meta_ref, q_ref, do_ref, att_ref, keys, lse_ref, row_ref, col_ref, dq_ref, dkv_ref,
    bias, back, q_all, do_all, p3, ds3, dq_all,
):
    rows, groups = q_ref.shape[0], keys.shape[1] // LANES

    def body(m, n):
        bias[:m, :n] = make_bias(row_ref[:m], col_ref[:, :n], recursion)
        split_pairs(q_ref[:m] * jnp.bfloat16(SCALE), q_all, True)
        split_pairs(do_ref[:m], do_all, False)
        split_pairs(do_ref[:m].astype(F32) * att_ref[:m].astype(F32), dq_all, True)
        at_once = stacked(m)

        def group(g, cols):
            kv = keys[:n, cols]
            cos, sin = turns(row_ref[:m], False)
            lane = lax.broadcasted_iota(jnp.int32, (m, LANES), 1)
            for first in range(0, GROUP, at_once):
                heads = [g * GROUP + first + j for j in range(at_once)]
                here = slice(first * m, (first + at_once) * m)
                stack = lambda parts: jnp.concatenate(parts, axis=0)
                logs = stack([jnp.sum(jnp.where(lane == h, lse_ref[:m], 0.0), axis=1, keepdims=True) for h in heads])
                dots = stack([jnp.sum(dq_all[h, :m], axis=1, keepdims=True) for h in heads])
                s = dotf(stack([q_all[h, :m] for h in heads]), kv, NT) + stack([bias[:m, :n]] * at_once)
                p = jnp.exp(s - logs)
                dp = dotf(stack([do_all[h, :m] for h in heads]), kv, NT)
                ds = (p * (dp - dots)).astype(BF16)
                p3[here, :n] = p.astype(BF16)
                ds3[here, :n] = ds
                dq = dotf(ds, kv) * SCALE
                for j, h in enumerate(heads):
                    one = dq[j * m : (j + 1) * m]
                    dq_all[h, :m] = one * cos - turn(one) * sin
            q3 = jnp.concatenate([q_all[g * GROUP + j, :m] for j in range(GROUP)], axis=0)
            do3 = jnp.concatenate([do_all[g * GROUP + j, :m] for j in range(GROUP)], axis=0)
            dkv = dotf(q3, ds3[: GROUP * m, :n], TN) + dotf(do3, p3[: GROUP * m, :n], TN)
            back[:n, cols] = dkv.T

        by_group(groups, group)
        join_pairs(dq_all, dq_ref, True, m)
        clear(m, dq_ref)

    choose(meta_ref, variants, body)
    spot = lax.broadcasted_iota(jnp.int32, (rows, back.shape[1]), 0)
    for block in range(dkv_ref.shape[0] // rows):
        part = back[pl.ds(pl.multiple_of(meta_ref[2 + 2 * block], 16), rows), :]
        part = jnp.where(spot < meta_ref[3 + 2 * block], part, 0.0)
        dkv_ref[block * rows : (block + 1) * rows, :] = part.astype(BF16)


def attend_back_call(recursion, variants, meta, q, do, att, kv, lse, row_info, col_info):
    rows, width = q.shape
    keys, both = kv.shape
    heads = both // LANES * GROUP
    inputs = (q, do, att, kv, lse, row_info, col_info)
    return call(
        functools.partial(attend_back_kernel, recursion, variants),
        "attend_back",
        meta,
        (1,),
        inputs,
        [IN_VMEM] * len(inputs),
        [IN_VMEM] * 2,
        [jax.ShapeDtypeStruct((rows, width), BF16), jax.ShapeDtypeStruct((keys, both), BF16)],
        [
            pltpu.VMEM((rows, keys), F32),
            pltpu.VMEM((keys, both), F32),
            pltpu.VMEM((heads, rows, LANES), BF16),
            pltpu.VMEM((heads, rows, LANES), BF16),
            pltpu.VMEM((GROUP * rows, keys), BF16),
            pltpu.VMEM((GROUP * rows, keys), BF16),
            pltpu.VMEM((heads, rows, LANES), F32),
        ],
        24,
        10 * rows * keys * LANES * heads,
        8 * q.size + 4 * keys * both,
    )


def inverse(x):
    return lax.rsqrt(jnp.mean(x * x, axis=-1, keepdims=True) + NORM_EPSILON)


def sigmoid(x):
    return 1.0 / (1.0 + jnp.exp(-x))


def roles(core, a, b):
    return jnp.where(core == 0, a, b), jnp.where(core == 0, b, a)


def by_steps(width, step, do):
    def one(c, _):
        do(pl.ds(pl.multiple_of(c * step, step), step))
        return 0

    lax.fori_loop(0, width // step, one, 0)


def post_kernel(variants, step, meta_ref, att, state, wo, gain, router_row, active, mine, theirs, down, *refs):
    following, after, normed2, branch, router, gate_ref, up_ref, inner_ref = refs
    core, width = meta_ref[1], state.shape[1]

    def body(m, _):
        attn = dotf(att[:m], wo[:, :width])
        x = state[:m] + attn
        after[:m, :] = x
        normed2[:m, :] = (x * inverse(x) * gain[...]).astype(BF16)
        branch[:m, :] = attn

        def part(cols):
            n2 = normed2[:m, :]
            gate, up = roles(core, dotf(n2, mine[:, cols]), dotf(n2, theirs[:, cols]))
            inner = (gate * sigmoid(gate) * up).astype(BF16)
            inner_ref[:m, cols] = inner
            gate_ref[:m, cols] = gate.astype(BF16)
            up_ref[:m, cols] = up.astype(BF16)
            branch[:m, :] += dotf(inner, down[cols, :])

        by_steps(inner_ref.shape[1], step, part)
        clear(m, after, normed2, branch, inner_ref, gate_ref, up_ref)

    choose(meta_ref, variants, body)
    x = state[...]
    router[...] = sigmoid(jnp.sum(x * router_row[...], axis=-1, keepdims=True))
    following[...] = x + active[...] * router[...] * branch[...]


def post_call(variants, meta, att, state, w, router_row, active, step=512):
    rows, width = state.shape
    ff = w["mine"].shape[1]
    shape = jax.ShapeDtypeStruct
    inputs = (att, state, w["wide_o"], w["gain_f"], router_row, active, w["mine"], w["theirs"], w["down"])
    outputs = [shape((rows, width), F32), shape((rows, width), F32), shape((rows, width), BF16), shape((rows, width), F32)]
    outputs += [shape((rows, 1), F32)] + [shape((rows, ff), BF16)] * 3
    return call(
        functools.partial(post_kernel, variants, step),
        "post",
        meta,
        (1,),
        inputs,
        [IN_VMEM] * len(inputs),
        [IN_VMEM] * len(outputs),
        outputs,
        [],
        16,
        2 * rows * width * (width + 3 * ff),
        2 * width * (width + 3 * ff),
    )


def post_back_kernel(
    variants, step, meta_ref, grad, branch, state, after, router, active, router_row, gain, wo, gate_ref, up_ref, mine, theirs,
    down, g_ffn, g_state, g_attn, g_att, g_router, g_gain, g_mine_ref, g_theirs_ref, g_branch, g_normed2,
):
    core, width = meta_ref[1], state.shape[1]

    def body(m, _):
        g = grad[:m]
        weight = active[:m] * router[:m]
        logit = jnp.sum(g * branch[:m], axis=-1, keepdims=True) * weight * (1.0 - router[:m])
        g_router[...] = jnp.sum(logit * state[:m], axis=0, keepdims=True)
        g_state[:m, :] = g + logit * router_row[...]
        if m < grad.shape[0]:
            g_state[m:, :] = grad[m:]
        low = g * weight
        g_branch[:m, :] = low
        g_ffn[:m, :] = low.astype(BF16)
        g_normed2[:m, :] = jnp.zeros((m, width), F32)

        def part(cols):
            g_inner = dotf(g_ffn[:m, :], down[cols, :], NT)
            gate, up = gate_ref[:m, cols].astype(F32), up_ref[:m, cols].astype(F32)
            sig = sigmoid(gate)
            g_gate = (g_inner * up * sig * (1.0 + gate * (1.0 - sig))).astype(BF16)
            g_up = (g_inner * gate * sig).astype(BF16)
            g_mine, g_theirs = roles(core, g_gate, g_up)
            g_mine_ref[:m, cols] = g_mine
            g_theirs_ref[:m, cols] = g_theirs
            g_normed2[:m, :] += dotf(g_mine, mine[:, cols], NT) + dotf(g_theirs, theirs[:, cols], NT)

        by_steps(gate_ref.shape[1], step, part)
        x, g = after[:m], g_normed2[:m, :]
        factor = inverse(x)
        unit = x * factor
        g_gain[...] = jnp.sum(g * unit, axis=0, keepdims=True)
        scaled = g * gain[...]
        g_after = factor * (scaled - unit * jnp.mean(scaled * unit, axis=-1, keepdims=True))
        g_state[:m, :] += g_after
        low = (g_after + g_branch[:m, :]).astype(BF16)
        g_attn[:m, :] = low
        g_att[:m, :] = dotf(low, wo[:, :width], NT).astype(BF16)
        clear(m, g_ffn, g_attn, g_att, g_mine_ref, g_theirs_ref)

    choose(meta_ref, variants, body)


def expand_back_kernel(step, meta_ref, g_ffn, gate_ref, up_ref, down, g_mine_ref, g_theirs_ref):
    core = meta_ref[1]

    def part(cols):
        g_inner = dotf(g_ffn[...], down[cols, :], NT)
        gate, up = gate_ref[:, cols].astype(F32), up_ref[:, cols].astype(F32)
        sig = sigmoid(gate)
        g_gate = (g_inner * up * sig * (1.0 + gate * (1.0 - sig))).astype(BF16)
        g_up = (g_inner * gate * sig).astype(BF16)
        g_mine_ref[:, cols], g_theirs_ref[:, cols] = roles(core, g_gate, g_up)

    by_steps(gate_ref.shape[1], step, part)


def expand_back_call(meta, g_ffn, gate, up, w, step=512):
    inputs = (g_ffn, gate, up, w["down"])
    return call(
        functools.partial(expand_back_kernel, step),
        "expand_back",
        meta,
        (1,),
        inputs,
        [IN_VMEM] * len(inputs),
        [IN_VMEM] * 2,
        [jax.ShapeDtypeStruct(gate.shape, BF16)] * 2,
        [],
        16,
        2 * gate.size * g_ffn.shape[1],
        2 * w["down"].size,
    )


def norm_back_kernel(step, meta_ref, g_mine, g_theirs, mine, theirs, after, gain, g_branch, grad, wo, g_state, g_attn, g_att, g_gain):
    width = after.shape[1]
    g = dotf(g_mine[...], mine[...], NT) + dotf(g_theirs[...], theirs[...], NT)
    x = after[...]
    factor = inverse(x)
    unit = x * factor
    g_gain[...] = jnp.sum(g * unit, axis=0, keepdims=True)
    scaled = g * gain[...]
    g_after = factor * (scaled - unit * jnp.mean(scaled * unit, axis=-1, keepdims=True))
    g_state[...] = grad[...] + g_after
    low = (g_after + g_branch[...]).astype(BF16)
    g_attn[...] = low
    g_att[...] = dotf(low, wo[:, :width], NT).astype(BF16)


def norm_back_call(meta, g_mine, g_theirs, after, g_branch, grad, w, step=512):
    rows, width = after.shape
    inputs = (g_mine, g_theirs, w["mine"], w["theirs"], after, w["gain_f"], g_branch, grad, w["wide_o"])
    shape = jax.ShapeDtypeStruct
    outputs = [shape((rows, width), k) for k in (F32, BF16, BF16)] + [shape((1, width), F32)]
    return call(
        functools.partial(norm_back_kernel, step),
        "norm_back",
        meta,
        (1,),
        inputs,
        [IN_VMEM] * len(inputs),
        [IN_VMEM] * len(outputs),
        outputs,
        [],
        16,
        2 * rows * width * (width + 2 * g_mine.shape[1]),
        2 * width * (width + 2 * g_mine.shape[1]),
    )


def post_back_call(variants, meta, grad, branch, state, after, router, active, router_row, gate, up, w, step=512):
    rows, width = state.shape
    ff = w["mine"].shape[1]
    shape = jax.ShapeDtypeStruct
    inputs = (grad, branch, state, after, router, active, router_row, w["gain_f"], w["wide_o"], gate, up)
    inputs += (w["mine"], w["theirs"], w["down"])
    outputs = [shape((rows, width), k) for k in (BF16, F32, BF16, BF16)]
    outputs += [shape((1, width), F32)] * 2 + [shape((rows, ff), BF16)] * 2
    return call(
        functools.partial(post_back_kernel, variants, step),
        "post_back",
        meta,
        (1,),
        inputs,
        [IN_VMEM] * len(inputs),
        [IN_VMEM] * len(outputs),
        outputs,
        [pltpu.VMEM((rows, width), F32)] * 2,
        16,
        2 * rows * width * (width + 3 * ff),
        2 * width * (width + 3 * ff),
    )


def qkv_back_kernel(
    variants, meta_ref, dq_ref, mine_ref, got_ref, wq_ref, wkv_ref, x_ref, gain_ref, up_ref, table_ref,
    dkv_ref, out_ref, gain_grad_ref,
):
    def body(m, _):
        cos, sin = turns(table_ref[:m], True)
        for at in range(0, dkv_ref.shape[1], LANES):
            cols = slice(at, at + LANES)
            u = mine_ref[:m, cols].astype(F32) + got_ref[:m, cols].astype(F32)
            dkv_ref[:m, cols] = (u * cos - turn(u) * sin).astype(BF16)
        clear(m, dkv_ref)
        g = dotf(dq_ref[:m], wq_ref[:, : dq_ref.shape[1]], NT) + dotf(dkv_ref[:m, :], wkv_ref[...], NT)
        x = x_ref[:m]
        factor = inverse(x)
        unit = x * factor
        gain_grad_ref[...] = jnp.sum(g * unit, axis=0, keepdims=True)
        scaled = g * gain_ref[...]
        out_ref[:m, :] = up_ref[:m] + factor * (scaled - unit * jnp.mean(scaled * unit, axis=-1, keepdims=True))
        if m < up_ref.shape[0]:
            out_ref[m:, :] = up_ref[m:]

    choose(meta_ref, variants, body)


def qkv_back_call(variants, meta, dq, mine, got, wq, wkv, x, gain, upstream, table):
    rows, width = x.shape
    both = wkv.shape[1]
    return call(
        functools.partial(qkv_back_kernel, variants),
        "qkv_back",
        meta,
        (1,),
        (dq, mine, got, wq, wkv, x, gain, upstream, table),
        [IN_VMEM] * 9,
        [IN_VMEM] * 3,
        [
            jax.ShapeDtypeStruct((rows, both), BF16),
            jax.ShapeDtypeStruct((rows, width), F32),
            jax.ShapeDtypeStruct((1, width), F32),
        ],
        [],
        16,
        2 * rows * width * (width + both),
        2 * width * (width + both) + 16 * rows * width,
    )


def weight_grad_kernel(fill, counts, hand, choices, stride, spot_ref, *refs):
    c = pl.program_id(0)
    n_left, n_right, n_extra, n_ready, levels = counts
    sources, refs = refs[: n_left * levels], refs[n_left * levels :]
    rights, refs = refs[: n_right * levels], refs[n_right * levels :]
    extra, ready, refs = refs[:n_extra], refs[n_extra : n_extra + n_ready], refs[n_extra + n_ready :]
    outs, handed = refs[:5], refs[5 : 5 + (hand is not None)]
    scratch = refs[5 + len(handed) :]
    staged, turned, values, sem = scratch[:n_left], list(scratch[n_left : 2 * n_left]), scratch[-3:-1], scratch[-1]
    if handed:
        turned[hand] = handed[0]
    turned += ready

    def run(sizes):
        starts = [sum(sizes[:i]) for i in range(levels)]
        depth = sum(sizes)

        @pl.when(c == 0)
        def _():
            copies = []
            for i, source in enumerate(sources):
                size = sizes[i % levels]
                target = staged[i // levels].at[pl.ds(starts[i % levels], size), :]
                copies.append(pltpu.make_async_copy(source.at[pl.ds(0, size), :], target, sem.at[i]))
                copies[-1].start()
            for i, copy in enumerate(copies):
                copy.wait()
                if i % levels == levels - 1:
                    turned[i // levels][:, :depth] = staged[i // levels][:depth, :].T

        def product(left, right):
            group = rights[right * levels : (right + 1) * levels]
            stacked = jnp.concatenate([a[:size, :] for a, size in zip(group, sizes)], axis=0)
            return dotf(turned[left][:, :depth], stacked)

        fill(spot_ref[1], c, product, values, extra)

    core = spot_ref[1]
    for i, sizes in enumerate(choices):
        pl.when(spot_ref[2] == i)(functools.partial(run, sizes))
    each, cut = outs[4].shape[1], outs[0].shape[1]
    kept, away = values
    for r in range(4):
        mine = other = pl.multiple_of((spot_ref[0] ^ r) * stride, 16)
        source = away
        if stride != each:
            other = pl.multiple_of(mine + (1 - core) * each, 16)
            mine = pl.multiple_of(mine + core * each, 16)
            source = kept
        outs[r % 2][r // 2] = kept[pl.ds(mine, cut), :]
        outs[2 + r // 2][r % 2] = kept[pl.ds(pl.multiple_of(mine + cut, 16), each - cut), :]
        outs[4][r] = source[pl.ds(other, each), :]


def fill_rows(core, c, product, values, extra):
    values[0][...] = product(0, 0).astype(BF16)


def fill_roles(core, c, product, values, extra):
    for i, value in enumerate(values):
        value[...] = product(0, i).astype(BF16)


def fill_choice(core, c, product, values, extra):
    kept, away = values
    first, second = product(0, 0).astype(BF16), product(1, 1).astype(BF16)
    kept[...] = jnp.where(core == 0, first, second)
    away[...] = jnp.where(core == 0, second, first)


def fill_groups(core, c, product, values, extra):
    kept, away = values
    v = product(0, 0)
    part = kept.shape[1] - LANES
    low, high = v[:, :part].astype(BF16), v[:, v.shape[1] - part :].astype(BF16)
    kept[:, :part] = jnp.where(core == 0, low, high)
    away[:, :part] = jnp.where(core == 0, high, low)
    vectors = extra[0][...].T
    rest = jnp.zeros((vectors.shape[0], LANES - vectors.shape[1]), F32)
    vectors = jnp.concatenate([vectors, rest], axis=1).astype(BF16)
    kept[:, part:] = vectors
    away[:, part:] = vectors


def weight_grad(spot, fill, lefts, rights, stride, each, n, step, choices, extra=(), ready=(), hand=None):
    levels, rows = len(rights[0]), rights[0][0].shape[0]
    depth = levels * rows
    cut = -(-each // 32) * 16
    shapes = [(2, cut, n), (2, cut, n), (2, each - cut, n), (2, each - cut, n), (4, each, n)]
    flops = 2 * depth * 4 * stride * sum(right[0].shape[1] for right in rights)
    sources, moving = [a for group in lefts for a in group], [a for group in rights for a in group]
    by_step = pl.BlockSpec((rows, step), lambda c, s: (0, c))
    given = [] if hand is None else [(lefts[hand][0].shape[1], depth)]
    at_once = lambda a: pl.BlockSpec(a.shape, lambda c, s: (0, 0))
    return pl.pallas_call(
        functools.partial(weight_grad_kernel, fill, (len(lefts), len(rights), len(extra), len(ready), levels), hand, choices, stride),
        grid_spec=pltpu.PrefetchScalarGridSpec(
            num_scalar_prefetch=1,
            grid=(-(-n // step),),
            in_specs=[pl.BlockSpec(memory_space=pl.ANY)] * len(sources)
            + [by_step if n > step else at_once(a) for a in moving]
            + [at_once(a) for a in extra]
            + [IN_VMEM] * len(ready),
            out_specs=[pl.BlockSpec(s[:2] + (step,), lambda c, s: (0, 0, c)) for s in shapes] + [IN_VMEM] * len(given),
            scratch_shapes=[pltpu.VMEM((depth, group[0].shape[1]), BF16) for group in lefts]
            + [pltpu.VMEM((group[0].shape[1], depth), BF16) for group in lefts]
            + [pltpu.VMEM((4 * stride, step), BF16)] * 2
            + [pltpu.SemaphoreType.DMA((max(len(sources), 1),))],
        ),
        out_shape=[jax.ShapeDtypeStruct(s, BF16) for s in shapes + given],
        compiler_params=pltpu.CompilerParams(vmem_limit_bytes=24 * MIB),
        cost_estimate=pl.CostEstimate(
            flops=flops, bytes_accessed=2 * sum(a.size for a in sources + moving) + 16 * each * n, transcendentals=0
        ),
        name="weight_grad",
    )(spot, *sources, *moving, *extra, *ready)


def settle_kernel(moves, spot_ref, *refs):
    out = refs[-1]
    for i, first, rows, place in moves:
        out[pl.ds(pl.multiple_of(place(spot_ref), 16), rows), :] = refs[i][first : first + rows, : out.shape[1]]


def copy_call(kernel, name, spot, arrays, shapes):
    return pl.pallas_call(
        kernel,
        grid_spec=pltpu.PrefetchScalarGridSpec(
            num_scalar_prefetch=1,
            grid=(1,),
            in_specs=[IN_VMEM] * len(arrays),
            out_specs=[IN_VMEM] * len(shapes),
        ),
        out_shape=[jax.ShapeDtypeStruct(shape, arrays[0].dtype) for shape in shapes],
        compiler_params=pltpu.CompilerParams(vmem_limit_bytes=16 * MIB),
        cost_estimate=pl.CostEstimate(flops=0, bytes_accessed=4 * sum(a.size for a in arrays), transcendentals=0),
        name=name,
    )(spot, *arrays)


def settle_call(spot, arrays, moves, rows, width=None):
    shape = (rows, width or arrays[0].shape[1])
    (out,) = copy_call(functools.partial(settle_kernel, moves), "settle", spot, arrays, [shape])
    return out


def unpack_kernel(part, spot_ref, mine, theirs, q_out, o_out, kv_out, tail_out):
    both = kv_out.shape[1]
    tail_out[...] = mine[:, mine.shape[1] - LANES :]

    def go(first, second):
        q_out[...] = first[:, part:]
        o_out[...] = second[:, part:]
        kv_out[:, :part] = first[:, :part]
        kv_out[:, part:] = second[:, 2 * part - both : part]

    pl.when(spot_ref[1] == 0)(lambda: go(mine, theirs))
    pl.when(spot_ref[1] == 1)(lambda: go(theirs, mine))


def unpack_call(spot, mine, theirs, part, both):
    rows, width = mine.shape
    shapes = [(rows, width - part), (rows, width - part), (rows, both), (rows, LANES)]
    return copy_call(functools.partial(unpack_kernel, part), "unpack", spot, (mine, theirs), shapes)


def finish_kernel(part, both, spot_ref, own, other, query, key, value, out, vectors):
    width = query.shape[1]

    def go(low, high):
        out[...] = low[:, part + LANES : part + LANES + width].astype(F32)
        query[...] = high[:, part + LANES : part + LANES + width].astype(F32)
        vectors[...] = low[:, part : part + LANES].astype(F32).T[: vectors.shape[0], :]
        groups = [low[:, at : at + LANES] for at in range(0, part, LANES)]
        groups += [high[:, at : at + LANES] for at in range(2 * part - both, part, LANES)]
        groups = [group.astype(F32) for group in groups]
        lane = lax.broadcasted_iota(jnp.int32, groups[0].shape, 1)
        for i in range(0, len(groups), 2):
            at = i * HEAD_DIM
            a, turned = groups[i], pltpu.roll(groups[i], HEAD_DIM, 1)
            if i + 1 < len(groups):
                b = groups[i + 1]
                key[at : at + LANES, :] = jnp.where(lane < HEAD_DIM, a, pltpu.roll(b, HEAD_DIM, 1)).T
                value[at : at + LANES, :] = jnp.where(lane < HEAD_DIM, turned, b).T
            else:
                key[at : at + HEAD_DIM, :] = a.T[:HEAD_DIM, :]
                value[at : at + HEAD_DIM, :] = turned.T[:HEAD_DIM, :]

    pl.when(spot_ref[1] == 0)(lambda: go(own, other))
    pl.when(spot_ref[1] == 1)(lambda: go(other, own))


def finish_rows_kernel(spot_ref, own, other, out):
    half, width = own.shape[0], out.shape[0]

    def go(low, high):
        out[:, :half] = low[:, :width].astype(F32).T
        out[:, half:] = high[:, :width].astype(F32).T

    pl.when(spot_ref[1] == 0)(lambda: go(own, other))
    pl.when(spot_ref[1] == 1)(lambda: go(other, own))


def finish_rows_call(spot, own, other, width):
    shape = jax.ShapeDtypeStruct((width, 2 * own.shape[0]), F32)
    return call(
        finish_rows_kernel, "finish_rows", spot, (1,), (own, other), [IN_VMEM] * 2, IN_VMEM, shape, [], 16, 0, 8 * own.size
    )


def finish_call(spot, own, other, part, both, width):
    rows = own.shape[0]
    shapes = [(rows, width), (both // 2, rows), (both // 2, rows), (rows, width), (8, rows)]
    return call(
        functools.partial(finish_kernel, part, both),
        "finish",
        spot,
        (1,),
        (own, other),
        [IN_VMEM] * 2,
        [IN_VMEM] * len(shapes),
        [jax.ShapeDtypeStruct(shape, F32) for shape in shapes],
        [],
        16,
        0,
        8 * own.size,
    )


def tie(*trees):
    return lax.optimization_barrier(trees)


def add(*terms):
    return sum(a.astype(F32) for a in terms).astype(BF16)


def at(a, index, axis):
    return lax.dynamic_index_in_dim(a, index, axis, keepdims=False)


class Place:
    def __init__(self, dp, cp):
        self.dp, self.cp, self.square = dp, cp, cp == 4
        dp_at, cp_at = lax.axis_index("dp"), lax.axis_index("cp")
        self.core, self.z = dp_at % 2, dp_at // 2
        self.y, self.x = cp_at // 2, cp_at % 2
        self.spot = jnp.stack([cp_at, self.core]).astype(jnp.int32)

    def over_x(self, a):
        return lax.ppermute(a, "cp", [(i, i ^ 1) for i in range(self.cp)])

    def over_y(self, a):
        return lax.ppermute(a, "cp", [(i, i ^ 2) for i in range(self.cp)])

    def over_core(self, a):
        return lax.ppermute(a, "dp", [(i, i ^ 1) for i in range(self.dp)])

    def move_tokens(self, a):
        if not self.square:
            return a
        pairs = []
        for d in range(self.dp):
            for c in range(self.cp):
                z, core, y, x = d // 2, d % 2, c // 2, c % 2
                pairs.append((d * self.cp + c, (2 * z + y) * self.cp + 2 * core + x))
        return lax.ppermute(a, ("dp", "cp"), pairs)

    def move_wide(self, a):
        return self.move_tokens(jnp.pad(a, ((0, 0), (0, -a.shape[1] % LANES))))

    def fit(self, rows, later):
        sizes = [m for m, _ in variants_of(rows, later[0][1].shape[1])]
        self.choices = (tuple(reversed(sizes)), (rows,) * RECUR)
        fits = jnp.bool_(True)
        for r, (meta, _) in enumerate(later):
            fits = fits & (meta[0] <= RECUR - 2 - r)
        self.grad_spot = jnp.concatenate([self.spot, jnp.where(fits, 0, 1)[None].astype(jnp.int32)])

    def key_block(self):
        return 2 * self.core + self.x if self.square else lax.axis_index("cp")

    def gather_keys(self, a, axis=0):
        if not self.square:
            return (lax.all_gather(a, "cp", axis=axis, tiled=True),)
        from_x, from_core = self.over_x(a), self.over_core(a)
        return a, from_x, from_core, self.over_core(from_x)

    def scatter_keys_first(self, a):
        if not self.square:
            own = lax.psum_scatter(a, "cp", scatter_dimension=0, tiled=True)
            return own, jnp.zeros_like(own)
        rows = a.shape[0] // 4
        return a[: 2 * rows], self.over_core(a[2 * rows :])

    def scatter_keys_second(self, pair):
        if not self.square:
            return pair
        rows = pair[0].shape[0] // 2
        pair = add(*pair)
        return pair[:rows], self.over_x(pair[rows:])


    def gather_first(self, a):
        if not self.square:
            return (lax.all_gather(a, "cp", axis=0, tiled=True),)
        return a, self.over_x(a), self.over_y(a)

    def gather_second(self, parts):
        if not self.square:
            return parts
        own, from_x, from_y = parts
        cut = -(-own.shape[0] // 32) * 16
        return parts + (self.over_y(from_x[:cut]), self.over_x(from_y[cut:]))

    def gather_whole(self, parts):
        if not self.square:
            return parts[0]
        rows, cut = parts[0].shape[0], parts[3].shape[0]

        def move(i, count, block, offset):
            return i, 0, count, lambda spot: (spot[0] ^ block) * rows + offset

        moves = [move(0, rows, 0, 0), move(1, rows, 1, 0), move(2, rows, 2, 0)]
        moves += [move(3, cut, 3, 0), move(4, rows - cut, 3, cut)]
        return settle_call(self.spot, parts, moves, 4 * rows)

    def interleave(self, mine, theirs, width):
        half = mine.shape[0] // self.cp

        def move(i, block):
            return i, block * half, half, lambda spot: (2 * block + (spot[1] if i == 0 else 1 - spot[1])) * half

        moves = [move(i, block) for block in range(self.cp) for i in range(2)]
        return settle_call(self.spot, (mine, theirs), moves, 2 * mine.shape[0], width)


    def halves(self, fill, lefts, rights, stride, each, n, step, extra=(), ready=(), hand=None):
        if self.square:
            return weight_grad(
                self.grad_spot, fill, [] if ready else lefts, rights, stride, each, n, step, self.choices, extra, ready, hand
            )
        products = []

        def product(left, right):
            a, b = (jnp.concatenate(group, axis=0) for group in (lefts[left], rights[right]))
            b = jnp.pad(b, ((0, 0), (0, max(n - b.shape[1], 0)))) if fill is not fill_groups else b
            return dotf(a, b, TN).astype(BF16)

        if fill is fill_rows:
            both = product(0, 0).reshape(self.cp, 2, each, n)
            products = at(both, self.core, 1), at(both, 1 - self.core, 1)
        elif fill is fill_roles:
            products = product(0, 0), product(0, 1)
        elif fill is fill_choice:
            first, second = product(0, 0), product(1, 1)
            products = self.pick(first, second), self.pick(second, first)
        else:
            kv, part = product(0, 0), n - LANES
            low, high = kv[:, :part], kv[:, kv.shape[1] - part :]
            vectors = jnp.pad(extra[0].T, ((0, 0), (0, LANES - extra[0].shape[0]))).astype(BF16)
            products = [jnp.concatenate([self.pick(*pair), vectors], axis=1) for pair in ((low, high), (high, low))]
        return [a.reshape(self.cp, each, n) for a in products]

    def scatter_ready(self, pieces, got, apart=False):
        if not self.square:
            return (add(pieces[0], got),)
        top, top_out, low, low_out = pieces[:4]
        got = got.reshape((2, 2) + got.shape[1:])
        cut = top.shape[1]
        if apart:
            over_x = [add(top_out[i], got[i, 1, :cut]) for i in range(2)]
            over_y = [add(low_out[i], got[1, i, cut:]) for i in range(2)]
            return top, low, got, over_x, over_y
        return top, low, got, add(top_out, got[:, 1, :cut]), add(low_out, got[1, :, cut:])

    def scatter_first(self, parts):
        if not self.square:
            return (lax.psum_scatter(parts[0], "cp", scatter_dimension=0, tiled=False),)
        return parts[:3] + (self.over_x(parts[3]), self.over_y(parts[4]))

    def scatter_open(self, parts):
        if not self.square:
            return self.scatter_first(parts)
        return parts + ([self.over_x(parts[3][1])], [self.over_y(parts[4][1])])

    def scatter_more(self, parts):
        if not self.square:
            return parts
        over_x, over_y, from_x, from_y = parts[3:]
        return parts[:3] + ([self.over_x(over_x[0])] + from_x, [self.over_y(over_y[0])] + from_y)

    def scatter_next(self, parts):
        if not self.square:
            return parts
        top, low, got, from_x, from_y = parts
        cut = top.shape[1]
        top_out = add(top[1], got[1, 0, :cut], from_x[1])
        low_out = add(low[1], got[0, 1, cut:], from_y[1])
        return parts + (top_out, low_out)

    def scatter_second(self, parts):
        if not self.square:
            return parts
        return parts[:5] + (self.over_y(parts[5]), self.over_x(parts[6]))

    def scatter_rows(self, parts):
        if not self.square:
            half = parts[0].shape[0] // 2
            return parts[0][:half], parts[0][half:]
        top, low, got, from_x, from_y, last_y, last_x = parts
        cut = top.shape[1]
        return add(top[0], got[0, 0, :cut], from_x[0], last_y), add(low[0], got[0, 0, cut:], from_y[0], last_x)

    def scatter_whole(self, parts):
        return jnp.concatenate(self.scatter_rows(parts), axis=0)


    def hop(self, a, moves):
        return lax.ppermute(a, "dp", [(2 * s + c, 2 * t + c) for s, t in moves for c in range(2)])

    def z_first(self, a):
        n, got = self.dp // 2, jnp.zeros_like(a)
        for t in range(n // 2 - 1):
            if t:
                a = add(a, got)
            got = self.hop(a, [(t, t + 1), (n - 1 - t, n - 2 - t)])
        return a, got

    def z_second(self, pair):
        n, a = self.dp // 2, add(*pair)
        return a, self.hop(a, [(n // 2 - 1, n // 2), (n // 2, n // 2 - 1)])

    def z_third(self, pair):
        n, a = self.dp // 2, add(*pair)
        back = a
        for t in reversed(range(n // 2 - 1)):
            if t < n // 2 - 2:
                a = jnp.where((self.z == t + 1) | (self.z == n - 2 - t), back, a)
            back = self.hop(a, [(t + 1, t), (n - 2 - t, n - 1 - t)])
        return a, back

    def z_whole(self, pair):
        n = self.dp // 2
        if n < 4:
            return pair[0]
        return jnp.where((self.z == 0) | (self.z == n - 1), pair[1], pair[0])

    def pick(self, a, b):
        return jnp.where(self.core == 0, a, b)


def inverse_rms(matrix):
    return lax.rsqrt(jnp.mean(matrix * matrix, axis=-1, keepdims=True) + NORM_EPSILON)


def row_table(documents, places):
    half = HEAD_DIM // 2
    inverse = jnp.power(ROPE_BASE, -2.0 * jnp.arange(half, dtype=F32) / HEAD_DIM)
    angles = places.astype(F32)[:, None] * inverse[None, :]
    cos, sin = jnp.cos(angles), jnp.sin(angles)
    spread = lambda a: jnp.broadcast_to(a.astype(F32)[:, None], (a.shape[0], LANES))
    return jnp.concatenate([cos] * 4 + [-sin, sin] * 2 + [spread(documents), spread(places)], axis=1)


def depth_order(depth):
    steps = jnp.arange(depth.shape[0])
    before = (depth[:, None] > depth[None, :]) | ((depth[:, None] == depth[None, :]) & (steps[:, None] < steps[None, :]))
    return jnp.sum(before, axis=0)[None, :] == steps[:, None]


def reorder(order, rows):
    return dotf(order.astype(BF16), rows).astype(BF16)


def all_keys(every, rows, core):
    blocks = every.shape[1] // rows
    spots = jnp.stack([rows * jnp.arange(blocks), jnp.full((blocks,), rows)], axis=1).reshape(-1)
    return jnp.concatenate([jnp.stack([0, core]), spots]).astype(jnp.int32), every


def active_keys(every, rows, core, square):
    keys = every.shape[1]
    blocks, steps = keys // rows, jnp.arange(rows)
    levels = jnp.arange(1, RECUR)[:, None]
    counts = jnp.sum((every[2][None] > levels).reshape(RECUR - 1, blocks, rows), axis=2)
    taken = (counts + 15) // 16 * 16
    ahead = jnp.arange(blocks)[:, None] < jnp.arange(blocks)[None, :]
    starts = jnp.sum(jnp.where(ahead[None], taken[:, :, None], 0), axis=1)
    target = jnp.where(steps < taken[:, :, None], starts[:, :, None] + steps, -1).reshape(RECUR - 1, 1, keys, 1)
    hit = target == jnp.arange(keys)
    cols = jnp.sum(jnp.where(hit, every[None, :, :, None] + 1, 0), axis=2) - 1
    total = jnp.sum(taken, axis=1)
    own = counts[:, 0] if square else jnp.max(counts, axis=1)
    (m, n), (wide_m, wide_n), _ = variants_of(rows, keys)
    body = jnp.where((own <= m) & (total <= n), 0, jnp.where((own <= wide_m) & (total <= wide_n), 1, 2))
    spots = jnp.stack([starts, counts], axis=2).reshape(RECUR - 1, -1)
    metas = jnp.concatenate([body[:, None], jnp.full_like(body, core)[:, None], spots], axis=1).astype(jnp.int32)
    return [(metas[i], cols[i].astype(jnp.int32)) for i in range(RECUR - 1)]


class Level:
    def __init__(self, recursion, place, context, meta, col_info):
        self.recursion, self.place, self.meta, self.col_info = recursion, place, meta, col_info
        self.table, depth = context
        rows, keys = self.table.shape[0], self.col_info.shape[1]
        self.variants = variants_of(rows, keys) if recursion else ((rows, keys),)
        self.active = (depth[:, None] > recursion).astype(F32)

    def project(self, state, w):
        self.state = state
        self.q, self.kv, self.normed = qkv_call(
            self.variants, self.meta, state, w["gain_a"], w["q"], w["kv"], self.table
        )

    def attend(self, kvs):
        self.att, self.lse, self.keys = attend_call(
            self.recursion, self.variants, self.meta, self.q, kvs, self.table, self.col_info
        )

    def post(self, w):
        self.router_row = w["router"][self.recursion][None, :]
        state, self.after, self.normed2, self.branch, self.router, self.gate, self.up, self.inner = post_call(
            self.variants, self.meta, self.att, self.state, w, self.router_row, self.active
        )
        return state

    def widen(self, w):
        self.attn = dotf(self.att, w["o"])
        self.after = self.state + self.attn
        self.normed2 = (self.after * inverse_rms(self.after) * w["gain_f"]).astype(BF16)

    def expand(self, w):
        mine, theirs = dotf(self.normed2, w["mine"]), dotf(self.normed2, w["theirs"])
        gate, up = self.place.pick(mine, theirs), self.place.pick(theirs, mine)
        self.inner = (jax.nn.silu(gate) * up).astype(BF16)
        self.gate, self.up = gate.astype(BF16), up.astype(BF16)

    def close(self, w):
        self.branch = self.attn + dotf(self.inner, w["down"])
        self.router_row = w["router"][self.recursion][None, :]
        self.router = jax.nn.sigmoid(jnp.sum(self.state * self.router_row, axis=-1, keepdims=True))
        return self.state + self.active * self.router * self.branch

    def back_open(self, grad):
        self.g_branch = grad * (self.active * self.router)
        g_logit = jnp.sum(grad * self.branch, axis=-1, keepdims=True)
        g_logit = g_logit * self.active * self.router * (1.0 - self.router)
        self.g_router = jnp.sum(g_logit * self.state, axis=0, keepdims=True)
        self.g_state = grad + g_logit * self.router_row
        self.g_ffn = self.g_branch.astype(BF16)

    def back_expand(self, w):
        self.g_mine, self.g_theirs = expand_back_call(self.meta, self.g_ffn, self.gate, self.up, w)

    def back_norm(self, w):
        self.g_state, self.g_attn, self.g_att, self.g_gain_f = norm_back_call(
            self.meta, self.g_mine, self.g_theirs, self.after, self.g_branch, self.g_state, w
        )

    def post_back(self, grad, w):
        out = post_back_call(
            self.variants, self.meta, grad, self.branch, self.state, self.after, self.router, self.active, self.router_row,
            self.gate, self.up, w,
        )
        self.g_ffn, self.g_state, self.g_attn, self.g_att, self.g_router, self.g_gain_f, self.g_mine, self.g_theirs = out

    def back_attend(self):
        self.dq, dkv = attend_back_call(
            self.recursion, self.variants, self.meta, self.q, self.g_att, self.att, self.keys, self.lse, self.table,
            self.col_info,
        )
        return dkv

    def back_project(self, mine, got, w):
        self.dkv, grad, self.g_gain_a = qkv_back_call(
            self.variants, self.meta, self.dq, mine, got, w["q"], w["kv"], self.state, w["gain_a"], self.g_state, self.table
        )
        return grad


def local(tokens, recur_depth, document_ids, cotangent, *shards, dp, cp):
    place = Place(dp, cp)
    wq, wk, wv, wo, gate, up, down, router, gain_a, gain_f = shards
    rows, each = tokens.shape[1], wq.shape[0]
    width, kv_heads = each * cp, wk.shape[1] // HEAD_DIM

    wkv = jnp.stack([wk.reshape(each, kv_heads, HEAD_DIM), wv.reshape(each, kv_heads, HEAD_DIM)], axis=2)
    wkv = wkv.reshape(each, -1)
    small = jnp.concatenate([gain_a[:, None], gain_f[:, None], router.T], axis=1)
    both = wkv.shape[1]
    part = -(-both // (2 * LANES)) * LANES
    spare = -(part + width + small.shape[1]) % LANES
    blend = [place.pick(wkv[:, :part], wkv[:, both - part :]), place.pick(wq, wo), small, jnp.zeros((each, spare), BF16)]
    blend = place.gather_first(jnp.concatenate(blend, axis=1))
    ids = place.move_tokens(jnp.stack([document_ids[0], recur_depth[0]]))
    state = place.move_tokens(tokens[0])
    gates = place.pick(gate, up)
    downs = place.pick(down[: down.shape[0] // 2], down[down.shape[0] // 2 :])
    padded = -(-width // LANES) * LANES
    downs = jnp.pad(downs, ((0, 0), (0, padded - width)))
    blend, ids, state, gates, downs = tie(blend, ids, state, gates, downs)

    blend = place.gather_second(blend)
    steps = jnp.arange(rows, dtype=jnp.int32)
    order = depth_order(ids[1])
    ids = jnp.stack([ids[0], place.key_block() * rows + steps, ids[1]])
    ids = jnp.sum(jnp.where(order[None], ids[:, None, :], 0), axis=2)
    every = jnp.concatenate(place.gather_keys(ids, 1), axis=1)
    table = row_table(ids[0], ids[1])
    state = reorder(order, state)
    context = (table, ids[2])
    blend, context, order, state, gates, every = tie(blend, context, order, state.astype(F32), gates, every)

    g_part = place.gather_first(gates)
    mine = place.gather_whole(blend)
    theirs = place.over_core(mine)
    w = dict(zip(("q", "o", "kv", "tail"), unpack_call(place.spot, mine, theirs, part, both)))
    edge = width % LANES
    small = w["tail"][:, edge : edge + small.shape[1]].T.astype(F32)
    w["wide_o"], w["o"] = w["o"], w["o"][:, :width]
    w["gain_a"], w["gain_f"], w["router"] = small[:1], small[1:2], small[2:]
    first = Level(0, place, context, *all_keys(every, rows, place.core))
    first.project(state, w)
    first.kv, downs, every = tie(first.kv, downs, every)

    kvs = place.gather_keys(first.kv)
    later = active_keys(every, rows, place.core, place.square)
    kvs, g_part, downs, later = tie(kvs, g_part, downs, later)

    g_part = place.gather_second(g_part)
    d_part = place.gather_first(downs)
    first.attend(kvs)
    first.widen(w)
    first.normed2, g_part, d_part = tie(first.normed2, g_part, d_part)
    place.fit(rows, later)
    levels = [first] + [Level(r + 1, place, context, *found) for r, found in enumerate(later)]

    d_part = place.gather_second(d_part)
    w["mine"] = place.gather_whole(g_part)
    w["theirs"] = place.over_core(w["mine"])
    first.expand(w)
    first.inner, d_part = tie(first.inner, d_part)

    mine = place.gather_whole(d_part)
    w["down"] = place.interleave(mine, place.over_core(mine), width)
    state = first.close(w)

    for level in levels[1:]:
        level.project(state, w)
        level.attend(place.gather_keys(level.kv))
        state = level.post(w)
    activations = place.move_wide(reorder(order.T, state.astype(BF16)))
    grad = reorder(order, place.move_tokens(cotangent[0])).astype(F32)

    for level in levels[:0:-1]:
        level.post_back(grad, w)
        pair = place.scatter_keys_second(place.scatter_keys_first(level.back_attend()))
        grad = level.back_project(*pair, w)

    every = lambda name: [getattr(level, name) for level in levels]
    ff = gate.shape[1]

    grad, activations = tie(grad, activations)
    first.back_open(grad)
    d = place.halves(fill_rows, [every("inner")], [every("g_ffn")], ff // cp, ff // cp // 2, padded, 512)
    d_got = place.over_core(d[-1])
    first.back_expand(w)
    d = place.scatter_ready(d, d_got)
    d, first.g_mine, first.g_theirs = tie(d, first.g_mine, first.g_theirs)

    d = place.scatter_first(d)
    u = place.halves(fill_roles, [every("normed2")], [every("g_mine"), every("g_theirs")], each, each, ff, 512)
    d, u = tie(d, u)

    u_got = place.over_core(u[-1])
    d = place.scatter_next(d)
    d, first.g_mine, first.g_theirs = tie(d, first.g_mine, first.g_theirs)
    d = place.scatter_second(d)
    first.back_norm(w)
    u = place.scatter_ready(u, u_got, True)
    d, u, first.g_att = tie(d, u, first.g_att)

    u = place.scatter_open(u)
    d = place.z_first(place.scatter_whole(d))
    dkv = first.back_attend()
    u, d, dkv = tie(u, d, dkv)

    pair = place.scatter_keys_first(dkv)
    (pair,) = tie(pair)
    pair = place.scatter_keys_second(pair)
    u = place.scatter_more(u)
    lefts, rights = [every("att"), every("normed")], [every("g_attn"), every("dq")]
    p = place.halves(fill_choice, lefts, rights, each, each, padded, 512, hand=1)
    u, pair, p = tie(u, pair, p)

    u = place.scatter_next(u)
    u, pair = tie(u, pair)
    u = place.scatter_second(u)
    p_got = place.over_core(p[4] if place.square else p[1])
    grad = first.back_project(*pair, w)
    vectors = every("g_router") + [sum(every("g_gain_a")), sum(every("g_gain_f"))]
    vectors = jnp.concatenate(vectors + [jnp.zeros((8 - len(vectors), width), F32)], axis=0)
    ready = p[5:] if place.square else ()
    k = place.halves(
        fill_groups, [every("normed")], [every("dkv")], each, each, part + LANES, part + LANES, (vectors,), ready=ready
    )
    p = place.scatter_ready(p, p_got)
    u, p, k, grad = tie(u, p, k, grad)

    k_got = place.over_core(k[-1])
    u, v = place.scatter_rows(u)
    u = place.z_first(u)
    p = place.scatter_first(p)
    k = place.scatter_first(place.scatter_ready(k, k_got))
    d = place.z_second(d)
    u, v, p, k, d = tie(u, v, p, k, d)

    p, k = place.scatter_next(p), place.scatter_next(k)
    u, v, p, k, d = tie(u, v, p, k, d)
    p, k = place.scatter_second(p), place.scatter_second(k)
    u, v = place.z_second(u), place.z_first(v)
    d = place.z_third(d)
    input_grad = place.move_wide(reorder(order.T, grad.astype(BF16)))
    u, v, p, k, d, input_grad, activations = tie(u, v, p, k, d, input_grad, activations)

    a = jnp.concatenate([place.scatter_whole(k), place.scatter_whole(p)], axis=1)
    u, v, a = tie(u, v, a)
    u, v, a = place.z_third(u), place.z_second(v), place.z_first(a)
    u, v, a = tie(u, v, a)

    a, v = place.z_second(a), place.z_third(v)
    d_own = place.z_whole(d)
    grad_down = finish_rows_call(place.spot, d_own, place.over_core(d_own), width).T
    input_grad, activations = (b[None, :, :width] for b in (input_grad, activations))
    a, v, grad_down, input_grad, activations = tie(a, v, grad_down, input_grad, activations)

    a = place.z_third(a)
    u_own = jnp.concatenate([place.z_whole(u), place.z_whole(v)], axis=0)
    u_other = place.over_core(u_own)
    grad_gate, grad_up = place.pick(u_own, u_other).astype(F32), place.pick(u_other, u_own).astype(F32)
    a, grad_gate, grad_up = tie(a, grad_gate, grad_up)

    own = place.z_whole(a)
    other = place.over_core(own)
    grad_query, grad_key, grad_value, grad_out, vectors = finish_call(place.spot, own, other, part, both, width)
    return (
        activations,
        input_grad,
        grad_query,
        grad_key.T,
        grad_value.T,
        grad_out,
        grad_gate,
        grad_up,
        grad_down,
        vectors[:RECUR],
        vectors[RECUR],
        vectors[RECUR + 1],
    )


def solution(mesh):
    by_token = P("dp", "cp", None)
    by_row = P("cp", None)
    in_specs = (by_token, P("dp", "cp"), P("dp", "cp"), by_token) + (by_row,) * 7 + (P(None, "cp"), P("cp"), P("cp"))
    out_specs = (by_token, by_token) + (by_row,) * 7 + (P(None, "cp"), P("cp"), P("cp"))
    step = functools.partial(local, dp=mesh.shape["dp"], cp=mesh.shape["cp"])
    return jax.shard_map(step, mesh=mesh, in_specs=in_specs, out_specs=out_specs, check_vma=False)
```

```python
import functools

import jax
import jax.numpy as jnp
from jax import lax
from jax.experimental import pallas as pl
from jax.experimental.pallas import tpu as pltpu
from jax.sharding import PartitionSpec as P

HEAD_DIM = 64
LANES = 128
GROUP = 3
RECUR = 3
NORM_EPSILON = 1e-05
MASKED_SCORE = -1e30
ROPE_BASE = 10000.0
SCALE = HEAD_DIM ** (-0.5)
MIB = 2**20
F32, BF16 = jnp.float32, jnp.bfloat16
NN = (((1,), (0,)), ((), ()))
NT = (((1,), (1,)), ((), ()))
TN = (((0,), (0,)), ((), ()))


def dotf(a, b, dims=NN):
    return lax.dot_general(a, b, dims, preferred_element_type=F32)


def turn(u):
    lane = lax.broadcasted_iota(jnp.int32, u.shape, 1) % HEAD_DIM
    return jnp.where(lane < HEAD_DIM // 2, pltpu.roll(u, LANES - 32, 1), pltpu.roll(u, 32, 1))


def variants_of(rows, keys):
    pick = lambda count, third, unit: (count * third // 3 // unit + 1) * unit
    return tuple((pick(rows, k, 32), pick(keys, k, LANES)) for k in (1, 2)) + ((rows, keys),)


def choose(meta_ref, variants, body):
    if len(variants) == 1:
        body(*variants[0])
    else:
        for i, variant in enumerate(variants):
            pl.when(meta_ref[0] == i)(functools.partial(body, *variant))


def clear(m, *refs):
    for ref in refs:
        if m < ref.shape[0]:
            ref[m:, :] = jnp.zeros((ref.shape[0] - m, ref.shape[1]), ref.dtype)


def call(kernel, name, meta, grid, inputs, in_specs, out_specs, out_shape, scratch, vmem, flops, traffic):
    return pl.pallas_call(
        kernel,
        grid_spec=pltpu.PrefetchScalarGridSpec(
            num_scalar_prefetch=1, grid=grid, in_specs=in_specs, out_specs=out_specs, scratch_shapes=scratch
        ),
        out_shape=out_shape,
        compiler_params=pltpu.CompilerParams(vmem_limit_bytes=vmem * MIB),
        cost_estimate=pl.CostEstimate(flops=flops, bytes_accessed=traffic, transcendentals=0),
        name=name,
    )(meta, *inputs)


def whole(*shape):
    return pl.BlockSpec(shape, lambda g, s: (0,) * len(shape))


IN_VMEM = pl.BlockSpec(memory_space=pltpu.VMEM)


def turns(table, keys):
    cos, sin = table[:, :LANES], table[:, LANES : 2 * LANES]
    if not keys:
        return cos, sin
    lane = lax.broadcasted_iota(jnp.int32, cos.shape, 1)
    return jnp.where(lane < HEAD_DIM, cos, 1.0), jnp.where(lane < HEAD_DIM, sin, 0.0)


def qkv_kernel(
    variants, meta_ref, x_ref, gain_ref, wq_ref, wkv_ref, table_ref, q_ref, kv_ref, normed_ref
):
    width = q_ref.shape[1]

    def body(m, _):
        x = x_ref[:m]
        factor = lax.rsqrt(jnp.mean(x * x, axis=-1, keepdims=True) + NORM_EPSILON)
        normed = (x * factor * gain_ref[...]).astype(BF16)
        normed_ref[:m, :] = normed
        kv = dotf(normed, wkv_ref[...])
        cos, sin = turns(table_ref[:m], True)
        for at in range(0, kv_ref.shape[1], LANES):
            u = kv[:, at : at + LANES]
            kv_ref[:m, at : at + LANES] = (u * cos + turn(u) * sin).astype(BF16)
        q = dotf(normed, wq_ref[:, :width])
        cos, sin = turns(table_ref[:m], False)
        for at in range(0, width, LANES):
            if at + LANES <= width:
                u = q[:, at : at + LANES]
            else:
                u = jnp.concatenate([q[:, at:], jnp.zeros((m, at + LANES - width), F32)], axis=1)
            r = (u * cos + turn(u) * sin).astype(BF16)
            q_ref[:m, at : min(at + LANES, width)] = r[:, : min(LANES, width - at)]
        clear(m, q_ref, kv_ref, normed_ref)

    choose(meta_ref, variants, body)


def qkv_call(variants, meta, x, gain, wq, wkv, table):
    rows, width = x.shape
    both = wkv.shape[1]
    return call(
        functools.partial(qkv_kernel, variants),
        "norm_qkv_rope",
        meta,
        (1,),
        (x, gain, wq, wkv, table),
        [IN_VMEM] * 5,
        [IN_VMEM] * 3,
        [jax.ShapeDtypeStruct((rows, k), BF16) for k in (width, both, width)],
        [],
        16,
        2 * rows * width * (width + both),
        2 * width * (width + both) + 8 * rows * width,
    )


def make_bias(row_table, col_info, recursion):
    doc_r, pos_r = (row_table[:, k : k + 1].astype(jnp.int32) for k in (2 * LANES + HEAD_DIM, 3 * LANES + HEAD_DIM))
    doc_c, pos_c, depth_c = col_info[0:1, :], col_info[1:2, :], col_info[2:3, :]
    live = (depth_c > recursion) | (pos_c == pos_r)
    allowed = (pos_c <= pos_r) & (doc_c == doc_r) & live
    return jnp.where(allowed, 0.0, MASKED_SCORE).astype(F32)


def split_pairs(packed, out, to_left):
    m, width = packed.shape
    lane = lax.broadcasted_iota(jnp.int32, (m, LANES), 1)
    for at in range(0, width, LANES):
        h = at // HEAD_DIM
        if at + LANES <= width:
            u = packed[:, at : at + LANES].astype(F32)
        else:
            u = jnp.concatenate([packed[:, at:].astype(F32), jnp.zeros((m, at + LANES - width), F32)], axis=1)
        v = pltpu.roll(u, HEAD_DIM, 1)
        first, second = (u, v) if to_left else (v, u)
        keep = (lane < HEAD_DIM) if to_left else (lane >= HEAD_DIM)
        out[h, :m] = jnp.where(keep, first, 0.0).astype(out.dtype)
        if at + LANES <= width:
            out[h + 1, :m] = jnp.where(keep, second, 0.0).astype(out.dtype)


def join_pairs(scr, out_ref, from_left, m):
    heads = scr.shape[0]
    lane = lax.broadcasted_iota(jnp.int32, (m, LANES), 1)
    for h in range(0, heads, 2):
        at = h * HEAD_DIM
        a = scr[h, :m] if from_left else pltpu.roll(scr[h, :m], HEAD_DIM, 1)
        if h + 1 < heads:
            b = pltpu.roll(scr[h + 1, :m], HEAD_DIM, 1) if from_left else scr[h + 1, :m]
            out_ref[:m, at : at + LANES] = jnp.where(lane < HEAD_DIM, a, b).astype(out_ref.dtype)
        else:
            out_ref[:m, at : at + HEAD_DIM] = a[:, :HEAD_DIM].astype(out_ref.dtype)


def compact_keys(meta_ref, key_refs, rows, keys):
    keys[...] = jnp.zeros_like(keys)
    block = 0
    for ref in key_refs:
        for first in range(0, ref.shape[0], rows):
            keys[pl.ds(pl.multiple_of(meta_ref[2 + 2 * block], 16), rows), :] = ref[first : first + rows, :]
            block += 1


def by_group(count, do):
    def one(g, _):
        do(g, pl.ds(pl.multiple_of(g * LANES, LANES), LANES))
        return 0

    lax.fori_loop(0, count, one, 0)


def stacked(m):
    return GROUP if GROUP * m <= 400 else 1


def attend_kernel(recursion, variants, count, meta_ref, q_ref, *refs):
    key_refs, (row_ref, col_ref, att_ref, lse_ref, keys, bias, q_all, o_all) = refs[:count], refs[count:]
    rows, groups = q_ref.shape[0], keys.shape[1] // LANES
    compact_keys(meta_ref, key_refs, rows, keys)
    lse_ref[...] = jnp.zeros_like(lse_ref)

    def body(m, n):
        bias[:m, :n] = make_bias(row_ref[:m], col_ref[:, :n], recursion)
        split_pairs(q_ref[:m] * jnp.bfloat16(SCALE), q_all, True)
        at_once = stacked(m)

        def group(g, cols):
            kv = keys[:n, cols]
            lane = lax.broadcasted_iota(jnp.int32, (m, LANES), 1)
            sets = [[g * GROUP + first + j for j in range(at_once)] for first in range(0, GROUP, at_once)]

            def score(heads):
                queries = jnp.concatenate([q_all[h, :m] for h in heads], axis=0)
                return dotf(queries, kv, NT) + jnp.concatenate([bias[:m, :n]] * at_once, axis=0)

            s = score(sets[0])
            for i, heads in enumerate(sets):
                following = score(sets[i + 1]) if i + 1 < len(sets) else None
                peak = jnp.max(s, axis=1, keepdims=True)
                e = jnp.exp(s - peak)
                total = jnp.sum(e, axis=1, keepdims=True)
                o = dotf(e.astype(BF16), kv) / total
                log = peak + jnp.log(total)
                for j, h in enumerate(heads):
                    here = slice(j * m, (j + 1) * m)
                    o_all[h, :m] = o[here]
                    lse_ref[:m, :] = jnp.where(lane == h, log[here], lse_ref[:m, :])
                s = following

        by_group(groups, group)
        join_pairs(o_all, att_ref, False, m)
        clear(m, att_ref)

    choose(meta_ref, variants, body)


def attend_call(recursion, variants, meta, q, kvs, row_info, col_info):
    rows, width = q.shape
    keys, both = sum(k.shape[0] for k in kvs), kvs[0].shape[1]
    heads = both // LANES * GROUP
    shape = jax.ShapeDtypeStruct
    inputs = (q, *kvs, row_info, col_info)
    return call(
        functools.partial(attend_kernel, recursion, variants, len(kvs)),
        "attend",
        meta,
        (1,),
        inputs,
        [IN_VMEM] * len(inputs),
        [IN_VMEM] * 3,
        [shape((rows, width), BF16), shape((rows, LANES), F32), shape((keys, both), BF16)],
        [
            pltpu.VMEM((rows, keys), F32),
            pltpu.VMEM((heads, rows, LANES), BF16),
            pltpu.VMEM((heads, rows, LANES), F32),
        ],
        16,
        4 * rows * keys * LANES * heads,
        4 * q.size + 2 * keys * both,
    )


def attend_back_kernel(
    recursion, variants, meta_ref, q_ref, do_ref, att_ref, keys, lse_ref, row_ref, col_ref, dq_ref, dkv_ref,
    bias, back, q_all, do_all, p3, ds3, dq_all,
):
    rows, groups = q_ref.shape[0], keys.shape[1] // LANES

    def body(m, n):
        bias[:m, :n] = make_bias(row_ref[:m], col_ref[:, :n], recursion)
        split_pairs(q_ref[:m] * jnp.bfloat16(SCALE), q_all, True)
        split_pairs(do_ref[:m], do_all, False)
        split_pairs(do_ref[:m].astype(F32) * att_ref[:m].astype(F32), dq_all, True)
        at_once = stacked(m)

        def group(g, cols):
            kv = keys[:n, cols]
            cos, sin = turns(row_ref[:m], False)
            lane = lax.broadcasted_iota(jnp.int32, (m, LANES), 1)
            stack = lambda parts: jnp.concatenate(parts, axis=0)
            sets = [[g * GROUP + first + j for j in range(at_once)] for first in range(0, GROUP, at_once)]

            def score(heads):
                s = dotf(stack([q_all[h, :m] for h in heads]), kv, NT) + stack([bias[:m, :n]] * at_once)
                return s, dotf(stack([do_all[h, :m] for h in heads]), kv, NT)

            s, dp = score(sets[0])
            for i, heads in enumerate(sets):
                following = score(sets[i + 1]) if i + 1 < len(sets) else (None, None)
                here = slice(i * at_once * m, (i + 1) * at_once * m)
                logs = stack([jnp.sum(jnp.where(lane == h, lse_ref[:m], 0.0), axis=1, keepdims=True) for h in heads])
                dots = stack([jnp.sum(dq_all[h, :m], axis=1, keepdims=True) for h in heads])
                p = jnp.exp(s - logs)
                ds = (p * (dp - dots)).astype(BF16)
                p3[here, :n] = p.astype(BF16)
                ds3[here, :n] = ds
                dq = dotf(ds, kv) * SCALE
                for j, h in enumerate(heads):
                    one = dq[j * m : (j + 1) * m]
                    dq_all[h, :m] = one * cos - turn(one) * sin
                s, dp = following
            q3 = jnp.concatenate([q_all[g * GROUP + j, :m] for j in range(GROUP)], axis=0)
            do3 = jnp.concatenate([do_all[g * GROUP + j, :m] for j in range(GROUP)], axis=0)
            dkv = dotf(q3, ds3[: GROUP * m, :n], TN) + dotf(do3, p3[: GROUP * m, :n], TN)
            back[:n, cols] = dkv.T

        by_group(groups, group)
        join_pairs(dq_all, dq_ref, True, m)
        clear(m, dq_ref)

    choose(meta_ref, variants, body)
    spot = lax.broadcasted_iota(jnp.int32, (rows, back.shape[1]), 0)
    for block in range(dkv_ref.shape[0] // rows):
        part = back[pl.ds(pl.multiple_of(meta_ref[2 + 2 * block], 16), rows), :]
        part = jnp.where(spot < meta_ref[3 + 2 * block], part, 0.0)
        dkv_ref[block * rows : (block + 1) * rows, :] = part.astype(BF16)


def attend_back_call(recursion, variants, meta, q, do, att, kv, lse, row_info, col_info):
    rows, width = q.shape
    keys, both = kv.shape
    heads = both // LANES * GROUP
    inputs = (q, do, att, kv, lse, row_info, col_info)
    return call(
        functools.partial(attend_back_kernel, recursion, variants),
        "attend_back",
        meta,
        (1,),
        inputs,
        [IN_VMEM] * len(inputs),
        [IN_VMEM] * 2,
        [jax.ShapeDtypeStruct((rows, width), BF16), jax.ShapeDtypeStruct((keys, both), BF16)],
        [
            pltpu.VMEM((rows, keys), F32),
            pltpu.VMEM((keys, both), F32),
            pltpu.VMEM((heads, rows, LANES), BF16),
            pltpu.VMEM((heads, rows, LANES), BF16),
            pltpu.VMEM((GROUP * rows, keys), BF16),
            pltpu.VMEM((GROUP * rows, keys), BF16),
            pltpu.VMEM((heads, rows, LANES), F32),
        ],
        24,
        10 * rows * keys * LANES * heads,
        8 * q.size + 4 * keys * both,
    )


def inverse(x):
    return lax.rsqrt(jnp.mean(x * x, axis=-1, keepdims=True) + NORM_EPSILON)


def sigmoid(x):
    return 1.0 / (1.0 + jnp.exp(-x))


def roles(core, a, b):
    return jnp.where(core == 0, a, b), jnp.where(core == 0, b, a)


def by_steps(width, step, do):
    def one(c, _):
        do(pl.ds(pl.multiple_of(c * step, step), step))
        return 0

    lax.fori_loop(0, width // step, one, 0)


def post_kernel(variants, step, meta_ref, att, state, wo, gain, router_row, active, mine, theirs, down, *refs):
    following, after, normed2, branch, router, gate_ref, up_ref, inner_ref = refs
    core, width = meta_ref[1], state.shape[1]

    def body(m, _):
        attn = dotf(att[:m], wo[:, :width])
        x = state[:m] + attn
        after[:m, :] = x
        normed2[:m, :] = (x * inverse(x) * gain[...]).astype(BF16)
        branch[:m, :] = attn

        def part(cols):
            n2 = normed2[:m, :]
            gate, up = roles(core, dotf(n2, mine[:, cols]), dotf(n2, theirs[:, cols]))
            inner = (gate * sigmoid(gate) * up).astype(BF16)
            inner_ref[:m, cols] = inner
            gate_ref[:m, cols] = gate.astype(BF16)
            up_ref[:m, cols] = up.astype(BF16)
            branch[:m, :] += dotf(inner, down[cols, :])

        by_steps(inner_ref.shape[1], step, part)
        clear(m, after, normed2, branch, inner_ref, gate_ref, up_ref)

    choose(meta_ref, variants, body)
    x = state[...]
    router[...] = sigmoid(jnp.sum(x * router_row[...], axis=-1, keepdims=True))
    following[...] = x + active[...] * router[...] * branch[...]


def post_call(variants, meta, att, state, w, router_row, active, step=512):
    rows, width = state.shape
    ff = w["mine"].shape[1]
    shape = jax.ShapeDtypeStruct
    inputs = (att, state, w["wide_o"], w["gain_f"], router_row, active, w["mine"], w["theirs"], w["down"])
    outputs = [shape((rows, width), F32), shape((rows, width), F32), shape((rows, width), BF16), shape((rows, width), F32)]
    outputs += [shape((rows, 1), F32)] + [shape((rows, ff), BF16)] * 3
    return call(
        functools.partial(post_kernel, variants, step),
        "post",
        meta,
        (1,),
        inputs,
        [IN_VMEM] * len(inputs),
        [IN_VMEM] * len(outputs),
        outputs,
        [],
        16,
        2 * rows * width * (width + 3 * ff),
        2 * width * (width + 3 * ff),
    )


def post_back_kernel(
    variants, step, meta_ref, grad, branch, state, after, router, active, router_row, gain, wo, gate_ref, up_ref, mine, theirs,
    down, g_ffn, g_state, g_attn, g_att, g_router, g_gain, g_mine_ref, g_theirs_ref, g_branch, g_normed2,
):
    core, width = meta_ref[1], state.shape[1]

    def body(m, _):
        g = grad[:m]
        weight = active[:m] * router[:m]
        logit = jnp.sum(g * branch[:m], axis=-1, keepdims=True) * weight * (1.0 - router[:m])
        g_router[...] = jnp.sum(logit * state[:m], axis=0, keepdims=True)
        g_state[:m, :] = g + logit * router_row[...]
        if m < grad.shape[0]:
            g_state[m:, :] = grad[m:]
        low = g * weight
        g_branch[:m, :] = low
        g_ffn[:m, :] = low.astype(BF16)
        g_normed2[:m, :] = jnp.zeros((m, width), F32)

        def part(cols):
            g_inner = dotf(g_ffn[:m, :], down[cols, :], NT)
            gate, up = gate_ref[:m, cols].astype(F32), up_ref[:m, cols].astype(F32)
            sig = sigmoid(gate)
            g_gate = (g_inner * up * sig * (1.0 + gate * (1.0 - sig))).astype(BF16)
            g_up = (g_inner * gate * sig).astype(BF16)
            g_mine, g_theirs = roles(core, g_gate, g_up)
            g_mine_ref[:m, cols] = g_mine
            g_theirs_ref[:m, cols] = g_theirs
            g_normed2[:m, :] += dotf(g_mine, mine[:, cols], NT) + dotf(g_theirs, theirs[:, cols], NT)

        by_steps(gate_ref.shape[1], step, part)
        x, g = after[:m], g_normed2[:m, :]
        factor = inverse(x)
        unit = x * factor
        g_gain[...] = jnp.sum(g * unit, axis=0, keepdims=True)
        scaled = g * gain[...]
        g_after = factor * (scaled - unit * jnp.mean(scaled * unit, axis=-1, keepdims=True))
        g_state[:m, :] += g_after
        low = (g_after + g_branch[:m, :]).astype(BF16)
        g_attn[:m, :] = low
        g_att[:m, :] = dotf(low, wo[:, :width], NT).astype(BF16)
        clear(m, g_ffn, g_attn, g_att, g_mine_ref, g_theirs_ref)

    choose(meta_ref, variants, body)


def expand_back_kernel(step, meta_ref, g_ffn, gate_ref, up_ref, down, g_mine_ref, g_theirs_ref):
    core = meta_ref[1]

    def part(cols):
        g_inner = dotf(g_ffn[...], down[cols, :], NT)
        gate, up = gate_ref[:, cols].astype(F32), up_ref[:, cols].astype(F32)
        sig = sigmoid(gate)
        g_gate = (g_inner * up * sig * (1.0 + gate * (1.0 - sig))).astype(BF16)
        g_up = (g_inner * gate * sig).astype(BF16)
        g_mine_ref[:, cols], g_theirs_ref[:, cols] = roles(core, g_gate, g_up)

    by_steps(gate_ref.shape[1], step, part)


def expand_back_call(meta, g_ffn, gate, up, w, step=512):
    inputs = (g_ffn, gate, up, w["down"])
    return call(
        functools.partial(expand_back_kernel, step),
        "expand_back",
        meta,
        (1,),
        inputs,
        [IN_VMEM] * len(inputs),
        [IN_VMEM] * 2,
        [jax.ShapeDtypeStruct(gate.shape, BF16)] * 2,
        [],
        16,
        2 * gate.size * g_ffn.shape[1],
        2 * w["down"].size,
    )


def norm_back_kernel(step, meta_ref, g_mine, g_theirs, mine, theirs, after, gain, g_branch, grad, wo, g_state, g_attn, g_att, g_gain):
    width = after.shape[1]
    g = dotf(g_mine[...], mine[...], NT) + dotf(g_theirs[...], theirs[...], NT)
    x = after[...]
    factor = inverse(x)
    unit = x * factor
    g_gain[...] = jnp.sum(g * unit, axis=0, keepdims=True)
    scaled = g * gain[...]
    g_after = factor * (scaled - unit * jnp.mean(scaled * unit, axis=-1, keepdims=True))
    g_state[...] = grad[...] + g_after
    low = (g_after + g_branch[...]).astype(BF16)
    g_attn[...] = low
    g_att[...] = dotf(low, wo[:, :width], NT).astype(BF16)


def norm_back_call(meta, g_mine, g_theirs, after, g_branch, grad, w, step=512):
    rows, width = after.shape
    inputs = (g_mine, g_theirs, w["mine"], w["theirs"], after, w["gain_f"], g_branch, grad, w["wide_o"])
    shape = jax.ShapeDtypeStruct
    outputs = [shape((rows, width), k) for k in (F32, BF16, BF16)] + [shape((1, width), F32)]
    return call(
        functools.partial(norm_back_kernel, step),
        "norm_back",
        meta,
        (1,),
        inputs,
        [IN_VMEM] * len(inputs),
        [IN_VMEM] * len(outputs),
        outputs,
        [],
        16,
        2 * rows * width * (width + 2 * g_mine.shape[1]),
        2 * width * (width + 2 * g_mine.shape[1]),
    )


def post_back_call(variants, meta, grad, branch, state, after, router, active, router_row, gate, up, w, step=512):
    rows, width = state.shape
    ff = w["mine"].shape[1]
    shape = jax.ShapeDtypeStruct
    inputs = (grad, branch, state, after, router, active, router_row, w["gain_f"], w["wide_o"], gate, up)
    inputs += (w["mine"], w["theirs"], w["down"])
    outputs = [shape((rows, width), k) for k in (BF16, F32, BF16, BF16)]
    outputs += [shape((1, width), F32)] * 2 + [shape((rows, ff), BF16)] * 2
    return call(
        functools.partial(post_back_kernel, variants, step),
        "post_back",
        meta,
        (1,),
        inputs,
        [IN_VMEM] * len(inputs),
        [IN_VMEM] * len(outputs),
        outputs,
        [pltpu.VMEM((rows, width), F32)] * 2,
        16,
        2 * rows * width * (width + 3 * ff),
        2 * width * (width + 3 * ff),
    )


def qkv_back_kernel(
    variants, meta_ref, dq_ref, mine_ref, got_ref, wq_ref, wkv_ref, x_ref, gain_ref, up_ref, table_ref,
    dkv_ref, out_ref, gain_grad_ref,
):
    def body(m, _):
        cos, sin = turns(table_ref[:m], True)
        for at in range(0, dkv_ref.shape[1], LANES):
            cols = slice(at, at + LANES)
            u = mine_ref[:m, cols].astype(F32) + got_ref[:m, cols].astype(F32)
            dkv_ref[:m, cols] = (u * cos - turn(u) * sin).astype(BF16)
        clear(m, dkv_ref)
        g = dotf(dq_ref[:m], wq_ref[:, : dq_ref.shape[1]], NT) + dotf(dkv_ref[:m, :], wkv_ref[...], NT)
        x = x_ref[:m]
        factor = inverse(x)
        unit = x * factor
        gain_grad_ref[...] = jnp.sum(g * unit, axis=0, keepdims=True)
        scaled = g * gain_ref[...]
        out_ref[:m, :] = up_ref[:m] + factor * (scaled - unit * jnp.mean(scaled * unit, axis=-1, keepdims=True))
        if m < up_ref.shape[0]:
            out_ref[m:, :] = up_ref[m:]

    choose(meta_ref, variants, body)


def qkv_back_call(variants, meta, dq, mine, got, wq, wkv, x, gain, upstream, table):
    rows, width = x.shape
    both = wkv.shape[1]
    return call(
        functools.partial(qkv_back_kernel, variants),
        "qkv_back",
        meta,
        (1,),
        (dq, mine, got, wq, wkv, x, gain, upstream, table),
        [IN_VMEM] * 9,
        [IN_VMEM] * 3,
        [
            jax.ShapeDtypeStruct((rows, both), BF16),
            jax.ShapeDtypeStruct((rows, width), F32),
            jax.ShapeDtypeStruct((1, width), F32),
        ],
        [],
        16,
        2 * rows * width * (width + both),
        2 * width * (width + both) + 16 * rows * width,
    )


def weight_grad_kernel(fill, counts, hand, choices, stride, spot_ref, *refs):
    c = pl.program_id(0)
    n_left, n_right, n_extra, n_ready, levels = counts
    sources, refs = refs[: n_left * levels], refs[n_left * levels :]
    rights, refs = refs[: n_right * levels], refs[n_right * levels :]
    extra, ready, refs = refs[:n_extra], refs[n_extra : n_extra + n_ready], refs[n_extra + n_ready :]
    outs, handed = refs[:5], refs[5 : 5 + (hand is not None)]
    scratch = refs[5 + len(handed) :]
    staged, turned, values, sem = scratch[:n_left], list(scratch[n_left : 2 * n_left]), scratch[-3:-1], scratch[-1]
    if handed:
        turned[hand] = handed[0]
    turned += ready

    def run(sizes):
        starts = [sum(sizes[:i]) for i in range(levels)]
        depth = sum(sizes)

        @pl.when(c == 0)
        def _():
            copies = []
            for i, source in enumerate(sources):
                size = sizes[i % levels]
                target = staged[i // levels].at[pl.ds(starts[i % levels], size), :]
                copies.append(pltpu.make_async_copy(source.at[pl.ds(0, size), :], target, sem.at[i]))
                copies[-1].start()
            for i, copy in enumerate(copies):
                copy.wait()
                if i % levels == levels - 1:
                    turned[i // levels][:, :depth] = staged[i // levels][:depth, :].T

        def product(left, right):
            group = rights[right * levels : (right + 1) * levels]
            stacked = jnp.concatenate([a[:size, :] for a, size in zip(group, sizes)], axis=0)
            return dotf(turned[left][:, :depth], stacked)

        fill(spot_ref[1], c, product, values, extra)

    core = spot_ref[1]
    for i, sizes in enumerate(choices):
        pl.when(spot_ref[2] == i)(functools.partial(run, sizes))
    each, cut = outs[4].shape[1], outs[0].shape[1]
    kept, away = values
    for r in range(4):
        mine = other = pl.multiple_of((spot_ref[0] ^ r) * stride, 16)
        source = away
        if stride != each:
            other = pl.multiple_of(mine + (1 - core) * each, 16)
            mine = pl.multiple_of(mine + core * each, 16)
            source = kept
        outs[r % 2][r // 2] = kept[pl.ds(mine, cut), :]
        outs[2 + r // 2][r % 2] = kept[pl.ds(pl.multiple_of(mine + cut, 16), each - cut), :]
        outs[4][r] = source[pl.ds(other, each), :]


def fill_rows(core, c, product, values, extra):
    values[0][...] = product(0, 0).astype(BF16)


def fill_roles(core, c, product, values, extra):
    for i, value in enumerate(values):
        value[...] = product(0, i).astype(BF16)


def fill_choice(core, c, product, values, extra):
    kept, away = values
    first, second = product(0, 0).astype(BF16), product(1, 1).astype(BF16)
    kept[...] = jnp.where(core == 0, first, second)
    away[...] = jnp.where(core == 0, second, first)


def fill_groups(core, c, product, values, extra):
    kept, away = values
    v = product(0, 0)
    part = kept.shape[1] - LANES
    low, high = v[:, :part].astype(BF16), v[:, v.shape[1] - part :].astype(BF16)
    kept[:, :part] = jnp.where(core == 0, low, high)
    away[:, :part] = jnp.where(core == 0, high, low)
    vectors = extra[0][...].T
    rest = jnp.zeros((vectors.shape[0], LANES - vectors.shape[1]), F32)
    vectors = jnp.concatenate([vectors, rest], axis=1).astype(BF16)
    kept[:, part:] = vectors
    away[:, part:] = vectors


def weight_grad(spot, fill, lefts, rights, stride, each, n, step, choices, extra=(), ready=(), hand=None):
    levels, rows = len(rights[0]), rights[0][0].shape[0]
    depth = levels * rows
    cut = -(-each // 32) * 16
    shapes = [(2, cut, n), (2, cut, n), (2, each - cut, n), (2, each - cut, n), (4, each, n)]
    flops = 2 * depth * 4 * stride * sum(right[0].shape[1] for right in rights)
    sources, moving = [a for group in lefts for a in group], [a for group in rights for a in group]
    by_step = pl.BlockSpec((rows, step), lambda c, s: (0, c))
    given = [] if hand is None else [(lefts[hand][0].shape[1], depth)]
    at_once = lambda a: pl.BlockSpec(a.shape, lambda c, s: (0, 0))
    return pl.pallas_call(
        functools.partial(weight_grad_kernel, fill, (len(lefts), len(rights), len(extra), len(ready), levels), hand, choices, stride),
        grid_spec=pltpu.PrefetchScalarGridSpec(
            num_scalar_prefetch=1,
            grid=(-(-n // step),),
            in_specs=[pl.BlockSpec(memory_space=pl.ANY)] * len(sources)
            + [by_step if n > step else at_once(a) for a in moving]
            + [at_once(a) for a in extra]
            + [IN_VMEM] * len(ready),
            out_specs=[pl.BlockSpec(s[:2] + (step,), lambda c, s: (0, 0, c)) for s in shapes] + [IN_VMEM] * len(given),
            scratch_shapes=[pltpu.VMEM((depth, group[0].shape[1]), BF16) for group in lefts]
            + [pltpu.VMEM((group[0].shape[1], depth), BF16) for group in lefts]
            + [pltpu.VMEM((4 * stride, step), BF16)] * 2
            + [pltpu.SemaphoreType.DMA((max(len(sources), 1),))],
        ),
        out_shape=[jax.ShapeDtypeStruct(s, BF16) for s in shapes + given],
        compiler_params=pltpu.CompilerParams(vmem_limit_bytes=24 * MIB),
        cost_estimate=pl.CostEstimate(
            flops=flops, bytes_accessed=2 * sum(a.size for a in sources + moving) + 16 * each * n, transcendentals=0
        ),
        name="weight_grad",
    )(spot, *sources, *moving, *extra, *ready)


def settle_kernel(moves, spot_ref, *refs):
    out = refs[-1]
    for i, first, rows, place in moves:
        out[pl.ds(pl.multiple_of(place(spot_ref), 16), rows), :] = refs[i][first : first + rows, : out.shape[1]]


def copy_call(kernel, name, spot, arrays, shapes):
    return pl.pallas_call(
        kernel,
        grid_spec=pltpu.PrefetchScalarGridSpec(
            num_scalar_prefetch=1,
            grid=(1,),
            in_specs=[IN_VMEM] * len(arrays),
            out_specs=[IN_VMEM] * len(shapes),
        ),
        out_shape=[jax.ShapeDtypeStruct(shape, arrays[0].dtype) for shape in shapes],
        compiler_params=pltpu.CompilerParams(vmem_limit_bytes=16 * MIB),
        cost_estimate=pl.CostEstimate(flops=0, bytes_accessed=4 * sum(a.size for a in arrays), transcendentals=0),
        name=name,
    )(spot, *arrays)


def settle_call(spot, arrays, moves, rows, width=None):
    shape = (rows, width or arrays[0].shape[1])
    (out,) = copy_call(functools.partial(settle_kernel, moves), "settle", spot, arrays, [shape])
    return out


def unpack_kernel(part, spot_ref, mine, theirs, q_out, o_out, kv_out, tail_out):
    both = kv_out.shape[1]
    tail_out[...] = mine[:, mine.shape[1] - LANES :]

    def go(first, second):
        q_out[...] = first[:, part:]
        o_out[...] = second[:, part:]
        kv_out[:, :part] = first[:, :part]
        kv_out[:, part:] = second[:, 2 * part - both : part]

    pl.when(spot_ref[1] == 0)(lambda: go(mine, theirs))
    pl.when(spot_ref[1] == 1)(lambda: go(theirs, mine))


def unpack_call(spot, mine, theirs, part, both):
    rows, width = mine.shape
    shapes = [(rows, width - part), (rows, width - part), (rows, both), (rows, LANES)]
    return copy_call(functools.partial(unpack_kernel, part), "unpack", spot, (mine, theirs), shapes)


def finish_kernel(part, both, spot_ref, own, other, query, key, value, out, vectors):
    width = query.shape[1]

    def go(low, high):
        out[...] = low[:, part + LANES : part + LANES + width].astype(F32)
        query[...] = high[:, part + LANES : part + LANES + width].astype(F32)
        vectors[...] = low[:, part : part + LANES].astype(F32).T[: vectors.shape[0], :]
        groups = [low[:, at : at + LANES] for at in range(0, part, LANES)]
        groups += [high[:, at : at + LANES] for at in range(2 * part - both, part, LANES)]
        groups = [group.astype(F32) for group in groups]
        lane = lax.broadcasted_iota(jnp.int32, groups[0].shape, 1)
        for i in range(0, len(groups), 2):
            at = i * HEAD_DIM
            a, turned = groups[i], pltpu.roll(groups[i], HEAD_DIM, 1)
            if i + 1 < len(groups):
                b = groups[i + 1]
                key[at : at + LANES, :] = jnp.where(lane < HEAD_DIM, a, pltpu.roll(b, HEAD_DIM, 1)).T
                value[at : at + LANES, :] = jnp.where(lane < HEAD_DIM, turned, b).T
            else:
                key[at : at + HEAD_DIM, :] = a.T[:HEAD_DIM, :]
                value[at : at + HEAD_DIM, :] = turned.T[:HEAD_DIM, :]

    pl.when(spot_ref[1] == 0)(lambda: go(own, other))
    pl.when(spot_ref[1] == 1)(lambda: go(other, own))


def finish_rows_kernel(spot_ref, own, other, out):
    half, width = own.shape[0], out.shape[0]

    def go(low, high):
        out[:, :half] = low[:, :width].astype(F32).T
        out[:, half:] = high[:, :width].astype(F32).T

    pl.when(spot_ref[1] == 0)(lambda: go(own, other))
    pl.when(spot_ref[1] == 1)(lambda: go(other, own))


def finish_rows_call(spot, own, other, width):
    shape = jax.ShapeDtypeStruct((width, 2 * own.shape[0]), F32)
    return call(
        finish_rows_kernel, "finish_rows", spot, (1,), (own, other), [IN_VMEM] * 2, IN_VMEM, shape, [], 16, 0, 8 * own.size
    )


def finish_call(spot, own, other, part, both, width):
    rows = own.shape[0]
    shapes = [(rows, width), (both // 2, rows), (both // 2, rows), (rows, width), (8, rows)]
    return call(
        functools.partial(finish_kernel, part, both),
        "finish",
        spot,
        (1,),
        (own, other),
        [IN_VMEM] * 2,
        [IN_VMEM] * len(shapes),
        [jax.ShapeDtypeStruct(shape, F32) for shape in shapes],
        [],
        16,
        0,
        8 * own.size,
    )


def tie(*trees):
    return lax.optimization_barrier(trees)


def add(*terms):
    return sum(a.astype(F32) for a in terms).astype(BF16)


def at(a, index, axis):
    return lax.dynamic_index_in_dim(a, index, axis, keepdims=False)


class Place:
    def __init__(self, dp, cp):
        self.dp, self.cp, self.square = dp, cp, cp == 4
        dp_at, cp_at = lax.axis_index("dp"), lax.axis_index("cp")
        self.core, self.z = dp_at % 2, dp_at // 2
        self.y, self.x = cp_at // 2, cp_at % 2
        self.spot = jnp.stack([cp_at, self.core]).astype(jnp.int32)

    def over_x(self, a):
        return lax.ppermute(a, "cp", [(i, i ^ 1) for i in range(self.cp)])

    def over_y(self, a):
        return lax.ppermute(a, "cp", [(i, i ^ 2) for i in range(self.cp)])

    def over_core(self, a):
        return lax.ppermute(a, "dp", [(i, i ^ 1) for i in range(self.dp)])

    def move_tokens(self, a):
        if not self.square:
            return a
        pairs = []
        for d in range(self.dp):
            for c in range(self.cp):
                z, core, y, x = d // 2, d % 2, c // 2, c % 2
                pairs.append((d * self.cp + c, (2 * z + y) * self.cp + 2 * core + x))
        return lax.ppermute(a, ("dp", "cp"), pairs)

    def move_wide(self, a):
        return self.move_tokens(jnp.pad(a, ((0, 0), (0, -a.shape[1] % LANES))))

    def fit(self, rows, later):
        sizes = [m for m, _ in variants_of(rows, later[0][1].shape[1])]
        self.choices = (tuple(reversed(sizes)), (rows,) * RECUR)
        fits = jnp.bool_(True)
        for r, (meta, _) in enumerate(later):
            fits = fits & (meta[0] <= RECUR - 2 - r)
        self.grad_spot = jnp.concatenate([self.spot, jnp.where(fits, 0, 1)[None].astype(jnp.int32)])

    def key_block(self):
        return 2 * self.core + self.x if self.square else lax.axis_index("cp")

    def gather_keys(self, a, axis=0):
        if not self.square:
            return (lax.all_gather(a, "cp", axis=axis, tiled=True),)
        from_x, from_core = self.over_x(a), self.over_core(a)
        return a, from_x, from_core, self.over_core(from_x)

    def scatter_keys_first(self, a):
        if not self.square:
            own = lax.psum_scatter(a, "cp", scatter_dimension=0, tiled=True)
            return own, jnp.zeros_like(own)
        rows = a.shape[0] // 4
        return a[: 2 * rows], self.over_core(a[2 * rows :])

    def scatter_keys_second(self, pair):
        if not self.square:
            return pair
        rows = pair[0].shape[0] // 2
        pair = add(*pair)
        return pair[:rows], self.over_x(pair[rows:])


    def gather_first(self, a):
        if not self.square:
            return (lax.all_gather(a, "cp", axis=0, tiled=True),)
        return a, self.over_x(a), self.over_y(a)

    def gather_second(self, parts):
        if not self.square:
            return parts
        own, from_x, from_y = parts
        cut = -(-own.shape[0] // 32) * 16
        return parts + (self.over_y(from_x[:cut]), self.over_x(from_y[cut:]))

    def gather_whole(self, parts):
        if not self.square:
            return parts[0]
        rows, cut = parts[0].shape[0], parts[3].shape[0]

        def move(i, count, block, offset):
            return i, 0, count, lambda spot: (spot[0] ^ block) * rows + offset

        moves = [move(0, rows, 0, 0), move(1, rows, 1, 0), move(2, rows, 2, 0)]
        moves += [move(3, cut, 3, 0), move(4, rows - cut, 3, cut)]
        return settle_call(self.spot, parts, moves, 4 * rows)

    def interleave(self, mine, theirs, width):
        half = mine.shape[0] // self.cp

        def move(i, block):
            return i, block * half, half, lambda spot: (2 * block + (spot[1] if i == 0 else 1 - spot[1])) * half

        moves = [move(i, block) for block in range(self.cp) for i in range(2)]
        return settle_call(self.spot, (mine, theirs), moves, 2 * mine.shape[0], width)


    def halves(self, fill, lefts, rights, stride, each, n, step, extra=(), ready=(), hand=None):
        if self.square:
            return weight_grad(
                self.grad_spot, fill, [] if ready else lefts, rights, stride, each, n, step, self.choices, extra, ready, hand
            )
        products = []

        def product(left, right):
            a, b = (jnp.concatenate(group, axis=0) for group in (lefts[left], rights[right]))
            b = jnp.pad(b, ((0, 0), (0, max(n - b.shape[1], 0)))) if fill is not fill_groups else b
            return dotf(a, b, TN).astype(BF16)

        if fill is fill_rows:
            both = product(0, 0).reshape(self.cp, 2, each, n)
            products = at(both, self.core, 1), at(both, 1 - self.core, 1)
        elif fill is fill_roles:
            products = product(0, 0), product(0, 1)
        elif fill is fill_choice:
            first, second = product(0, 0), product(1, 1)
            products = self.pick(first, second), self.pick(second, first)
        else:
            kv, part = product(0, 0), n - LANES
            low, high = kv[:, :part], kv[:, kv.shape[1] - part :]
            vectors = jnp.pad(extra[0].T, ((0, 0), (0, LANES - extra[0].shape[0]))).astype(BF16)
            products = [jnp.concatenate([self.pick(*pair), vectors], axis=1) for pair in ((low, high), (high, low))]
        return [a.reshape(self.cp, each, n) for a in products]

    def scatter_ready(self, pieces, got, apart=False):
        if not self.square:
            return (add(pieces[0], got),)
        top, top_out, low, low_out = pieces[:4]
        got = got.reshape((2, 2) + got.shape[1:])
        cut = top.shape[1]
        if apart:
            over_x = [add(top_out[i], got[i, 1, :cut]) for i in range(2)]
            over_y = [add(low_out[i], got[1, i, cut:]) for i in range(2)]
            return top, low, got, over_x, over_y
        return top, low, got, add(top_out, got[:, 1, :cut]), add(low_out, got[1, :, cut:])

    def scatter_first(self, parts):
        if not self.square:
            return (lax.psum_scatter(parts[0], "cp", scatter_dimension=0, tiled=False),)
        return parts[:3] + (self.over_x(parts[3]), self.over_y(parts[4]))

    def scatter_open(self, parts):
        if not self.square:
            return self.scatter_first(parts)
        return parts + ([self.over_x(parts[3][1])], [self.over_y(parts[4][1])])

    def scatter_more(self, parts):
        if not self.square:
            return parts
        over_x, over_y, from_x, from_y = parts[3:]
        return parts[:3] + ([self.over_x(over_x[0])] + from_x, [self.over_y(over_y[0])] + from_y)

    def scatter_next(self, parts):
        if not self.square:
            return parts
        top, low, got, from_x, from_y = parts
        cut = top.shape[1]
        top_out = add(top[1], got[1, 0, :cut], from_x[1])
        low_out = add(low[1], got[0, 1, cut:], from_y[1])
        return parts + (top_out, low_out)

    def scatter_second(self, parts):
        if not self.square:
            return parts
        return parts[:5] + (self.over_y(parts[5]), self.over_x(parts[6]))

    def scatter_rows(self, parts):
        if not self.square:
            half = parts[0].shape[0] // 2
            return parts[0][:half], parts[0][half:]
        top, low, got, from_x, from_y, last_y, last_x = parts
        cut = top.shape[1]
        return add(top[0], got[0, 0, :cut], from_x[0], last_y), add(low[0], got[0, 0, cut:], from_y[0], last_x)

    def scatter_whole(self, parts):
        return jnp.concatenate(self.scatter_rows(parts), axis=0)


    def hop(self, a, moves):
        return lax.ppermute(a, "dp", [(2 * s + c, 2 * t + c) for s, t in moves for c in range(2)])

    def z_first(self, a):
        n, got = self.dp // 2, jnp.zeros_like(a)
        for t in range(n // 2 - 1):
            if t:
                a = add(a, got)
            got = self.hop(a, [(t, t + 1), (n - 1 - t, n - 2 - t)])
        return a, got

    def z_second(self, pair):
        n, a = self.dp // 2, add(*pair)
        return a, self.hop(a, [(n // 2 - 1, n // 2), (n // 2, n // 2 - 1)])

    def z_third(self, pair):
        n, a = self.dp // 2, add(*pair)
        back = a
        for t in reversed(range(n // 2 - 1)):
            if t < n // 2 - 2:
                a = jnp.where((self.z == t + 1) | (self.z == n - 2 - t), back, a)
            back = self.hop(a, [(t + 1, t), (n - 2 - t, n - 1 - t)])
        return a, back

    def z_whole(self, pair):
        n = self.dp // 2
        if n < 4:
            return pair[0]
        return jnp.where((self.z == 0) | (self.z == n - 1), pair[1], pair[0])

    def pick(self, a, b):
        return jnp.where(self.core == 0, a, b)


def inverse_rms(matrix):
    return lax.rsqrt(jnp.mean(matrix * matrix, axis=-1, keepdims=True) + NORM_EPSILON)


def row_table(documents, places):
    half = HEAD_DIM // 2
    inverse = jnp.power(ROPE_BASE, -2.0 * jnp.arange(half, dtype=F32) / HEAD_DIM)
    angles = places.astype(F32)[:, None] * inverse[None, :]
    cos, sin = jnp.cos(angles), jnp.sin(angles)
    spread = lambda a: jnp.broadcast_to(a.astype(F32)[:, None], (a.shape[0], LANES))
    return jnp.concatenate([cos] * 4 + [-sin, sin] * 2 + [spread(documents), spread(places)], axis=1)


def depth_order(depth):
    steps = jnp.arange(depth.shape[0])
    before = (depth[:, None] > depth[None, :]) | ((depth[:, None] == depth[None, :]) & (steps[:, None] < steps[None, :]))
    return jnp.sum(before, axis=0)[None, :] == steps[:, None]


def reorder(order, rows):
    return dotf(order.astype(BF16), rows).astype(BF16)


def all_keys(every, rows, core):
    blocks = every.shape[1] // rows
    spots = jnp.stack([rows * jnp.arange(blocks), jnp.full((blocks,), rows)], axis=1).reshape(-1)
    return jnp.concatenate([jnp.stack([0, core]), spots]).astype(jnp.int32), every


def active_keys(every, rows, core, square):
    keys = every.shape[1]
    blocks, steps = keys // rows, jnp.arange(rows)
    levels = jnp.arange(1, RECUR)[:, None]
    counts = jnp.sum((every[2][None] > levels).reshape(RECUR - 1, blocks, rows), axis=2)
    taken = (counts + 15) // 16 * 16
    ahead = jnp.arange(blocks)[:, None] < jnp.arange(blocks)[None, :]
    starts = jnp.sum(jnp.where(ahead[None], taken[:, :, None], 0), axis=1)
    target = jnp.where(steps < taken[:, :, None], starts[:, :, None] + steps, -1).reshape(RECUR - 1, 1, keys, 1)
    hit = target == jnp.arange(keys)
    cols = jnp.sum(jnp.where(hit, every[None, :, :, None] + 1, 0), axis=2) - 1
    total = jnp.sum(taken, axis=1)
    own = counts[:, 0] if square else jnp.max(counts, axis=1)
    (m, n), (wide_m, wide_n), _ = variants_of(rows, keys)
    body = jnp.where((own <= m) & (total <= n), 0, jnp.where((own <= wide_m) & (total <= wide_n), 1, 2))
    spots = jnp.stack([starts, counts], axis=2).reshape(RECUR - 1, -1)
    metas = jnp.concatenate([body[:, None], jnp.full_like(body, core)[:, None], spots], axis=1).astype(jnp.int32)
    return [(metas[i], cols[i].astype(jnp.int32)) for i in range(RECUR - 1)]


class Level:
    def __init__(self, recursion, place, context, meta, col_info):
        self.recursion, self.place, self.meta, self.col_info = recursion, place, meta, col_info
        self.table, depth = context
        rows, keys = self.table.shape[0], self.col_info.shape[1]
        self.variants = variants_of(rows, keys) if recursion else ((rows, keys),)
        self.active = (depth[:, None] > recursion).astype(F32)

    def project(self, state, w):
        self.state = state
        self.q, self.kv, self.normed = qkv_call(
            self.variants, self.meta, state, w["gain_a"], w["q"], w["kv"], self.table
        )

    def attend(self, kvs):
        self.att, self.lse, self.keys = attend_call(
            self.recursion, self.variants, self.meta, self.q, kvs, self.table, self.col_info
        )

    def post(self, w):
        self.router_row = w["router"][self.recursion][None, :]
        state, self.after, self.normed2, self.branch, self.router, self.gate, self.up, self.inner = post_call(
            self.variants, self.meta, self.att, self.state, w, self.router_row, self.active
        )
        return state

    def widen(self, w):
        self.attn = dotf(self.att, w["o"])
        self.after = self.state + self.attn
        self.normed2 = (self.after * inverse_rms(self.after) * w["gain_f"]).astype(BF16)

    def expand(self, w):
        mine, theirs = dotf(self.normed2, w["mine"]), dotf(self.normed2, w["theirs"])
        gate, up = self.place.pick(mine, theirs), self.place.pick(theirs, mine)
        self.inner = (jax.nn.silu(gate) * up).astype(BF16)
        self.gate, self.up = gate.astype(BF16), up.astype(BF16)

    def close(self, w):
        self.branch = self.attn + dotf(self.inner, w["down"])
        self.router_row = w["router"][self.recursion][None, :]
        self.router = jax.nn.sigmoid(jnp.sum(self.state * self.router_row, axis=-1, keepdims=True))
        return self.state + self.active * self.router * self.branch

    def back_open(self, grad):
        self.g_branch = grad * (self.active * self.router)
        g_logit = jnp.sum(grad * self.branch, axis=-1, keepdims=True)
        g_logit = g_logit * self.active * self.router * (1.0 - self.router)
        self.g_router = jnp.sum(g_logit * self.state, axis=0, keepdims=True)
        self.g_state = grad + g_logit * self.router_row
        self.g_ffn = self.g_branch.astype(BF16)

    def back_expand(self, w):
        self.g_mine, self.g_theirs = expand_back_call(self.meta, self.g_ffn, self.gate, self.up, w)

    def back_norm(self, w):
        self.g_state, self.g_attn, self.g_att, self.g_gain_f = norm_back_call(
            self.meta, self.g_mine, self.g_theirs, self.after, self.g_branch, self.g_state, w
        )

    def post_back(self, grad, w):
        out = post_back_call(
            self.variants, self.meta, grad, self.branch, self.state, self.after, self.router, self.active, self.router_row,
            self.gate, self.up, w,
        )
        self.g_ffn, self.g_state, self.g_attn, self.g_att, self.g_router, self.g_gain_f, self.g_mine, self.g_theirs = out

    def back_attend(self):
        self.dq, dkv = attend_back_call(
            self.recursion, self.variants, self.meta, self.q, self.g_att, self.att, self.keys, self.lse, self.table,
            self.col_info,
        )
        return dkv

    def back_project(self, mine, got, w):
        self.dkv, grad, self.g_gain_a = qkv_back_call(
            self.variants, self.meta, self.dq, mine, got, w["q"], w["kv"], self.state, w["gain_a"], self.g_state, self.table
        )
        return grad


def local(tokens, recur_depth, document_ids, cotangent, *shards, dp, cp):
    place = Place(dp, cp)
    wq, wk, wv, wo, gate, up, down, router, gain_a, gain_f = shards
    rows, each = tokens.shape[1], wq.shape[0]
    width, kv_heads = each * cp, wk.shape[1] // HEAD_DIM

    wkv = jnp.stack([wk.reshape(each, kv_heads, HEAD_DIM), wv.reshape(each, kv_heads, HEAD_DIM)], axis=2)
    wkv = wkv.reshape(each, -1)
    small = jnp.concatenate([gain_a[:, None], gain_f[:, None], router.T], axis=1)
    both = wkv.shape[1]
    part = -(-both // (2 * LANES)) * LANES
    spare = -(part + width + small.shape[1]) % LANES
    blend = [place.pick(wkv[:, :part], wkv[:, both - part :]), place.pick(wq, wo), small, jnp.zeros((each, spare), BF16)]
    blend = place.gather_first(jnp.concatenate(blend, axis=1))
    ids = place.move_tokens(jnp.stack([document_ids[0], recur_depth[0]]))
    state = place.move_tokens(tokens[0])
    gates = place.pick(gate, up)
    downs = place.pick(down[: down.shape[0] // 2], down[down.shape[0] // 2 :])
    padded = -(-width // LANES) * LANES
    downs = jnp.pad(downs, ((0, 0), (0, padded - width)))
    blend, ids, state, gates, downs = tie(blend, ids, state, gates, downs)

    blend = place.gather_second(blend)
    steps = jnp.arange(rows, dtype=jnp.int32)
    order = depth_order(ids[1])
    ids = jnp.stack([ids[0], place.key_block() * rows + steps, ids[1]])
    ids = jnp.sum(jnp.where(order[None], ids[:, None, :], 0), axis=2)
    every = jnp.concatenate(place.gather_keys(ids, 1), axis=1)
    table = row_table(ids[0], ids[1])
    state = reorder(order, state)
    context = (table, ids[2])
    blend, context, order, state, gates, every = tie(blend, context, order, state.astype(F32), gates, every)

    g_part = place.gather_first(gates)
    mine = place.gather_whole(blend)
    theirs = place.over_core(mine)
    w = dict(zip(("q", "o", "kv", "tail"), unpack_call(place.spot, mine, theirs, part, both)))
    edge = width % LANES
    small = w["tail"][:, edge : edge + small.shape[1]].T.astype(F32)
    w["wide_o"], w["o"] = w["o"], w["o"][:, :width]
    w["gain_a"], w["gain_f"], w["router"] = small[:1], small[1:2], small[2:]
    first = Level(0, place, context, *all_keys(every, rows, place.core))
    first.project(state, w)
    first.kv, downs, every = tie(first.kv, downs, every)

    kvs = place.gather_keys(first.kv)
    later = active_keys(every, rows, place.core, place.square)
    kvs, g_part, downs, later = tie(kvs, g_part, downs, later)

    g_part = place.gather_second(g_part)
    d_part = place.gather_first(downs)
    first.attend(kvs)
    first.widen(w)
    first.normed2, g_part, d_part = tie(first.normed2, g_part, d_part)
    place.fit(rows, later)
    levels = [first] + [Level(r + 1, place, context, *found) for r, found in enumerate(later)]

    d_part = place.gather_second(d_part)
    w["mine"] = place.gather_whole(g_part)
    w["theirs"] = place.over_core(w["mine"])
    first.expand(w)
    first.inner, d_part = tie(first.inner, d_part)

    mine = place.gather_whole(d_part)
    w["down"] = place.interleave(mine, place.over_core(mine), width)
    state = first.close(w)

    for level in levels[1:]:
        level.project(state, w)
        level.attend(place.gather_keys(level.kv))
        state = level.post(w)
    activations = place.move_wide(reorder(order.T, state.astype(BF16)))
    grad = reorder(order, place.move_tokens(cotangent[0])).astype(F32)

    for level in levels[:0:-1]:
        level.post_back(grad, w)
        pair = place.scatter_keys_second(place.scatter_keys_first(level.back_attend()))
        grad = level.back_project(*pair, w)

    every = lambda name: [getattr(level, name) for level in levels]
    ff = gate.shape[1]

    grad, activations = tie(grad, activations)
    first.back_open(grad)
    d = place.halves(fill_rows, [every("inner")], [every("g_ffn")], ff // cp, ff // cp // 2, padded, 512)
    d_got = place.over_core(d[-1])
    first.back_expand(w)
    d = place.scatter_ready(d, d_got)
    d, first.g_mine, first.g_theirs = tie(d, first.g_mine, first.g_theirs)

    d = place.scatter_first(d)
    u = place.halves(fill_roles, [every("normed2")], [every("g_mine"), every("g_theirs")], each, each, ff, 512)
    d, u = tie(d, u)

    u_got = place.over_core(u[-1])
    d = place.scatter_next(d)
    d, first.g_mine, first.g_theirs = tie(d, first.g_mine, first.g_theirs)
    d = place.scatter_second(d)
    first.back_norm(w)
    u = place.scatter_ready(u, u_got, True)
    d, u, first.g_att = tie(d, u, first.g_att)

    u = place.scatter_open(u)
    d = place.z_first(place.scatter_whole(d))
    dkv = first.back_attend()
    u, d, dkv = tie(u, d, dkv)

    pair = place.scatter_keys_first(dkv)
    (pair,) = tie(pair)
    pair = place.scatter_keys_second(pair)
    u = place.scatter_more(u)
    lefts, rights = [every("att"), every("normed")], [every("g_attn"), every("dq")]
    p = place.halves(fill_choice, lefts, rights, each, each, padded, 512, hand=1)
    u, pair, p = tie(u, pair, p)

    u = place.scatter_next(u)
    u, pair = tie(u, pair)
    u = place.scatter_second(u)
    p_got = place.over_core(p[4] if place.square else p[1])
    grad = first.back_project(*pair, w)
    vectors = every("g_router") + [sum(every("g_gain_a")), sum(every("g_gain_f"))]
    vectors = jnp.concatenate(vectors + [jnp.zeros((8 - len(vectors), width), F32)], axis=0)
    ready = p[5:] if place.square else ()
    k = place.halves(
        fill_groups, [every("normed")], [every("dkv")], each, each, part + LANES, part + LANES, (vectors,), ready=ready
    )
    p = place.scatter_ready(p, p_got)
    u, p, k, grad = tie(u, p, k, grad)

    k_got = place.over_core(k[-1])
    u, v = place.scatter_rows(u)
    u = place.z_first(u)
    p = place.scatter_first(p)
    k = place.scatter_first(place.scatter_ready(k, k_got))
    d = place.z_second(d)
    u, v, p, k, d = tie(u, v, p, k, d)

    p, k = place.scatter_next(p), place.scatter_next(k)
    u, v, p, k, d = tie(u, v, p, k, d)
    p, k = place.scatter_second(p), place.scatter_second(k)
    u, v = place.z_second(u), place.z_first(v)
    d = place.z_third(d)
    input_grad = place.move_wide(reorder(order.T, grad.astype(BF16)))
    u, v, p, k, d, input_grad, activations = tie(u, v, p, k, d, input_grad, activations)

    a = jnp.concatenate([place.scatter_whole(k), place.scatter_whole(p)], axis=1)
    u, v, a = tie(u, v, a)
    u, v, a = place.z_third(u), place.z_second(v), place.z_first(a)
    u, v, a = tie(u, v, a)

    a, v = place.z_second(a), place.z_third(v)
    d_own = place.z_whole(d)
    grad_down = finish_rows_call(place.spot, d_own, place.over_core(d_own), width).T
    input_grad, activations = (b[None, :, :width] for b in (input_grad, activations))
    a, v, grad_down, input_grad, activations = tie(a, v, grad_down, input_grad, activations)

    a = place.z_third(a)
    u_own = jnp.concatenate([place.z_whole(u), place.z_whole(v)], axis=0)
    u_other = place.over_core(u_own)
    grad_gate, grad_up = place.pick(u_own, u_other).astype(F32), place.pick(u_other, u_own).astype(F32)
    a, grad_gate, grad_up = tie(a, grad_gate, grad_up)

    own = place.z_whole(a)
    other = place.over_core(own)
    grad_query, grad_key, grad_value, grad_out, vectors = finish_call(place.spot, own, other, part, both, width)
    return (
        activations,
        input_grad,
        grad_query,
        grad_key.T,
        grad_value.T,
        grad_out,
        grad_gate,
        grad_up,
        grad_down,
        vectors[:RECUR],
        vectors[RECUR],
        vectors[RECUR + 1],
    )


def solution(mesh):
    by_token = P("dp", "cp", None)
    by_row = P("cp", None)
    in_specs = (by_token, P("dp", "cp"), P("dp", "cp"), by_token) + (by_row,) * 7 + (P(None, "cp"), P("cp"), P("cp"))
    out_specs = (by_token, by_token) + (by_row,) * 7 + (P(None, "cp"), P("cp"), P("cp"))
    step = functools.partial(local, dp=mesh.shape["dp"], cp=mesh.shape["cp"])
    return jax.shard_map(step, mesh=mesh, in_specs=in_specs, out_specs=out_specs, check_vma=False)
```
